32 devices in a mesh: dp: 8 (over z, y), blk: 4 (over x, core).
Axes of the slice: x: 2, y: 2, z: 4, core: 2. Of those that a mesh axis runs over, the one named last changes fastest.
Arguments:
- tokens: bfloat16 [32, 512, 768], P('dp', 'blk'), may hold values from -6 to 6
- lengths: int32 [32, 8], P('dp'), may hold values from 1 to 385, 512 in all within a row
- w_qkv: bfloat16 [768, 2304], replicated, may hold values from -0.21875 to 0.21875
- bias_qv: float32 [1536], replicated, may hold values from -3 to 3
- w_out: bfloat16 [768, 768], replicated, may hold values from -0.875 to 0.875
- bias_out: float32 [768], replicated, may hold values from -3 to 3
- norm1_gain: float32 [768], replicated, may hold values from 0.25 to 1.75
- norm1_bias: float32 [768], replicated, may hold values from -3 to 3
- w_up: bfloat16 [768, 3072], replicated, may hold values from -0.21875 to 0.21875
- bias_up: float32 [3072], replicated, may hold values from -3 to 3
- w_down: bfloat16 [3072, 768], replicated, may hold values from -0.109375 to 0.109375
- bias_down: float32 [768], replicated, may hold values from -3 to 3
- norm2_gain: float32 [768], replicated, may hold values from 0.25 to 1.75
- norm2_bias: float32 [768], replicated, may hold values from -3 to 3
- cotangent: bfloat16 [32, 512, 768], P('dp', 'blk'), may hold values from -6 to 6
Outputs:
- outputs: bfloat16 [32, 512, 768], P('dp', 'blk')
- grad_tokens: bfloat16 [32, 512, 768], P('dp', 'blk')
- grad_w_qkv: float32 [768, 2304], P('dp')
- grad_bias_qv: float32 [1536], P('dp')
- grad_w_out: float32 [768, 768], P('dp')
- grad_bias_out: float32 [768], P('dp')
- grad_norm1_gain: float32 [768], P('dp')
- grad_norm1_bias: float32 [768], P('dp')
- grad_w_up: float32 [768, 3072], P('dp')
- grad_bias_up: float32 [3072], P('dp')
- grad_w_down: float32 [3072, 768], P('dp')
- grad_bias_down: float32 [768], P('dp')
- grad_norm2_gain: float32 [768], P('dp')
- grad_norm2_bias: float32 [768], P('dp')
The draws below stay inside these ranges and needn't reach their ends.
Inputs may be any that keep to these rules, and one draw needn't show every extreme that they name: Each row's page lengths sum to 512; in each row the longest page has exactly the largest length.
All inputs are finite; a program needn't handle non-finite values.
Results may differ from the reference program's by a relative error of at most 0.019.
Values may be sent and summed in bfloat16 or wider, within the bound.
No kernel may reach another device: no remote copies, remote signals or barrier semaphores. Data moves between devices by JAX's collectives and lax.ppermute only.
A program may use at most 128 MiB of HBM per device.

```python
import math
import jax
import jax.numpy as jnp
import numpy as np
from jax import lax

D = 768
HEADS = 12
HEAD_DIM = 64
FF = 3072
SEQ = 512
NSEG = 8
ROWS = 32
N_BLK = 4


def spiked(array, rng, source, target, parts, factor):
    def block_of(dim):
        return (jnp.arange(array.shape[dim]) // (array.shape[dim] // parts)).reshape((-1,) + (1,) * (array.ndim - 1 - dim))

    first = jax.random.permutation(rng, parts)[block_of(target)]
    other_side = (block_of(target) + parts // 2) % parts
    return jnp.where((block_of(source) == first) | (block_of(source) == other_side), factor * array, array)


def shard_levels(rng, dims, cuts, least, top_value):
    def one(axis_at, parts):
        heights = jax.random.uniform(jax.random.fold_in(jax.random.fold_in(rng, 6), axis_at), (parts,), jnp.float32, least / len(cuts), top_value / len(cuts))
        return jnp.repeat(jnp.exp(heights), dims[axis_at] // parts).reshape((-1,) + (1,) * (len(dims) - axis_at - 1))

    factor_of = one(*cuts[0])
    for cut in cuts[1:]:
        factor_of = factor_of * one(*cut)
    return factor_of


def split_up(amount, total, bound, skew):
    portions = [(1 << 20) // math.isqrt(rank ** skew) + 1 for rank in range(2, amount + 1)]
    spare, holding = total - bound - (amount - 1), [1] * (amount - 1)
    while spare > 0:
        candidates = [i for i in range(amount - 1) if holding[i] < bound]
        whole, remaining = sum([portions[i] for i in candidates]), spare
        for i in candidates:
            addition = min(bound - holding[i], max(1, remaining * portions[i] // whole), spare)
            holding[i] = holding[i] + addition
            spare = spare - addition
    return np.array([bound] + holding)


def ragged(own_key, amount, total, most, slope):
    if amount == 2:
        one = jax.random.randint(own_key, (), max(1, total - most), min(most, total - 1) + 1)
        return jnp.stack([one, total - one])
    tallies = jnp.asarray(split_up(amount, total, most, slope), jnp.int32)
    couples = (amount - 1) // 2
    giver, receiver = tallies[1:1 + 2 * couples:2], tallies[2:2 + 2 * couples:2]
    room = jnp.minimum(giver - 1, most - receiver)
    moved = jax.random.randint(jax.random.fold_in(own_key, 1), (couples,), 0, 1 << 20) % (room + 1)
    tallies = tallies.at[1:1 + 2 * couples:2].set(giver - moved).at[2:2 + 2 * couples:2].set(receiver + moved)
    return tallies[jax.random.permutation(jax.random.fold_in(own_key, 2), amount)]


def normal_values(key, extent, scale, most, pieces=(), held_as=jnp.bfloat16):
    array = scale * jax.random.normal(key, extent, jnp.float32)
    if pieces:
        array = array * shard_levels(key, extent, pieces, -0.22, 0.18)
    return jnp.clip(array, -most, most).astype(held_as)


def heavy_noise(rng, dims, scale, most, shards, heavy, held_as=jnp.bfloat16):
    entries = scale * jax.random.normal(rng, dims, jnp.float32)
    if shards:
        entries = entries * shard_levels(rng, dims, shards, -0.22, 0.18)
    return jnp.clip(spiked(entries, jax.random.fold_in(rng, 3), *heavy), -most, most).astype(held_as)


def setup_inputs(seed: int = 0) -> dict:
    splits = jax.random.split(jax.random.key(seed), 16)
    return {
        "tokens": heavy_noise(splits[0], (ROWS, SEQ, D), 1.0, 6.0, ((0, 8), (1, 4)), (0, 2, 8, 2.0)),
        "lengths": jax.vmap(lambda own: ragged(own, NSEG, SEQ, (N_BLK - 1) * (SEQ // N_BLK) + 1, 2))(jax.random.split(splits[1], ROWS)).reshape((ROWS, NSEG)).astype(jnp.int32),
        "w_qkv": normal_values(splits[2], (D, 3 * D), D ** -0.5, 0.21875),
        "bias_qv": normal_values(splits[3], (2 * D,), 0.5, 3.0, (), jnp.float32),
        "w_out": normal_values(splits[4], (D, D), (D // 16) ** -0.5, 0.875),
        "bias_out": normal_values(splits[5], (D,), 0.5, 3.0, (), jnp.float32),
        "norm1_gain": jnp.clip(1.0 + 0.15 * jax.random.normal(splits[6], (D,), jnp.float32), 0.25, 1.75),
        "norm1_bias": normal_values(splits[7], (D,), 0.5, 3.0, (), jnp.float32),
        "w_up": normal_values(splits[8], (D, FF), D ** -0.5, 0.21875),
        "bias_up": normal_values(splits[9], (FF,), 0.5, 3.0, (), jnp.float32),
        "w_down": normal_values(splits[10], (FF, D), FF ** -0.5, 0.109375),
        "bias_down": normal_values(splits[11], (D,), 0.5, 3.0, (), jnp.float32),
        "norm2_gain": jnp.clip(1.0 + 0.15 * jax.random.normal(splits[12], (D,), jnp.float32), 0.25, 1.75),
        "norm2_bias": normal_values(splits[13], (D,), 0.5, 3.0, (), jnp.float32),
        "cotangent": heavy_noise(splits[14], (ROWS, SEQ, D), 1.0, 6.0, ((0, 8), (1, 4)), (0, 2, 8, 2.0)),
    }


@jax.custom_vjp
def low(v):
    return lax.optimization_barrier(v.astype(jnp.bfloat16)).astype(jnp.float32)

@jax.custom_vjp
def low_back(v):
    return v

def low_keep(v):
    return (low(v), None)

def low_pass(kept, grad):
    return (grad,)

def back_keep(v):
    return (v, None)

def back_low(kept, grad):
    return (low(grad),)
low.defvjp(low_keep, low_pass)
low_back.defvjp(back_keep, back_low)
HIGHEST_PRECISION = lax.Precision.HIGHEST
EPSILON = 1e-12
MASKED = -1e+30

def page_numbers(lengths, total_slots):
    page_ends = jnp.cumsum(lengths, axis=1)
    slot_ids = jnp.arange(total_slots, dtype=jnp.int32)
    return lax.optimization_barrier(jnp.sum((slot_ids[None, :, None] >= page_ends[:, None, :]).astype(jnp.int32), axis=2))

def layer_norm(inputs, gain_vec, shift_vec):
    centre = inputs - lax.optimization_barrier(jnp.mean(inputs, axis=-1, keepdims=True))
    spread = lax.optimization_barrier(jnp.mean(centre * centre, axis=-1, keepdims=True))
    return centre * lax.rsqrt(spread + EPSILON) * gain_vec + shift_vec

def row_attention(inputs_row):
    queries, key_rows, value_rows, page_ids = inputs_row
    scaling = 1.0 / math.sqrt(HEAD_DIM)
    scores = low_back(jnp.einsum('qhd,khd->hqk', queries, key_rows, precision=HIGHEST_PRECISION) * scaling)
    same_page = page_ids[:, None] == page_ids[None, :]
    masked = jnp.where(same_page[None], scores, MASKED)
    row_max = lax.optimization_barrier(jnp.max(masked, axis=-1, keepdims=True))
    exponent = jnp.exp(masked - row_max)
    weights = low(exponent / lax.optimization_barrier(jnp.sum(exponent, axis=-1, keepdims=True)))
    return jnp.einsum('hqk,khd->qhd', weights, value_rows, precision=HIGHEST_PRECISION)

def encoder_layer(params, tokens, page_ids):
    w_qkv, bias_qv, w_out, bias_out, norm1_gain, norm1_bias, w_up, bias_up, w_down, bias_down, norm2_gain, norm2_bias = params
    row_count = tokens.shape[0]
    flat_tokens = tokens.reshape(row_count * SEQ, D)
    projected = jnp.dot(flat_tokens, w_qkv, precision=HIGHEST_PRECISION)
    queries = low_back(low(projected[:, :D] + bias_qv[:D]))
    key_rows = low_back(low(projected[:, D:2 * D]))
    value_rows = low_back(low(projected[:, 2 * D:] + bias_qv[D:]))
    head_shape = (row_count, SEQ, HEADS, HEAD_DIM)
    context = lax.map(jax.checkpoint(row_attention), (queries.reshape(head_shape), key_rows.reshape(head_shape), value_rows.reshape(head_shape), page_ids))
    context = low_back(low(context.reshape(row_count * SEQ, D)))
    attended = low_back(jnp.dot(context, w_out, precision=HIGHEST_PRECISION) + bias_out)
    first_norm = layer_norm(flat_tokens + attended, norm1_gain, norm1_bias)
    raised = low_back(jnp.dot(low(first_norm), w_up, precision=HIGHEST_PRECISION) + bias_up)
    activated = low(jax.nn.gelu(raised, approximate=False))
    lowered = low_back(jnp.dot(activated, w_down, precision=HIGHEST_PRECISION) + bias_down)
    return layer_norm(first_norm + lowered, norm2_gain, norm2_bias).reshape(row_count, SEQ, D)

def reference(tokens, lengths, w_qkv, bias_qv, w_out, bias_out, norm1_gain, norm1_bias, w_up, bias_up, w_down, bias_down, norm2_gain, norm2_bias, cotangent):
    params = tuple((item.astype(jnp.float32) for item in (w_qkv, bias_qv, w_out, bias_out, norm1_gain, norm1_bias, w_up, bias_up, w_down, bias_down, norm2_gain, norm2_bias)))
    page_ids = page_numbers(lengths, SEQ)
    group_rows = 8
    groups = ROWS // group_rows

    def visit_group(totals, group_items):
        block_tokens, block_pages, block_grads = group_items
        outputs, pullback = jax.vjp(lambda p, t: encoder_layer(p, t, block_pages), params, block_tokens)
        grad_params, grad_tokens = pullback(block_grads)
        totals = jax.tree.map(lambda left, right: left + right, totals, grad_params)
        return (totals, (outputs.astype(jnp.bfloat16), grad_tokens.astype(jnp.bfloat16)))
    zero_grads = jax.tree.map(jnp.zeros_like, params)
    group_inputs = (tokens.astype(jnp.float32).reshape(groups, group_rows, SEQ, D), page_ids.reshape(groups, group_rows, SEQ), cotangent.astype(jnp.float32).reshape(groups, group_rows, SEQ, D))
    totals, (outputs, grad_tokens) = lax.scan(visit_group, zero_grads, group_inputs)
    grad_w_qkv, grad_bias_qv, grad_w_out, grad_bias_out, grad_norm1_gain, grad_norm1_bias, grad_w_up, grad_bias_up, grad_w_down, grad_bias_down, grad_norm2_gain, grad_norm2_bias = totals
    return (outputs.reshape(ROWS, SEQ, D), grad_tokens.reshape(ROWS, SEQ, D), grad_w_qkv, grad_bias_qv, grad_w_out, grad_bias_out, grad_norm1_gain, grad_norm1_bias, grad_w_up, grad_bias_up, grad_w_down, grad_bias_down, grad_norm2_gain, grad_norm2_bias)
```

```python
import functools
import math

import jax
import jax.numpy as jnp
from jax import lax
from jax.experimental import pallas as pl
from jax.experimental.pallas import tpu as pltpu
from jax.sharding import PartitionSpec as P

HEADS = 12
EPSILON = 1e-12
MASKED = -1e30
VMEM_BYTES = 56 * 2**20

f32 = jnp.float32
bf16 = jnp.bfloat16
NN = (((1,), (0,)), ((), ()))
NT = (((1,), (1,)), ((), ()))
TN = (((0,), (0,)), ((), ()))


def dot(left, right, dims=NN):
    return lax.dot_general(left, right, dims, preferred_element_type=f32)


def whole(shape):
    return pl.BlockSpec(shape, lambda i: (0,) * len(shape))


def params():
    return pltpu.CompilerParams(vmem_limit_bytes=VMEM_BYTES)


def cost(flops, bytes_accessed, transcendentals=0):
    return pl.CostEstimate(
        flops=flops, bytes_accessed=bytes_accessed, transcendentals=transcendentals
    )


def column_sum(values):
    return jnp.sum(values, axis=0, keepdims=True)


def row_mean(values):
    return jnp.mean(values, axis=-1, keepdims=True)


def normalize(inputs):
    centre = inputs - row_mean(inputs)
    inverse = lax.rsqrt(row_mean(centre * centre) + EPSILON)
    return centre * inverse, inverse


def normalize_back(scaled, normed, inverse):
    return inverse * (scaled - row_mean(scaled) - normed * row_mean(scaled * normed))


def attend_kernel(
    row_ref, x0, x1, x2, x3, wq, wk, wv, bq, bv, wo, bo,
    q_out, k_out, v_out, prob_out, context_out, normed_out, inverse_out,
    tokens, mask, total, *, steps, slots, pages, head_width,
):
    step = pl.program_id(0)
    count = tokens.shape[0]
    wide = wq.shape[1]

    @pl.when(step == 0)
    def _():
        for i, block in enumerate((x0, x1, x2, x3)):
            tokens[i * slots : (i + 1) * slots, :] = block[...]
        position = row_ref[pages]

        def page_of(dim):
            at = lax.broadcasted_iota(jnp.int32, (count, count), dim)
            slot = ((at // slots) ^ position) * slots + at % slots
            page = jnp.zeros((count, count), jnp.int32)
            end = 0
            for c in range(pages):
                end = end + row_ref[c]
                page = page + (slot >= end).astype(jnp.int32)
            return page

        mask[...] = jnp.where(page_of(0) == page_of(1), 0.0, MASKED)
        total[...] = jnp.zeros_like(total)

    x = tokens[...]
    q = (dot(x, wq[...]) + bq[...]).astype(bf16)
    k = dot(x, wk[...]).astype(bf16)
    v = (dot(x, wv[...]) + bv[...]).astype(bf16)
    q_out[...] = q
    k_out[...] = k
    v_out[...] = v
    scaled_q = q * jnp.asarray(1.0 / math.sqrt(head_width), bf16)
    head = lax.broadcasted_iota(jnp.int32, (count, wide), 1) // head_width
    none = jnp.zeros((count, wide), bf16)
    context = jnp.zeros((count, wide), f32)
    for h in range(wide // head_width):
        scores = dot(k, jnp.where(head == h, scaled_q, none), NT) + mask[...]
        powers = jnp.exp(scores - jnp.max(scores, axis=0, keepdims=True))
        probs = (powers * (1.0 / jnp.sum(powers, axis=0, keepdims=True))).astype(bf16)
        prob_out[h] = probs
        context = context + dot(probs, jnp.where(head == h, v, none), TN)
    context = context.astype(bf16)
    context_out[...] = context
    total[...] += dot(context, wo[...])

    @pl.when(step == steps - 1)
    def _():
        normed, inverse = normalize(tokens[...].astype(f32) + (total[...] + bo[...]))
        normed_out[...] = normed
        inverse_out[...] = inverse


def attend(row, blocks, w_qkv, bias_qv, w_out, bias_out):
    slots, width = blocks[0].shape
    count = slots * len(blocks)
    head_width = width // HEADS
    wide = 4 * head_width
    steps = width // wide

    def weight(part):
        return pl.BlockSpec((width, wide), lambda i: (0, part * steps + i))

    def shift(part):
        return pl.BlockSpec((1, wide), lambda i: (0, part * steps + i))

    columns = pl.BlockSpec((count, wide), lambda i: (0, i))
    narrow = jax.ShapeDtypeStruct((count, width), bf16)
    return pl.pallas_call(
        functools.partial(
            attend_kernel,
            steps=steps, slots=slots, pages=row.shape[0] - 1, head_width=head_width,
        ),
        grid=(steps,),
        in_specs=[pl.BlockSpec(memory_space=pltpu.SMEM)]
        + [whole((slots, width))] * 4
        + [weight(0), weight(1), weight(2), shift(0), shift(1)]
        + [pl.BlockSpec((wide, width), lambda i: (i, 0)), whole((1, width))],
        out_specs=[
            columns, columns, columns,
            pl.BlockSpec((4, count, count), lambda i: (i, 0, 0)),
            columns, whole((count, width)), whole((count, 1)),
        ],
        out_shape=[
            narrow, narrow, narrow,
            jax.ShapeDtypeStruct((HEADS, count, count), bf16),
            narrow,
            jax.ShapeDtypeStruct((count, width), f32),
            jax.ShapeDtypeStruct((count, 1), f32),
        ],
        scratch_shapes=[
            pltpu.VMEM((count, width), bf16),
            pltpu.VMEM((count, count), f32),
            pltpu.VMEM((count, width), f32),
        ],
        compiler_params=params(),
        cost_estimate=cost(8 * count * width * width, 40 * 2**20),
        name="attend",
    )(row, *blocks, w_qkv, w_qkv, w_qkv, bias_qv[None], bias_qv[None], w_out, bias_out[None])


def feed_kernel(
    normed_one, gain_one, shift_one, w_up, b_up, w_down, b_down, gain_two, shift_two, cotangent,
    active_out, slope_out, result_out, lowered_out, sum_out, first_out, vector_out,
    total, *, steps,
):
    step = pl.program_id(0)

    @pl.when(step == 0)
    def _():
        first_out[...] = (normed_one[...] * gain_one[...] + shift_one[...]).astype(bf16)
        total[...] = jnp.zeros_like(total)

    raised = dot(first_out[...], w_up[...]) + b_up[...]
    cumulative = 0.5 * (1.0 + lax.erf(raised * (1.0 / math.sqrt(2.0))))
    activated = (raised * cumulative).astype(bf16)
    active_out[...] = activated
    bell = jnp.exp(-0.5 * raised * raised) * (1.0 / math.sqrt(2.0 * math.pi))
    slope_out[...] = (cumulative + raised * bell).astype(bf16)
    total[...] += dot(activated, w_down[...])

    @pl.when(step == steps - 1)
    def _():
        first_norm = normed_one[...] * gain_one[...] + shift_one[...]
        normed, inverse = normalize(first_norm + (total[...] + b_down[...]))
        result_out[...] = (normed * gain_two[...] + shift_two[...]).astype(bf16)
        upstream = cotangent[...].astype(f32)
        grad_sum = normalize_back(upstream * gain_two[...], normed, inverse)
        lowered = grad_sum.astype(bf16)
        sum_out[...] = grad_sum
        lowered_out[...] = lowered
        vector_out[0:1, :] = column_sum(upstream * normed)
        vector_out[1:2, :] = column_sum(upstream)
        vector_out[2:3, :] = column_sum(lowered.astype(f32))


def feed(normed, gain_one, shift_one, w_up, b_up, w_down, b_down, gain_two, shift_two, cotangent):
    count, width = normed.shape
    hidden = w_up.shape[1]
    steps = 4
    wide = hidden // steps
    columns = pl.BlockSpec((count, wide), lambda i: (0, i))
    vector = whole((1, width))
    narrow = jax.ShapeDtypeStruct((count, width), bf16)
    return pl.pallas_call(
        functools.partial(feed_kernel, steps=steps),
        grid=(steps,),
        in_specs=[
            whole((count, width)), vector, vector,
            pl.BlockSpec((width, wide), lambda i: (0, i)),
            pl.BlockSpec((1, wide), lambda i: (0, i)),
            pl.BlockSpec((wide, width), lambda i: (i, 0)),
            vector, vector, vector, whole((count, width)),
        ],
        out_specs=[columns, columns] + [whole((count, width))] * 4 + [whole((8, width))],
        out_shape=[
            jax.ShapeDtypeStruct((count, hidden), bf16),
            jax.ShapeDtypeStruct((count, hidden), bf16),
            narrow, narrow,
            jax.ShapeDtypeStruct((count, width), f32),
            narrow,
            jax.ShapeDtypeStruct((8, width), f32),
        ],
        scratch_shapes=[pltpu.VMEM((count, width), f32)],
        compiler_params=params(),
        cost_estimate=cost(4 * count * width * hidden, 40 * 2**20),
        name="feed",
    )(
        normed, gain_one[None], shift_one[None], w_up, b_up[None], w_down, b_down[None],
        gain_two[None], shift_two[None], cotangent,
    )


def feed_back_kernel(
    lowered, active, slope, w_down, w_up, first, sum_two, normed_one, inverse_one, gain_one,
    down_out, up_out, bias_out, attended_out, sum_out, vector_out,
    turned, total, *, steps,
):
    step = pl.program_id(0)

    @pl.when(step == 0)
    def _():
        turned[...] = first[...].T
        total[...] = sum_two[...]

    down_out[...] = dot(active[...], lowered[...], TN).astype(bf16)
    raised = (dot(lowered[...], w_down[...], NT) * slope[...].astype(f32)).astype(bf16)
    bias_out[...] = column_sum(raised.astype(f32))
    up_out[...] = dot(turned[...], raised).astype(bf16)
    total[...] += dot(raised, w_up[...], NT)

    @pl.when(step == steps - 1)
    def _():
        upstream = total[...]
        normed = normed_one[...]
        grad_sum = normalize_back(upstream * gain_one[...], normed, inverse_one[...])
        attended = grad_sum.astype(bf16)
        sum_out[...] = grad_sum
        attended_out[...] = attended
        vector_out[0:1, :] = column_sum(upstream * normed)
        vector_out[1:2, :] = column_sum(upstream)
        vector_out[2:3, :] = column_sum(attended.astype(f32))


def feed_back(lowered, active, slope, w_down, w_up, first, sum_two, normed, inverse, gain_one):
    count, width = normed.shape
    hidden = w_up.shape[1]
    steps = 4
    wide = hidden // steps
    columns = pl.BlockSpec((count, wide), lambda i: (0, i))
    return pl.pallas_call(
        functools.partial(feed_back_kernel, steps=steps),
        grid=(steps,),
        in_specs=[
            whole((count, width)), columns, columns,
            pl.BlockSpec((wide, width), lambda i: (i, 0)),
            pl.BlockSpec((width, wide), lambda i: (0, i)),
            whole((count, width)), whole((count, width)), whole((count, width)),
            whole((count, 1)), whole((1, width)),
        ],
        out_specs=[
            pl.BlockSpec((wide, width), lambda i: (i, 0)),
            pl.BlockSpec((None, width, wide), lambda i: (i, 0, 0)),
            pl.BlockSpec((1, wide), lambda i: (0, i)),
            whole((count, width)), whole((count, width)), whole((8, width)),
        ],
        out_shape=[
            jax.ShapeDtypeStruct((hidden, width), bf16),
            jax.ShapeDtypeStruct((steps, width, wide), bf16),
            jax.ShapeDtypeStruct((1, hidden), f32),
            jax.ShapeDtypeStruct((count, width), bf16),
            jax.ShapeDtypeStruct((count, width), f32),
            jax.ShapeDtypeStruct((8, width), f32),
        ],
        scratch_shapes=[pltpu.VMEM((width, count), bf16), pltpu.VMEM((count, width), f32)],
        compiler_params=params(),
        cost_estimate=cost(8 * count * width * hidden, 50 * 2**20),
        name="feed_back",
    )(lowered, active, slope, w_down, w_up, first, sum_two, normed, inverse, gain_one[None])


def attend_back_kernel(
    x0, x1, x2, x3, attended, sum_one, context, prob, q_ref, k_ref, v_ref, wq, wk, wv, wo,
    pieces_out, tokens_out, bias_q, bias_v,
    turned, total, *, steps, slots, head_width,
):
    step = pl.program_id(0)
    count = attended.shape[0]
    wide = wq.shape[1]

    @pl.when(step == 0)
    def _():
        for i, block in enumerate((x0, x1, x2, x3)):
            turned[:, i * slots : (i + 1) * slots] = block[...].T
        total[...] = sum_one[...]

    grad_context = dot(attended[...], wo[...], NT).astype(bf16)
    grad_out = dot(context[...], attended[...], TN).astype(bf16)
    scaling = jnp.asarray(1.0 / math.sqrt(head_width), bf16)
    scaled_q = q_ref[...] * scaling
    scaled_k = k_ref[...] * scaling
    v = v_ref[...]
    head = lax.broadcasted_iota(jnp.int32, (count, wide), 1) // head_width
    none = jnp.zeros((count, wide), bf16)
    grad_q = jnp.zeros((count, wide), f32)
    grad_k = grad_q
    grad_v = grad_q
    for h in range(wide // head_width):
        mine = head == h
        probs = prob[h]
        wider = probs.astype(f32)
        upstream = jnp.where(mine, grad_context, none)
        weighted = wider * dot(v, upstream, NT)
        balance = jnp.sum(weighted, axis=0, keepdims=True)
        grad_scores = (weighted - wider * balance).astype(bf16)
        grad_v = grad_v + dot(probs, upstream)
        grad_k = grad_k + dot(grad_scores, jnp.where(mine, scaled_q, none))
        grad_q = grad_q + dot(grad_scores, jnp.where(mine, scaled_k, none), TN)
    grad_q = grad_q.astype(bf16)
    grad_k = grad_k.astype(bf16)
    grad_v = grad_v.astype(bf16)
    bias_q[...] = column_sum(grad_q.astype(f32))
    bias_v[...] = column_sum(grad_v.astype(f32))
    x_turned = turned[...]
    pieces = (
        dot(x_turned, grad_q).astype(bf16),
        dot(x_turned, grad_k).astype(bf16),
        dot(x_turned, grad_v).astype(bf16),
    )
    for s in range(steps):

        @pl.when(step == s)
        def _():
            for i, piece in enumerate(pieces):
                pieces_out[i, :, s * wide : (s + 1) * wide] = piece
            pieces_out[3, s * wide : (s + 1) * wide, :] = grad_out

    total[...] += (
        dot(grad_q, wq[...], NT) + dot(grad_k, wk[...], NT) + dot(grad_v, wv[...], NT)
    )

    @pl.when(step == steps - 1)
    def _():
        tokens_out[...] = total[...].astype(bf16)


def attend_back(blocks, attended, sum_one, context, prob, q, k, v, w_qkv, w_out):
    slots, width = blocks[0].shape
    count = slots * len(blocks)
    head_width = width // HEADS
    wide = 4 * head_width
    steps = width // wide

    def weight(part):
        return pl.BlockSpec((width, wide), lambda i: (0, part * steps + i))

    columns = pl.BlockSpec((count, wide), lambda i: (0, i))
    vector = pl.BlockSpec((1, wide), lambda i: (0, i))
    return pl.pallas_call(
        functools.partial(attend_back_kernel, steps=steps, slots=slots, head_width=head_width),
        grid=(steps,),
        in_specs=[whole((slots, width))] * 4
        + [
            whole((count, width)), whole((count, width)), columns,
            pl.BlockSpec((4, count, count), lambda i: (i, 0, 0)),
            columns, columns, columns, weight(0), weight(1), weight(2),
            pl.BlockSpec((wide, width), lambda i: (i, 0)),
        ],
        out_specs=[whole((4, width, width)), whole((count, width)), vector, vector],
        out_shape=[
            jax.ShapeDtypeStruct((4, width, width), bf16),
            jax.ShapeDtypeStruct((count, width), bf16),
            jax.ShapeDtypeStruct((1, width), f32),
            jax.ShapeDtypeStruct((1, width), f32),
        ],
        scratch_shapes=[pltpu.VMEM((width, count), bf16), pltpu.VMEM((count, width), f32)],
        compiler_params=params(),
        cost_estimate=cost(16 * count * width * width, 40 * 2**20),
        name="attend_back",
    )(*blocks, attended, sum_one, context, prob, q, k, v, w_qkv, w_qkv, w_qkv, w_out)


def swap(block, axis, bit):
    return lax.ppermute(block, axis, [(i, i ^ bit) for i in range(lax.axis_size(axis))])


def pick(block, index, dim=0):
    return lax.dynamic_index_in_dim(block, index, dim, keepdims=False)


def own_bit(axis, bit):
    return (lax.axis_index(axis) // bit) % 2


def added(terms):
    total = terms[0].astype(f32)
    for term in terms[1:]:
        total = total + term.astype(f32)
    return total


def reduce_pieces(piece, order):
    dims = [("blk", 2), ("blk", 1)] + [("dp", 1 << i) for i in reversed(range(dp_bits()))]
    terms = [piece]
    for stage in order:
        at = dims.index(stage)
        dims.pop(at)
        mine = own_bit(*stage)
        sent = added([pick(t, 1 - mine, at) for t in terms]).astype(bf16)
        terms = [pick(t, mine, at) for t in terms] + [swap(sent, *stage)]
    return added(terms).astype(bf16)


def dp_bits():
    return lax.axis_size("dp").bit_length() - 1


def spread(piece):
    position = lax.axis_index("blk")
    across = swap(piece, "blk", 2)
    pair = jnp.stack([piece, across])
    other = swap(pair, "blk", 1)
    every = jnp.stack([pair, other], axis=1)
    every = every.reshape((4,) + piece.shape)
    return [pick(every, position ^ i) for i in range(4)]


def shards(
    tokens, lengths, w_qkv, bias_qv, w_out, bias_out, norm1_gain, norm1_bias, w_up, bias_up,
    w_down, bias_down, norm2_gain, norm2_bias, cotangent,
):
    rows, slots, width = tokens.shape
    hidden = w_up.shape[1]
    shares = lax.axis_size("dp")
    position = lax.axis_index("blk")
    group = lax.axis_index("dp")

    def gather_row(array):
        return [pick(array, position)] + [
            swap(pick(array, position ^ i), "blk", i) for i in range(1, rows)
        ]

    def scatter_row(array):
        parts = array.reshape(rows, slots, width)
        parts = jnp.stack([parts[0]] + [swap(parts[i], "blk", i) for i in range(1, rows)])
        return jnp.stack([pick(parts, position ^ i) for i in range(rows)])

    row = jnp.concatenate([pick(lengths, position), position[None].astype(jnp.int32)])
    blocks = gather_row(tokens)
    cotangent_row = jnp.concatenate(gather_row(cotangent))
    q, k, v, prob, context, normed, inverse = attend(row, blocks, w_qkv, bias_qv, w_out, bias_out)
    active, slope, outputs, lowered, sum_two, first, vector_two = feed(
        normed, norm1_gain, norm1_bias, w_up, bias_up, w_down, bias_down,
        norm2_gain, norm2_bias, cotangent_row,
    )
    grad_down, grad_up, grad_bias_up, attended, sum_one, vector_one = feed_back(
        lowered, active, slope, w_down, w_up, first, sum_two, normed, inverse, norm1_gain
    )
    pieces, grad_tokens, grad_bias_q, grad_bias_v = attend_back(
        blocks, attended, sum_one, context, prob, q, k, v, w_qkv, w_out
    )

    bits = dp_bits()
    halves = (2,) * bits
    share = width // shares
    dp_dims = [("dp", 1 << i) for i in range(bits)]
    turns = [("blk", 2)] + dp_dims[:2]
    rest = dp_dims[2:]
    core = [("blk", 1)]

    def turned(first_turn):
        return core + turns[first_turn:] + turns[:first_turn] + rest

    down_piece = jnp.moveaxis(
        grad_down.reshape(shares, 4, hidden // shares // 4, width), 1, 0
    ).reshape((2, 2) + halves + (hidden // shares // 4, width))
    down = reduce_pieces(down_piece, turned(0))
    up = reduce_pieces(grad_up.reshape((2, 2) + halves + (share, hidden // 4)), turned(1))
    qkv = reduce_pieces(pieces.reshape((2, 2) + halves + (share, width)), turned(2))

    vectors = jnp.concatenate(
        [grad_bias_q, grad_bias_v, vector_one[:3], vector_two[:3], grad_bias_up.reshape(-1, width)]
    )
    for axis, bit in core + turns + rest:
        vectors = vectors + swap(vectors, axis, bit)

    def own_share(vector):
        flat = vector.reshape(-1)
        size = flat.shape[0] // shares
        return lax.dynamic_slice_in_dim(flat, group * size, size)

    down = jnp.concatenate(spread(down)).astype(f32)
    up = jnp.concatenate(spread(up), axis=1).astype(f32)
    grad_q, grad_k, grad_v, grad_out = spread(qkv)
    return (
        scatter_row(outputs),
        scatter_row(grad_tokens),
        jnp.concatenate([grad_q, grad_k, grad_v], axis=1).astype(f32),
        own_share(vectors[0:2]),
        grad_out.astype(f32),
        own_share(vectors[4]),
        own_share(vectors[2]),
        own_share(vectors[3]),
        up,
        own_share(vectors[8:]),
        down,
        own_share(vectors[7]),
        own_share(vectors[5]),
        own_share(vectors[6]),
    )


def solution(mesh):
    row_spec = P("dp", "blk", None)
    in_specs = (row_spec, P("dp", None)) + (P(),) * 12 + (row_spec,)
    wide, flat = P("dp", None), P("dp")
    out_specs = (
        row_spec, row_spec, wide, flat, wide, flat, flat, flat, wide, flat, wide, flat, flat, flat,
    )
    return jax.shard_map(shards, mesh=mesh, in_specs=in_specs, out_specs=out_specs, check_vma=False)
```

```python
import functools
import math

import jax
import jax.numpy as jnp
from jax import lax
from jax.experimental import pallas as pl
from jax.experimental.pallas import tpu as pltpu
from jax.sharding import PartitionSpec as P

HEADS = 12
EPSILON = 1e-12
MASKED = -1e30
f32 = jnp.float32
bf16 = jnp.bfloat16
NN = (((1,), (0,)), ((), ()))
NT = (((1,), (1,)), ((), ()))
TN = (((0,), (0,)), ((), ()))
VMEM = pl.BlockSpec(memory_space=pltpu.VMEM)
SMEM = pl.BlockSpec(memory_space=pltpu.SMEM)
HBM = pl.BlockSpec(memory_space=pltpu.HBM)
ANY = pl.BlockSpec(memory_space=pl.ANY)


WEIGHTS = {
    "attend": 20 * 10**9, "feed": 20 * 10**9, "grad_down": 20 * 10**9, "grad_up": 10**7,
    "first_back": 20 * 10**9, "attend_back": 40 * 10**9, "grad_tokens": 10 * 10**9,
}


def dot(left, right, dims=NN):
    return lax.dot_general(left, right, dims, preferred_element_type=f32)


def call(
    kernel, name, scalars, arrays, outs, flops, scratch=(), far=(), far_outs=(), copies=0, room=8, after=()
):
    scratch = list(scratch)
    if copies:
        scratch.append(pltpu.SemaphoreType.DMA((copies,)))
    first, last = len(scalars) + len(arrays) + len(far), len(after)

    def body(*refs):
        kernel(*refs[:first], *refs[first + last :])

    return pl.pallas_call(
        body,
        in_specs=[SMEM] * len(scalars) + [VMEM] * len(arrays) + [HBM] * len(far) + [ANY] * last,
        out_specs=[VMEM] * len(outs) + [HBM] * len(far_outs),
        out_shape=[*outs, *[pltpu.HBM(a.shape, a.dtype) for a in far_outs]],
        scratch_shapes=scratch,
        compiler_params=pltpu.CompilerParams(vmem_limit_bytes=room * 2**20),
        cost_estimate=pl.CostEstimate(flops=WEIGHTS.get(name, 0), bytes_accessed=0, transcendentals=0),
        name=name,
    )(
        *scalars, *arrays, *[pltpu.with_memory_space_constraint(a, pltpu.HBM) for a in far], *after
    )


def shape(*dims, dtype=bf16):
    return jax.ShapeDtypeStruct(dims, dtype)


def cut(i, size):
    return pl.ds(pl.multiple_of(i * size, size), size)


def copy(source, target, semaphore):
    return pltpu.make_async_copy(source, target, semaphore)


def column_sum(values):
    return jnp.sum(values, axis=0, keepdims=True)


def row_mean(values):
    return jnp.mean(values, axis=-1, keepdims=True)


def normalize(inputs):
    centre = inputs - row_mean(inputs)
    inverse = lax.rsqrt(row_mean(centre * centre) + EPSILON)
    return centre * inverse, inverse


def normalize_back(scaled, normed, inverse):
    return inverse * (scaled - row_mean(scaled) - normed * row_mean(scaled * normed))


BIAS_Q, BIAS_V, BIAS_OUT, GAIN_ONE, SHIFT_ONE, BIAS_DOWN, GAIN_TWO, SHIFT_TWO, BIAS_UP = range(9)


def vector(ref, row):
    return ref[row : row + 1, :]


def attend_kernel(
    row_ref, x0, x1, x2, x3, vectors, w_qkv, w_out,
    normed_out, inverse_out, q_out, k_out, v_out, prob_out, context_out, tokens_out,
    weights, out_weights, tokens, mask, q_kept, k_kept, v_kept, context_kept, probs_kept, sems,
    *, pages, head_width,
):
    slots = x0.shape[0]
    count, width = tokens.shape
    wide = 4 * head_width
    groups = width // wide

    def load(i, part):
        here = cut(i + part * groups, wide)
        return copy(w_qkv.at[:, here], weights.at[i, part], sems.at[3 * i + part])

    def keep(i, number, source, target):
        return copy(source.at[:, cut(i, wide)], target.at[:, cut(i, wide)], sems.at[number * groups + i])

    def keep_probs(i):
        return copy(probs_kept.at[i], prob_out.at[pl.ds(4 * i, 4)], sems.at[7 * groups + i])

    kept = ((3, q_kept, q_out), (4, k_kept, k_out), (5, v_kept, v_out), (6, context_kept, context_out))
    for part in range(3):
        load(0, part).start()
    load_out = copy(w_out, out_weights, sems.at[8 * groups])
    for i, block in enumerate((x0, x1, x2, x3)):
        tokens[i * slots : (i + 1) * slots, :] = block[...]
    keep_tokens = copy(tokens, tokens_out, sems.at[8 * groups + 1])
    keep_tokens.start()
    position = row_ref[pages]

    def page_of(shape, dim):
        at = lax.broadcasted_iota(jnp.int32, shape, dim)
        slot = ((at // slots) ^ position) * slots + at % slots
        page = jnp.zeros(shape, jnp.int32)
        end = 0
        for c in range(pages):
            end = end + row_ref[c]
            page = page + (slot >= end).astype(jnp.int32)
        return page

    mask[...] = jnp.where(
        page_of((count, count), 0) == page_of((1, count), 1), 0.0, MASKED
    )
    head = lax.broadcasted_iota(jnp.int32, (count, wide), 1) // head_width
    none = jnp.zeros((count, wide), bf16)

    @pl.loop(0, groups)
    def _(i):
        here = cut(i, wide)

        @pl.when(i + 1 < groups)
        def _():
            for part in range(3):
                load(i + 1, part).start()

        @pl.when(i + 1 == groups)
        def _():
            load_out.start()

        for part in range(3):
            load(i, part).wait()
        x = tokens[...]
        q = (dot(x, weights[i, 0]) + vectors[BIAS_Q : BIAS_Q + 1, here]).astype(bf16)
        k = dot(x, weights[i, 1]).astype(bf16)
        v = (dot(x, weights[i, 2]) + vectors[BIAS_V : BIAS_V + 1, here]).astype(bf16)
        q_kept[:, here] = q
        k_kept[:, here] = k
        v_kept[:, here] = v
        scaled_q = q * jnp.asarray(1.0 / math.sqrt(head_width), bf16)
        context = jnp.zeros((count, wide), f32)
        for h in range(4):
            scores = dot(k, jnp.where(head == h, scaled_q, none), NT) + mask[...]
            powers = jnp.exp(scores - jnp.max(scores, axis=0, keepdims=True))
            probs = (powers * (1.0 / jnp.sum(powers, axis=0, keepdims=True))).astype(bf16)
            probs_kept[i, h] = probs
            context = context + dot(probs, jnp.where(head == h, v, none), TN)
        context_kept[:, here] = context.astype(bf16)
        for number, source, target in kept:
            keep(i, number, source, target).start()
        keep_probs(i).start()

    load_out.wait()
    attended = dot(context_kept[...], out_weights[...]) + vector(vectors, BIAS_OUT)
    normed, inverse = normalize(tokens[...].astype(f32) + attended)
    normed_out[...] = normed
    inverse_out[...] = inverse
    for i in range(groups):
        for number, source, target in kept:
            keep(i, number, source, target).wait()
        keep_probs(i).wait()
    keep_tokens.wait()


def attend(row, blocks, w_qkv, w_out, vectors):
    slots, width = blocks[0].shape
    count = slots * len(blocks)
    head_width = width // HEADS
    wide = 4 * head_width
    groups = width // wide
    narrow, full = shape(count, width), shape(count, width, dtype=f32)
    rows = pltpu.VMEM((count, width), bf16)
    return call(
        functools.partial(attend_kernel, pages=row.shape[0] - 1, head_width=head_width),
        "attend", [row], [*blocks, vectors],
        [full, shape(count, 1, dtype=f32)],
        8 * count * width * width + 16 * count * count * width,
        [
            pltpu.VMEM((groups, 3, width, wide), bf16), pltpu.VMEM((width, width), bf16), rows,
            pltpu.VMEM((count, count), f32), rows, rows, rows, rows,
            pltpu.VMEM((groups, 4, count, count), bf16),
        ],
        [w_qkv, w_out],
        [narrow, narrow, narrow, shape(HEADS, count, count), narrow, narrow],
        8 * groups + 2, 26,
    )


def feed_kernel(
    normed_one, vectors, c0, c1, c2, c3, w_up, w_down,
    active_out, slope_out, r0, r1, r2, r3, lowered_out, first_out, vector_out, sum_out, normed_far,
    total, sems,
):
    width = w_up.shape[0]
    steps = w_up.shape[1] // width

    keep_normed = copy(normed_one, normed_far, sems.at[0])
    keep_normed.start()
    first_norm = normed_one[...] * vector(vectors, GAIN_ONE) + vector(vectors, SHIFT_ONE)
    first_out[...] = first_norm.astype(bf16)
    total[...] = first_norm + vector(vectors, BIAS_DOWN)

    @pl.loop(0, steps)
    def _(i):
        here = cut(i, width)

        raised = dot(first_out[...], w_up[:, here]) + vectors[pl.ds(BIAS_UP + i, 1), :]
        cumulative = 0.5 * (1.0 + lax.erf(raised * (1.0 / math.sqrt(2.0))))
        activated = (raised * cumulative).astype(bf16)
        active_out[:, here] = activated
        bell = jnp.exp(-0.5 * raised * raised) * (1.0 / math.sqrt(2.0 * math.pi))
        slope_out[:, here] = (cumulative + raised * bell).astype(bf16)
        total[...] += dot(activated, w_down[here, :])

    normed, inverse = normalize(total[...])
    gain = vector(vectors, GAIN_TWO)
    result = (normed * gain + vector(vectors, SHIFT_TWO)).astype(bf16)
    slots = c0.shape[0]
    for i, block in enumerate((r0, r1, r2, r3)):
        block[...] = result[i * slots : (i + 1) * slots, :]
    upstream = jnp.concatenate([c0[...], c1[...], c2[...], c3[...]]).astype(f32)
    grad_sum = normalize_back(upstream * gain, normed, inverse)
    total[...] = grad_sum
    keep_sum = copy(total, sum_out, sems.at[1])
    keep_sum.start()
    lowered = grad_sum.astype(bf16)
    lowered_out[...] = lowered
    vector_out[0:1, :] = column_sum(upstream * normed)
    vector_out[1:2, :] = column_sum(upstream)
    vector_out[2:3, :] = column_sum(lowered.astype(f32))
    keep_sum.wait()
    keep_normed.wait()


def feed(normed, w_up, w_down, vectors, cotangents):
    count, width = normed.shape
    hidden = w_up.shape[1]
    narrow, full = shape(count, width), shape(count, width, dtype=f32)
    return call(
        feed_kernel, "feed", [], [normed, vectors, *cotangents, w_up, w_down],
        [shape(count, hidden)] * 2
        + [shape(*cotangents[0].shape)] * 4
        + [narrow, narrow, shape(8, width, dtype=f32)],
        4 * count * width * hidden,
        [pltpu.VMEM((count, width), f32)], [], [full, full], 2, 14,
    )


def grad_down_kernel(place, active, lowered, keep, send, *, shares):
    width = lowered.shape[1]
    hidden = active.shape[1]
    rows = hidden // shares // 4
    odd = place[0] == 1

    @pl.loop(0, hidden // width)
    def _(i):
        value = dot(active[:, cut(i, width)], lowered[...], TN).astype(bf16)
        count = width // rows // 4
        for d in range(count):
            for x in range(2):
                at = (d * 4 + x * 2) * rows
                first = value[at : at + rows, :]
                second = value[at + rows : at + 2 * rows, :]
                keep[x, i * count + d] = jnp.where(odd, second, first)
                send[x, i * count + d] = jnp.where(odd, first, second)


def grad_down_plain(active, lowered, down):
    width = lowered.shape[1]

    @pl.loop(0, active.shape[1] // width)
    def _(i):
        down[cut(i, width), :] = dot(active[:, cut(i, width)], lowered[...], TN).astype(bf16)


def grad_down(place, active, lowered, shares):
    count, width = lowered.shape
    hidden = active.shape[1]
    rows = hidden // shares // 4
    flops = 2 * count * width * hidden
    if rows % 16 or width % (4 * rows):
        (whole,) = call(
            grad_down_plain, "grad_down", [], [active, lowered], [shape(hidden, width)], flops,
            room=12,
        )
        parts = jnp.moveaxis(whole.reshape(shares, 2, 2, rows, width), 0, 2)
        parts = [parts[:, i] for i in range(2)]
        odd = place[0] == 1
        return jnp.where(odd, parts[1], parts[0]), jnp.where(odd, parts[0], parts[1])
    return call(
        functools.partial(grad_down_kernel, shares=shares), "grad_down",
        [place], [active, lowered], [shape(2, shares, rows, width)] * 2, flops, room=12,
    )


def grad_up_kernel(
    place, lowered, slope, first, w_down, raised_out, keep, send, bias_out, turned
):
    width = lowered.shape[1]
    turned[...] = first[...].T

    def work(b):
        here = cut(b, width)
        raised = dot(lowered[...], w_down[here, :], NT) * slope[:, here].astype(f32)
        raised = raised.astype(bf16)
        raised_out[:, here] = raised
        bias_out[pl.ds(b, 1), :] = column_sum(raised.astype(f32))
        return dot(turned[...], raised).astype(bf16)

    @pl.loop(0, 2)
    def _(x):
        send[x] = work(2 * x + 1 - place[0])
        keep[x] = work(2 * x + place[0])


def grad_up(place, lowered, slope, w_down, first):
    count, width = lowered.shape
    hidden = w_down.shape[0]
    return call(
        grad_up_kernel, "grad_up", [place], [lowered, slope, first, w_down],
        [shape(count, hidden)] + [shape(2, width, width)] * 2
        + [shape(hidden // width, width, dtype=f32)],
        4 * count * width * hidden,
        [pltpu.VMEM((width, count), bf16)], room=12,
    )


def first_back_kernel(
    raised, inverse_one, vectors, w_up, sum_two, normed_one,
    attended_out, vector_out, sum_out, total, sum_kept, normed, sems,
):
    load_sum = copy(sum_two, sum_kept, sems.at[0])
    load_sum.start()
    load_normed = copy(normed_one, normed, sems.at[1])
    load_normed.start()
    total[...] = dot(raised[...], w_up[...], NT)

    load_sum.wait()
    load_normed.wait()
    upstream = total[...] + sum_kept[...]
    grad_sum = normalize_back(
        upstream * vector(vectors, GAIN_ONE), normed[...], inverse_one[...]
    )
    total[...] = grad_sum
    keep_sum = copy(total, sum_out, sems.at[2])
    keep_sum.start()
    attended = grad_sum.astype(bf16)
    attended_out[...] = attended
    vector_out[0:1, :] = column_sum(upstream * normed[...])
    vector_out[1:2, :] = column_sum(upstream)
    vector_out[2:3, :] = column_sum(attended.astype(f32))
    keep_sum.wait()


def first_back(raised, w_up, sum_two, normed, inverse, vectors, after):
    count, width = normed.shape
    hidden = w_up.shape[1]
    full = shape(count, width, dtype=f32)
    rows = pltpu.VMEM((count, width), f32)
    return call(
        first_back_kernel, "first_back", [], [raised, inverse, vectors, w_up],
        [shape(count, width), shape(8, width, dtype=f32)],
        2 * count * width * hidden,
        [rows, rows, rows], [sum_two, normed], [full], 3, 14, after,
    )


def small_pieces(shares, width):
    q, v, gain_one, shift_one, out, gain_two, shift_two, down, up = range(9)
    share = width // shares

    def flat(row, first):
        return row + first // width, first % width

    def pieces(d):
        at = d * share
        return (
            (flat(q, 2 * at), flat(q, 2 * at + share), (out, at)),
            ((gain_one, at), (shift_one, at), (down, at)),
            ((gain_two, at), (shift_two, at), flat(up, 4 * at)),
            tuple(flat(up, 4 * at + j * share) for j in (1, 2, 3)),
        )

    return [pieces(d) for d in range(shares)]


def attend_back_kernel(
    place, attended, vector_one, vector_two, bias_up, tokens, context, prob, q_ref, k_ref, v_ref, w_out,
    keep_0, keep_1, keep_2, send_0, send_1, send_2, small_keep, small_send, grads_out,
    rows_kept, turned, turned_context, probs_kept, q_kept, k_kept, v_kept, weights, sums, small, sems,
    *, head_width,
):
    count, width = attended.shape
    wide = 4 * head_width
    groups = width // wide
    shares = small_keep.shape[1]

    def load(i):
        here = cut(i, wide)
        pairs = (
            (w_out.at[here, :], weights.at[here, :]),
            (v_ref.at[:, here], v_kept.at[:, here]),
            (prob.at[pl.ds(4 * i, 4)], probs_kept.at[i]),
            (q_ref.at[:, here], q_kept.at[:, here]),
            (k_ref.at[:, here], k_kept.at[:, here]),
        )
        return [copy(s, t, sems.at[5 * i + n]) for n, (s, t) in enumerate(pairs)]

    load_tokens = copy(tokens, rows_kept.at[0], sems.at[5 * groups])
    load_context = copy(context, rows_kept.at[1], sems.at[5 * groups + 1])
    load_tokens.start()
    load_context.start()
    for one in load(0):
        one.start()
    load_tokens.wait()
    turned[...] = rows_kept[0].T
    load_context.wait()
    turned_context[...] = rows_kept[1].T
    head = lax.broadcasted_iota(jnp.int32, (count, wide), 1) // head_width
    none = jnp.zeros((count, wide), bf16)
    odd = place[0] == 1

    @pl.loop(0, groups)
    def _(i):
        here = cut(i, wide)

        @pl.when(i + 1 < groups)
        def _():
            for one in load(i + 1):
                one.start()

        for one in load(i):
            one.wait()
        grad_context = dot(attended[...], weights[here, :], NT).astype(bf16)
        scaling = jnp.asarray(1.0 / math.sqrt(head_width), bf16)
        scaled_q = q_kept[:, here] * scaling
        scaled_k = k_kept[:, here] * scaling
        v = v_kept[:, here]
        grad_q = jnp.zeros((count, wide), f32)
        grad_k = grad_q
        grad_v = grad_q
        for h in range(4):
            mine = head == h
            probs = probs_kept[i, h]
            wider = probs.astype(f32)
            upstream = jnp.where(mine, grad_context, none)
            weighted = wider * dot(v, upstream, NT)
            balance = jnp.sum(weighted, axis=0, keepdims=True)
            grad_scores = (weighted - wider * balance).astype(bf16)
            grad_v = grad_v + dot(probs, upstream)
            grad_k = grad_k + dot(grad_scores, jnp.where(mine, scaled_q, none))
            grad_q = grad_q + dot(grad_scores, jnp.where(mine, scaled_k, none), TN)
        grad_q = grad_q.astype(bf16)
        grad_k = grad_k.astype(bf16)
        grad_v = grad_v.astype(bf16)
        grads_out[:, here] = grad_q
        grads_out[:, cut(i + groups, wide)] = grad_k
        grads_out[:, cut(i + 2 * groups, wide)] = grad_v
        sums[0:1, here] = column_sum(grad_q.astype(f32))
        sums[1:2, here] = column_sum(grad_v.astype(f32))
        pieces = (
            dot(turned[...], grad_q).astype(bf16),
            dot(turned[...], grad_k).astype(bf16),
            dot(turned[...], grad_v).astype(bf16),
            dot(turned_context[...], attended[:, here]).astype(bf16),
        )
        for s, (keep, send) in enumerate(((keep_0, send_0), (keep_1, send_1), (keep_2, send_2))):

            @pl.when(i == s)
            def _(keep=keep, send=send):
                for x in range(2):
                    keep[x] = jnp.where(odd, pieces[2 * x + 1], pieces[2 * x])
                    send[x] = jnp.where(odd, pieces[2 * x], pieces[2 * x + 1])

    sums[2:5, :] = vector_one[0:3, :]
    sums[5:8, :] = vector_two[0:3, :]
    sums[8:12, :] = bias_up[...]
    share = width // shares
    small[...] = jnp.zeros_like(small)
    for d, by_blk in enumerate(small_pieces(shares, width)):
        for b, three in enumerate(by_blk):
            for j, (row, column) in enumerate(three):
                small[b, d, j : j + 1, 0:share] = sums[row : row + 1, column : column + share]
    for x in range(2):
        even_part = small[2 * x].astype(bf16)
        odd_part = small[2 * x + 1].astype(bf16)
        small_keep[x] = jnp.where(odd, odd_part, even_part)
        small_send[x] = jnp.where(odd, even_part, odd_part)


def attend_back(place, attended, small, far, shares, after):
    count, width = attended.shape
    head_width = width // HEADS
    wide = 4 * head_width
    groups = width // wide
    rows, turned = pltpu.VMEM((count, width), bf16), pltpu.VMEM((width, count), bf16)
    keep_0, keep_1, keep_2, send_0, send_1, send_2, small_keep, small_send, grads = call(
        functools.partial(attend_back_kernel, head_width=head_width),
        "attend_back", [place], [attended, *small],
        [shape(2, width, wide)] * 6 + [shape(2, shares, 16, wide)] * 2 + [shape(count, 3 * width)],
        10 * count * width * width + 40 * count * count * width,
        [
            pltpu.VMEM((2, count, width), bf16), turned, turned,
            pltpu.VMEM((groups, 4, count, count), bf16), rows, rows, rows,
            pltpu.VMEM((width, width), bf16),
            pltpu.VMEM((16, width), f32), pltpu.VMEM((4, shares, 16, wide), f32),
        ],
        far, [], 5 * groups + 2, 28, after,
    )
    return [keep_0, keep_1, keep_2], [send_0, send_1, send_2], small_keep, small_send, grads


def grad_tokens_kernel(grads, sum_one, w_qkv, r0, r1, r2, r3, total, weights, sems):
    width = sum_one.shape[1]

    def load(i):
        return copy(w_qkv.at[:, cut(i, width)], weights.at[i], sems.at[i])

    load_sum = copy(sum_one, total, sems.at[3])
    load(0).start()
    load_sum.start()
    load(1).start()
    load_sum.wait()

    @pl.loop(0, 3)
    def _(i):
        @pl.when(i == 0)
        def _():
            load(2).start()

        load(i).wait()
        total[...] += dot(grads[:, cut(i, width)], weights[i], NT)

    result = total[...].astype(bf16)
    slots = r0.shape[0]
    for i, block in enumerate((r0, r1, r2, r3)):
        block[...] = result[i * slots : (i + 1) * slots, :]


def grad_tokens(sum_one, grads, w_qkv, slots, after):
    count, width = sum_one.shape
    return call(
        grad_tokens_kernel, "grad_tokens", [], [grads], [shape(slots, width)] * 4,
        6 * count * width * width,
        [pltpu.VMEM((count, width), f32), pltpu.VMEM((3, width, width), bf16)],
        [sum_one, w_qkv], [], 4, 12, after,
    )


def swap(block, axis, bit):
    return lax.ppermute(block, axis, [(i, i ^ bit) for i in range(lax.axis_size(axis))])


def pick(block, index, dim=0):
    return lax.dynamic_index_in_dim(block, index, dim, keepdims=False)


def every(count, work):
    if count <= 8:
        for number in range(count):
            work(number)
    else:
        pl.loop(0, count)(work)


def cut_units(bits, units, extra, orders, flip, after):
    parts, dims = len(orders), len(orders[0])
    arrays, numbers = [], {}
    for array in [a for unit in units for part in unit for a in part[:2]] + list(extra):
        if id(array) not in numbers:
            numbers[id(array)] = len(arrays)
            arrays.append(array)
    rows = arrays[0].shape[-2]
    size = sum({id(part[0]): part[0].shape[-1] for part in units[0]}.values()) // parts
    more = [extra[0].shape[-2] if extra and s == 0 else 0 for s in range(parts)]
    outs = [shape(2 ** (dims - 1), len(units) * rows + m, size) for m in more]

    def kernel(bits_ref, *refs):
        ins, results = refs[: len(arrays)], refs[len(arrays) :]

        def work(number):
            for s, order in enumerate(orders):
                index = [None] * dims
                index[order[0]] = bits_ref[order[0]] ^ flip
                for i, n in enumerate(order[1:]):
                    index[n] = (number >> (dims - 2 - i)) & 1
                for u, unit in enumerate(units):
                    kept, arrived, column = unit[s]
                    at = (*index, slice(None), slice(column * size, (column + 1) * size))
                    total = ins[numbers[id(kept)]][at] + ins[numbers[id(arrived)]][at]
                    results[s][number, u * rows : (u + 1) * rows] = total
                if more[s]:
                    kept, arrived = [ins[numbers[id(a)]] for a in extra]
                    at = tuple(index)
                    results[s][number, len(units) * rows :] = kept[at] + arrived[at]

        every(2 ** (dims - 1), work)

    return call(kernel, "cut_units", [bits], arrays, outs, 0, after=after)


def halve(bits, pairs, axes, join, after=()):
    taken = pairs[0][0].shape[0] // (2 if axes else 1)
    sizes = [a.shape[1] for a, _ in pairs]
    width = pairs[0][0].shape[2]
    flips = (1, 0) if axes else (0,)
    outs = [shape(taken, sum(sizes), width)] if join else [shape(taken, n, width) for n in sizes]
    arrays = [a for pair in pairs for a in pair]

    def kernel(bits_ref, *refs):
        ins, results = refs[: len(arrays)], refs[len(arrays) :]

        def work(number):
            for f, flip in enumerate(flips):
                for s in range(len(pairs)):
                    at = number + ((bits_ref[axes[s]] ^ flip) * taken if axes else 0)
                    total = ins[2 * s][at] + ins[2 * s + 1][at]
                    if join:
                        first = sum(sizes[:s])
                        results[f][number, first : first + sizes[s]] = total
                    else:
                        results[f * len(pairs) + s][number] = total

        every(taken, work)

    made = call(kernel, "halve", [bits], arrays, outs * len(flips), 0, after=after)
    return made[: len(outs)], made[len(outs) :]


class Group:
    def __init__(self, units, extra, bits, names):
        self.units, self.extra, self.bits, self.names = units, extra, bits, names
        size = len(names)
        turn = [0, size - 1, size - 2]
        rest = list(range(size - 3, 0, -1))
        self.orders = [turn[s:] + turn[:s] + rest for s in range(3)]
        self.stage = 0
        self.pairs = None

    def step(self, after=()):
        if self.stage == 0:
            sent = cut_units(self.bits, self.units, self.extra, self.orders, 1, after)
            keep = cut_units(self.bits, self.units, self.extra, self.orders, 0, [sent[0]])
        else:
            axes = [order[self.stage] for order in self.orders]
            sent, keep = halve(self.bits, self.pairs, axes, self.stage == 3, after)
        arrived = [
            swap(block, *self.names[order[self.stage]]) for block, order in zip(sent, self.orders)
        ]
        self.pairs = list(zip(keep, arrived))
        self.stage += 1
        return sent

    def finish(self, after=()):
        (own,), _ = halve(self.bits, self.pairs, None, False, after)
        across = swap(own, "blk", 2)
        return own, swap(own, "blk", 1), across, swap(across, "blk", 1)


def chosen(place, b, refs):
    relative = place[1] ^ b
    values = [ref[...] for ref in refs]
    return jnp.where(
        relative < 2,
        jnp.where(relative == 0, values[0], values[1]),
        jnp.where(relative == 2, values[2], values[3]),
    ).astype(f32)


def place_feed(place, pieces, rows, shares):
    size = pieces[0].shape[2]
    width = 3 * size

    def kernel(place_ref, p0, p1, p2, p3, down, up):
        for b in range(4):
            for s in range(3):
                at = 2 * s * rows
                columns = slice(s * size, (s + 1) * size)
                value = chosen(place_ref, b, [p.at[0, at : at + rows] for p in (p0, p1, p2, p3)])
                down[b * rows : (b + 1) * rows, columns] = value
                at = at + rows
                columns = slice(b * width + s * size, b * width + (s + 1) * size)
                value = chosen(place_ref, b, [p.at[0, at : at + rows] for p in (p0, p1, p2, p3)])
                up[:, columns] = value

    return call(
        kernel, "place_feed", [place], pieces,
        [shape(4 * rows, width, dtype=f32), shape(rows, 4 * width, dtype=f32)], 0,
    )


def place_own(place, pieces, rows, shares):
    size = pieces[0].shape[2]
    width = 3 * size
    share = width // shares
    extra = pieces[0].shape[1] - 3 * rows

    def kernel(place_ref, p0, p1, p2, p3, qkv, out, *small):
        refs = (p0, p1, p2, p3)
        bias_qv, bias_out, gain_one, shift_one, bias_up, bias_down, gain_two, shift_two = small
        for b in range(4):
            for s in range(3):
                at = s * rows + (extra if s else 0)
                value = chosen(place_ref, b, [p.at[0, at : at + rows] for p in refs])
                columns = slice(s * size, (s + 1) * size)
                if b == 3:
                    out[:, columns] = value
                else:
                    qkv[:, b * width + s * size : b * width + (s + 1) * size] = value
            value = chosen(place_ref, b, [p.at[0, rows : rows + extra] for p in refs])
            targets = (
                ((bias_qv, 0), (bias_qv, 1), (bias_out, 0)),
                ((gain_one, 0), (shift_one, 0), (bias_down, 0)),
                ((gain_two, 0), (shift_two, 0), (bias_up, 0)),
                ((bias_up, 1), (bias_up, 2), (bias_up, 3)),
            )[b]
            for j, (ref, part) in enumerate(targets):
                ref[:, part * share : (part + 1) * share] = value[j : j + 1, 0:share]

    vectors = [shape(1, n * share, dtype=f32) for n in (2, 1, 1, 1, 4, 1, 1, 1)]
    return call(
        kernel, "place_own", [place], pieces,
        [shape(rows, 3 * width, dtype=f32), shape(rows, width, dtype=f32), *vectors], 0,
    )


def place_rows(place, blocks, after):
    slots, width = blocks[0].shape

    def kernel(place_ref, *refs):
        for i in range(4):
            refs[4][place_ref[1] ^ i] = refs[i][...]

    return call(kernel, "place_rows", [place], blocks, [shape(4, slots, width)], 0, after=after)[0]


def shards(
    tokens, lengths, w_qkv, bias_qv, w_out, bias_out, norm1_gain, norm1_bias, w_up, bias_up,
    w_down, bias_down, norm2_gain, norm2_bias, cotangent,
):
    rows, slots, width = tokens.shape
    shares = lax.axis_size("dp")
    dp_bits = shares.bit_length() - 1
    position = lax.axis_index("blk").astype(jnp.int32)
    group = lax.axis_index("dp").astype(jnp.int32)
    place = jnp.stack([position % 2, position])
    names = [("blk", 2)] + [("dp", 1 << i) for i in reversed(range(dp_bits))]
    bits = jnp.stack([position // 2] + [(group >> i) % 2 for i in reversed(range(dp_bits))])

    def gather_row(array):
        return [pick(array, position)] + [
            swap(pick(array, position ^ i), "blk", i) for i in (2, 3, 1)
        ]

    def in_order(blocks):
        return [blocks[0], blocks[3], blocks[1], blocks[2]]

    def scatter_row(blocks, after=()):
        moved = [blocks[0]] + [swap(blocks[i], "blk", i) for i in range(1, rows)]
        return place_rows(place, moved, after)

    vectors = jnp.concatenate(
        [bias_qv, bias_out, norm1_gain, norm1_bias, bias_down, norm2_gain, norm2_bias, bias_up]
    ).reshape(-1, width)
    row = jnp.concatenate([pick(lengths, position), position[None]])
    blocks = gather_row(tokens)
    blocks, cotangent = lax.optimization_barrier((blocks, cotangent))
    blocks = in_order(blocks)
    cotangents = in_order(gather_row(cotangent))
    normed, inverse, q, k, v, prob, context, row_tokens = attend(
        row, blocks, w_qkv, w_out, vectors
    )
    active, slope, o0, o1, o2, o3, lowered, first, vector_two, sum_two, normed_far = feed(
        normed, w_up, w_down, vectors, cotangents
    )
    keep_down, send_down = grad_down(place, active, lowered, shares)
    got_down = swap(send_down, "blk", 1)
    raised, keep_up, send_up, grad_bias_up = grad_up(place, lowered, slope, w_down, first)
    got_up = swap(send_up, "blk", 1)
    outputs = scatter_row([o0, o1, o2, o3], [raised])
    attended, vector_one, sum_one = first_back(
        raised, w_up, sum_two, normed_far, inverse, vectors, [outputs]
    )

    def chunks(array):
        return array.reshape((2,) * (1 + dp_bits) + (-1, array.shape[-1]))

    def thirds(kept, arrived):
        return [(kept, arrived, s) for s in range(3)]

    feed_group = Group(
        [
            thirds(chunks(keep_down), chunks(got_down)),
            thirds(chunks(keep_up), chunks(got_up)),
        ],
        (), bits, names,
    )
    sent = feed_group.step([attended])
    keeps, sends, small_keep, small_send, grads = attend_back(
        place, attended, [vector_one, vector_two, grad_bias_up],
        [row_tokens, context, prob, q, k, v, w_out], shares, [sent[0]],
    )
    gots = [swap(send, "blk", 1) for send in sends]
    small_got = swap(small_send, "blk", 1)
    sent = feed_group.step([grads])
    tokens_parts = grad_tokens(sum_one, grads, w_qkv, slots, [sent[0]])
    own_group = Group(
        [[(chunks(keep), chunks(got), 0) for keep, got in zip(keeps, gots)]],
        (chunks(small_keep), chunks(small_got)), bits, names,
    )
    sent = own_group.step([tokens_parts[0]])
    for stage in range(2, dp_bits + 1):
        sent = feed_group.step([sent[0]])
        if stage > 2:
            sent = own_group.step([sent[0]])
    sent = own_group.step([sent[0]])
    feed_pieces = feed_group.finish([sent[0]])
    sent = own_group.step([feed_pieces[0]])
    own_pieces = own_group.finish([sent[0]])

    share = width // shares
    down, up = place_feed(place, feed_pieces, share, shares)
    (
        grad_w_qkv, grad_w_out, sum_qv, sum_out, sum_gain_one, sum_shift_one, sum_up, sum_down,
        sum_gain_two, sum_shift_two,
    ) = place_own(place, own_pieces, share, shares)
    return (
        outputs,
        scatter_row(tokens_parts),
        grad_w_qkv,
        sum_qv[0],
        grad_w_out,
        sum_out[0],
        sum_gain_one[0],
        sum_shift_one[0],
        up,
        sum_up[0],
        down,
        sum_down[0],
        sum_gain_two[0],
        sum_shift_two[0],
    )


def solution(mesh):
    row_spec = P("dp", "blk", None)
    in_specs = (row_spec, P("dp", None)) + (P(),) * 12 + (row_spec,)
    wide, flat = P("dp", None), P("dp")
    out_specs = (
        row_spec, row_spec, wide, flat, wide, flat, flat, flat, wide, flat, wide, flat, flat, flat,
    )
    return jax.shard_map(shards, mesh=mesh, in_specs=in_specs, out_specs=out_specs, check_vma=False)
```

```python
import functools
import math

import jax
import jax.numpy as jnp
from jax import lax
from jax.experimental import pallas as pl
from jax.experimental.pallas import tpu as pltpu
from jax.sharding import PartitionSpec as P

HEADS = 12
EPSILON = 1e-12
MASKED = -1e30
f32 = jnp.float32
bf16 = jnp.bfloat16
NN = (((1,), (0,)), ((), ()))
NT = (((1,), (1,)), ((), ()))
TN = (((0,), (0,)), ((), ()))
VMEM = pl.BlockSpec(memory_space=pltpu.VMEM)
SMEM = pl.BlockSpec(memory_space=pltpu.SMEM)
HBM = pl.BlockSpec(memory_space=pltpu.HBM)
ANY = pl.BlockSpec(memory_space=pl.ANY)


WEIGHTS = {
    "prepare": 10**12, "attend": 10**12, "feed": 10**12, "grad_up": 10**12,
    "grad_down": 10**12, "attend_back": 10**12, "grad_tokens": 10**12,
}


def dot(left, right, dims=NN):
    return lax.dot_general(left, right, dims, preferred_element_type=f32)


def call(
    kernel, name, scalars, arrays, outs, scratch=(), far=(), far_outs=(), copies=0, room=10, after=()
):
    scratch = list(scratch)
    if copies:
        scratch.append(pltpu.SemaphoreType.DMA((copies,)))
    first, last = len(scalars) + len(arrays) + len(far), len(after)
    results = len(outs) + len(far_outs)
    mark = jax.ShapeDtypeStruct((8, 128), f32)

    def body(*refs):
        mine = refs[first + last :]
        mine[results][...] = jnp.zeros(mark.shape, mark.dtype)
        kernel(*refs[:first], *mine[:results], *mine[results + 1 :])

    return pl.pallas_call(
        body,
        in_specs=[SMEM] * len(scalars) + [VMEM] * len(arrays) + [HBM] * len(far) + [VMEM] * last,
        out_specs=[VMEM] * len(outs) + [HBM] * len(far_outs) + [VMEM],
        out_shape=[*outs, *[pltpu.HBM(a.shape, a.dtype) for a in far_outs], mark],
        scratch_shapes=scratch,
        compiler_params=pltpu.CompilerParams(vmem_limit_bytes=room * 2**20),
        cost_estimate=pl.CostEstimate(
            flops=WEIGHTS.get(name, 0), bytes_accessed=0, transcendentals=0
        ),
        name=name,
    )(
        *scalars, *arrays, *[pltpu.with_memory_space_constraint(a, pltpu.HBM) for a in far], *after
    )


def shape(*dims, dtype=bf16):
    return jax.ShapeDtypeStruct(dims, dtype)


def cut(i, size):
    return pl.ds(pl.multiple_of(i * size, size), size)


def copy(source, target, semaphore):
    return pltpu.make_async_copy(source, target, semaphore)


def column_sum(values):
    return jnp.sum(values, axis=0, keepdims=True)


def row_mean(values):
    return jnp.mean(values, axis=-1, keepdims=True)


def normalize(inputs):
    centre = inputs - row_mean(inputs)
    inverse = lax.rsqrt(row_mean(centre * centre) + EPSILON)
    return centre * inverse, inverse


def normalize_back(scaled, normed, inverse):
    return inverse * (scaled - row_mean(scaled) - normed * row_mean(scaled * normed))


BIAS_Q, BIAS_V, BIAS_OUT, GAIN_ONE, SHIFT_ONE, BIAS_DOWN, GAIN_TWO, SHIFT_TWO, BIAS_UP = range(9)


def vector(ref, row):
    return ref[row : row + 1, :]


def only(rows, h, height):
    parts = [jnp.zeros((height, rows.shape[1]), rows.dtype)] * (rows.shape[0] // height)
    parts[h] = rows[h * height : (h + 1) * height, :]
    return jnp.concatenate(parts)


def prepare_kernel(row_ref, w_qkv, w_out, qkv_near, out_near, mask, sems, *, pages, slots):
    load_qkv = copy(w_qkv, qkv_near, sems.at[0])
    load_qkv.start()
    load_out = copy(w_out, out_near, sems.at[1])
    load_out.start()
    count = mask.shape[0]
    position = row_ref[pages]

    def page_of(shape, dim):
        at = lax.broadcasted_iota(jnp.int32, shape, dim)
        slot = ((at // slots) ^ position) * slots + at % slots
        page = jnp.zeros(shape, jnp.int32)
        end = 0
        for c in range(pages):
            end = end + row_ref[c]
            page = page + (slot >= end).astype(jnp.int32)
        return page

    mask[...] = jnp.where(
        page_of((count, count), 0) == page_of((1, count), 1), 0.0, MASKED
    )
    load_qkv.wait()
    load_out.wait()


def prepare(row, w_qkv, w_out, slots, count):
    return call(
        functools.partial(prepare_kernel, pages=row.shape[0] - 1, slots=slots),
        "prepare", [row], [],
        [shape(*w_qkv.shape), shape(*w_out.shape), shape(count, count, dtype=f32)],
        far=[w_qkv, w_out], copies=2,
    )[:3]


def attend_kernel(
    x0, x1, x2, x3, vectors, w_qkv, w_out, mask,
    normed_out, inverse_out, q_out, k_out, v_out, prob_out, context_out, tokens_out,
    tokens, q_kept, k_kept, v_kept, context_kept, probs_kept, sems, *, head_width,
):
    slots = x0.shape[0]
    count, width = tokens.shape
    wide = 4 * head_width
    groups = width // wide
    kept = ((0, q_kept, q_out), (1, k_kept, k_out), (2, v_kept, v_out), (3, context_kept, context_out))

    def keep(i, number, source, target):
        here = cut(i, wide)
        return copy(source.at[:, here], target.at[:, here], sems.at[number * groups + i])

    def keep_probs(i, h):
        return copy(
            probs_kept.at[4 * i + h], prob_out.at[4 * i + h], sems.at[4 * groups + 1 + 4 * i + h]
        )

    for i, block in enumerate((x0, x1, x2, x3)):
        tokens[i * slots : (i + 1) * slots, :] = block[...]
    keep_tokens = copy(tokens, tokens_out, sems.at[4 * groups])
    keep_tokens.start()

    @pl.loop(0, groups)
    def _(i):
        here = cut(i, wide)
        x = tokens[...]
        q = (dot(x, w_qkv[:, here]) + vectors[BIAS_Q : BIAS_Q + 1, here]).astype(bf16)
        k = dot(x, w_qkv[:, cut(i + groups, wide)]).astype(bf16)
        v = dot(x, w_qkv[:, cut(i + 2 * groups, wide)]) + vectors[BIAS_V : BIAS_V + 1, here]
        v = v.astype(bf16)
        q_kept[:, here] = q
        k_kept[:, here] = k
        v_kept[:, here] = v
        q_turned = (q * jnp.asarray(1.0 / math.sqrt(head_width), bf16)).T
        v_turned = v.T
        context = []
        for h in range(4):
            scores = dot(k, only(q_turned, h, head_width)) + mask[...]
            powers = jnp.exp(scores - jnp.max(scores, axis=0, keepdims=True))
            probs = (powers * (1.0 / jnp.sum(powers, axis=0, keepdims=True))).astype(bf16)
            probs_kept[4 * i + h] = probs
            keep_probs(i, h).start()
            context.append(dot(v_turned[h * head_width : (h + 1) * head_width, :], probs))
        context_kept[:, here] = jnp.concatenate(context).astype(bf16).T
        for number, source, target in kept:
            keep(i, number, source, target).start()

    attended = dot(context_kept[...], w_out[...]) + vector(vectors, BIAS_OUT)
    normed, inverse = normalize(tokens[...].astype(f32) + attended)
    normed_out[...] = normed
    inverse_out[...] = inverse
    for i in range(groups):
        for number, source, target in kept:
            keep(i, number, source, target).wait()
        for h in range(4):
            keep_probs(i, h).wait()
    keep_tokens.wait()


def attend(blocks, vectors, w_qkv, w_out, mask):
    slots, width = blocks[0].shape
    count = slots * len(blocks)
    groups = HEADS // 4
    narrow = shape(count, width)
    rows = pltpu.VMEM((count, width), bf16)
    return call(
        functools.partial(attend_kernel, head_width=width // HEADS),
        "attend", [], [*blocks, vectors, w_qkv, w_out, mask],
        [shape(count, width, dtype=f32), shape(count, 1, dtype=f32)],
        [rows, rows, rows, rows, rows, pltpu.VMEM((HEADS, count, count), bf16)],
        far_outs=[narrow, narrow, narrow, shape(HEADS, count, count), narrow, narrow],
        copies=4 * groups + 1 + HEADS, room=24,
    )[:8]


def feed_kernel(
    place, normed_one, vectors, c0, c1, c2, c3, w_up, w_down,
    keep_active, send_active, slope_out, lowered_out, first_out, r0, r1, r2, r3, vector_out,
    sum_out, normed_far, total, sems, *, shares,
):
    width = w_up.shape[0]
    hidden = w_up.shape[1]
    keep_normed = copy(normed_one, normed_far, sems.at[0])
    keep_normed.start()
    first_norm = normed_one[...] * vector(vectors, GAIN_ONE) + vector(vectors, SHIFT_ONE)
    first_out[...] = first_norm.astype(bf16)
    total[...] = first_norm + vector(vectors, BIAS_DOWN)
    odd = place[0] == 1
    rows = hidden // shares // 4
    apart = send_active is not None

    @pl.loop(0, hidden // width)
    def _(i):
        here = cut(i, width)
        raised = dot(first_out[...], w_up[:, here]) + vectors[pl.ds(BIAS_UP + i, 1), :]
        cumulative = 0.5 * (1.0 + lax.erf(raised * (1.0 / math.sqrt(2.0))))
        activated = (raised * cumulative).astype(bf16)
        bell = jnp.exp(-0.5 * raised * raised) * (1.0 / math.sqrt(2.0 * math.pi))
        slope_out[:, here] = (cumulative + raised * bell).astype(bf16)
        total[...] += dot(activated, w_down[here, :])
        turned = activated.T
        if apart:
            count = width // rows // 4
            for d in range(count):
                for x in range(2):
                    at = (d * 4 + x * 2) * rows
                    even_part = turned[at : at + rows, :]
                    odd_part = turned[at + rows : at + 2 * rows, :]
                    keep_active[x, i * count + d] = jnp.where(odd, odd_part, even_part)
                    send_active[x, i * count + d] = jnp.where(odd, even_part, odd_part)
        else:
            keep_active[here, :] = turned

    normed, inverse = normalize(total[...])
    gain = vector(vectors, GAIN_TWO)
    result = (normed * gain + vector(vectors, SHIFT_TWO)).astype(bf16)
    slots = c0.shape[0]
    for i, block in enumerate((r0, r1, r2, r3)):
        block[...] = result[i * slots : (i + 1) * slots, :]
    upstream = jnp.concatenate([c0[...], c1[...], c2[...], c3[...]]).astype(f32)
    grad_sum = normalize_back(upstream * gain, normed, inverse)
    total[...] = grad_sum
    keep_sum = copy(total, sum_out, sems.at[1])
    keep_sum.start()
    lowered = grad_sum.astype(bf16)
    lowered_out[...] = lowered
    vector_out[0:1, :] = column_sum(upstream * normed)
    vector_out[1:2, :] = column_sum(upstream)
    vector_out[2:3, :] = column_sum(lowered.astype(f32))
    keep_sum.wait()
    keep_normed.wait()


def feed(place, normed, vectors, cotangents, w_up, w_down, shares):
    count, width = normed.shape
    hidden = w_up.shape[1]
    rows = hidden // shares // 4
    narrow, full = shape(count, width), shape(count, width, dtype=f32)
    apart = rows % 16 == 0 and width % (4 * rows) == 0
    kernel = functools.partial(feed_kernel, shares=shares)
    if apart:
        active = [shape(2, shares, rows, count)] * 2
    else:
        active = [shape(hidden, count)]
        whole = kernel

        def kernel(*refs):
            whole(*refs[:10], None, *refs[10:])

    made = call(
        kernel, "feed", [place], [normed, vectors, *cotangents, w_up, w_down],
        active + [shape(count, hidden), narrow, narrow]
        + [shape(*cotangents[0].shape)] * 4 + [shape(8, width, dtype=f32)],
        [pltpu.VMEM((count, width), f32)], far_outs=[full, full], copies=2, room=14,
    )[:-1]
    if apart:
        return made
    parts = jnp.moveaxis(made[0].reshape(shares, 2, 2, rows, count), 0, 2)
    odd = place[0] == 1
    keep = jnp.where(odd, parts[:, 1], parts[:, 0])
    send = jnp.where(odd, parts[:, 0], parts[:, 1])
    return [keep, send, *made[1:]]


def grad_up_kernel(
    place, lowered, slope, first, w_down, inverse_one, vectors, w_up, sum_two, normed_one,
    keep, send, bias_out, attended_out, vector_out, sum_out,
    turned, raised_kept, weights, normed, total, sems,
):
    width = lowered.shape[1]
    loads = (copy(w_up, weights, sems.at[0]), copy(sum_two, total, sems.at[1]), copy(normed_one, normed, sems.at[2]))
    for one in loads:
        one.start()
    turned[...] = first[...].T

    def work(b):
        here = cut(b, width)
        raised = dot(lowered[...], w_down[here, :], NT) * slope[:, here].astype(f32)
        raised = raised.astype(bf16)
        raised_kept[:, here] = raised
        bias_out[pl.ds(b, 1), :] = column_sum(raised.astype(f32))
        return dot(turned[...], raised).astype(bf16)

    @pl.loop(0, 2)
    def _(x):
        send[x] = work(2 * x + 1 - place[0])
        keep[x] = work(2 * x + place[0])

    for one in loads:
        one.wait()
    upstream = total[...] + dot(raised_kept[...], weights[...], NT)
    grad_sum = normalize_back(
        upstream * vector(vectors, GAIN_ONE), normed[...], inverse_one[...]
    )
    total[...] = grad_sum
    keep_sum = copy(total, sum_out, sems.at[3])
    keep_sum.start()
    attended = grad_sum.astype(bf16)
    attended_out[...] = attended
    vector_out[0:1, :] = column_sum(upstream * normed[...])
    vector_out[1:2, :] = column_sum(upstream)
    vector_out[2:3, :] = column_sum(attended.astype(f32))
    keep_sum.wait()


def grad_up(place, lowered, slope, first, w_down, inverse, vectors, w_up, sum_two, normed):
    count, width = lowered.shape
    hidden = w_down.shape[0]
    full = pltpu.VMEM((count, width), f32)
    return call(
        grad_up_kernel, "grad_up", [place], [lowered, slope, first, w_down, inverse, vectors],
        [shape(2, width, width)] * 2
        + [shape(hidden // width, width, dtype=f32), shape(count, width)]
        + [shape(8, width, dtype=f32)],
        [
            pltpu.VMEM((width, count), bf16), pltpu.VMEM((count, hidden), bf16),
            pltpu.VMEM((width, hidden), bf16), full, full,
        ],
        far=[w_up, sum_two, normed], far_outs=[shape(count, width, dtype=f32)], copies=4, room=28,
    )


def grad_down_kernel(active, other_active, lowered, other_lowered, down):
    _, shares, rows, count = active.shape
    width = lowered.shape[1]

    for x in range(2):

        @pl.loop(0, shares, step=2)
        def _(d):
            mine = active[x, pl.ds(d, 2)].reshape(2 * rows, count)
            other = other_active[x, pl.ds(d, 2)].reshape(2 * rows, count)
            value = dot(mine, lowered[...]) + dot(other, other_lowered[...])
            down[x, pl.ds(d, 2)] = value.astype(bf16).reshape(2, rows, width)


def grad_down(active, other_active, lowered, other_lowered, after):
    _, shares, rows, _ = active.shape
    return call(
        grad_down_kernel, "grad_down", [], [active, other_active, lowered, other_lowered],
        [shape(2, shares, rows, lowered.shape[1])], after=after,
    )


def small_pieces(shares, width):
    q, v, gain_one, shift_one, out, gain_two, shift_two, down, up = range(9)
    share = width // shares

    def flat(row, first):
        return row + first // width, first % width

    def pieces(d):
        at = d * share
        return (
            (flat(q, 2 * at), flat(q, 2 * at + share), (out, at)),
            ((gain_one, at), (shift_one, at), (down, at)),
            ((gain_two, at), (shift_two, at), flat(up, 4 * at)),
            tuple(flat(up, 4 * at + j * share) for j in (1, 2, 3)),
        )

    return [pieces(d) for d in range(shares)]


def attend_back_kernel(
    place, attended, vector_one, vector_two, bias_up, tokens, context, prob, q_ref, k_ref, v_ref, w_out,
    grads_out, keep_0, keep_1, keep_2, send_0, send_1, send_2, small_keep, small_send,
    rows_kept, turned, turned_context, probs_kept, q_kept, k_kept, v_kept, weights, sums, small, sems,
    *, head_width,
):
    count, width = attended.shape
    wide = 4 * head_width
    groups = width // wide
    shares = small_keep.shape[1]

    def load(i):
        here = cut(i, wide)
        pairs = [
            (w_out.at[here, :], weights.at[here, :]),
            (v_ref.at[:, here], v_kept.at[:, here]),
            (q_ref.at[:, here], q_kept.at[:, here]),
            (k_ref.at[:, here], k_kept.at[:, here]),
        ]
        pairs = pairs + [(prob.at[4 * i + h], probs_kept.at[4 * i + h]) for h in range(4)]
        return [copy(s, t, sems.at[8 * i + n]) for n, (s, t) in enumerate(pairs)]

    load_tokens = copy(tokens, rows_kept.at[0], sems.at[8 * groups])
    load_context = copy(context, rows_kept.at[1], sems.at[8 * groups + 1])
    for one in load(0):
        one.start()
    load_tokens.start()
    load_context.start()
    head = lax.broadcasted_iota(jnp.int32, (count, wide), 1) // head_width
    none = jnp.zeros((count, wide), bf16)
    odd = place[0] == 1

    @pl.loop(0, groups)
    def _(i):
        here = cut(i, wide)

        @pl.when(i + 1 < groups)
        def _():
            for one in load(i + 1):
                one.start()

        waits = load(i)
        waits[0].wait()
        grad_context = dot(attended[...], weights[here, :], NT).astype(bf16)
        context_turned = grad_context.T
        scaling = jnp.asarray(1.0 / math.sqrt(head_width), bf16)
        for one in waits[1:4]:
            one.wait()
        scaled_q = q_kept[:, here] * scaling
        k_turned = (k_kept[:, here] * scaling).T
        v = v_kept[:, here]

        @pl.when(i == 0)
        def _():
            load_tokens.wait()
            turned[...] = rows_kept[0].T
            load_context.wait()
            turned_context[...] = rows_kept[1].T

        for one in waits[4:]:
            one.wait()
        grad_k = jnp.zeros((count, wide), f32)
        grad_v = grad_k
        grad_q = []
        for h in range(4):
            mine = head == h
            probs = probs_kept[4 * i + h]
            wider = probs.astype(f32)
            weighted = wider * dot(v, only(context_turned, h, head_width))
            balance = jnp.sum(weighted, axis=0, keepdims=True)
            grad_scores = (weighted - wider * balance).astype(bf16)
            grad_v = grad_v + dot(probs, jnp.where(mine, grad_context, none))
            grad_k = grad_k + dot(grad_scores, jnp.where(mine, scaled_q, none))
            grad_q.append(dot(k_turned[h * head_width : (h + 1) * head_width, :], grad_scores))
        grad_q = jnp.concatenate(grad_q).astype(bf16).T
        grad_k = grad_k.astype(bf16)
        grad_v = grad_v.astype(bf16)
        grads_out[:, here] = grad_q
        grads_out[:, cut(i + groups, wide)] = grad_k
        grads_out[:, cut(i + 2 * groups, wide)] = grad_v
        sums[0:1, here] = column_sum(grad_q.astype(f32))
        sums[1:2, here] = column_sum(grad_v.astype(f32))
        pieces = (
            dot(turned[...], grad_q).astype(bf16),
            dot(turned[...], grad_k).astype(bf16),
            dot(turned[...], grad_v).astype(bf16),
            dot(turned_context[...], attended[:, here]).astype(bf16),
        )
        for s, (keep, send) in enumerate(((keep_0, send_0), (keep_1, send_1), (keep_2, send_2))):

            @pl.when(i == s)
            def _(keep=keep, send=send):
                for x in range(2):
                    keep[x] = jnp.where(odd, pieces[2 * x + 1], pieces[2 * x])
                    send[x] = jnp.where(odd, pieces[2 * x], pieces[2 * x + 1])

    sums[2:5, :] = vector_one[0:3, :]
    sums[5:8, :] = vector_two[0:3, :]
    sums[8:12, :] = bias_up[...]
    share = width // shares
    small[...] = jnp.zeros_like(small)
    for d, by_blk in enumerate(small_pieces(shares, width)):
        for b, three in enumerate(by_blk):
            for j, (row, column) in enumerate(three):
                small[b, d, j : j + 1, 0:share] = sums[row : row + 1, column : column + share]
    for x in range(2):
        even_part = small[2 * x].astype(bf16)
        odd_part = small[2 * x + 1].astype(bf16)
        small_keep[x] = jnp.where(odd, odd_part, even_part)
        small_send[x] = jnp.where(odd, even_part, odd_part)


def attend_back(place, attended, small, far, shares, after):
    count, width = attended.shape
    wide = 4 * (width // HEADS)
    groups = width // wide
    rows, turned = pltpu.VMEM((count, width), bf16), pltpu.VMEM((width, count), bf16)
    grads, keep_0, keep_1, keep_2, send_0, send_1, send_2, small_keep, small_send, mark = call(
        functools.partial(attend_back_kernel, head_width=width // HEADS),
        "attend_back", [place], [attended, *small],
        [shape(count, 3 * width)] + [shape(2, width, wide)] * 6 + [shape(2, shares, 16, wide)] * 2,
        [
            pltpu.VMEM((2, count, width), bf16), turned, turned,
            pltpu.VMEM((HEADS, count, count), bf16), rows, rows, rows,
            pltpu.VMEM((width, width), bf16),
            pltpu.VMEM((16, width), f32), pltpu.VMEM((4, shares, 16, wide), f32),
        ],
        far=far, copies=8 * groups + 2, room=26, after=after,
    )
    return [keep_0, keep_1, keep_2], [send_0, send_1, send_2], small_keep, small_send, grads, mark


def grad_tokens_kernel(grads, w_qkv, sum_one, r0, r1, r2, r3, total, sems):
    load = copy(sum_one, total, sems.at[0])
    load.start()
    product = dot(grads[...], w_qkv[...], NT)
    load.wait()
    result = (total[...] + product).astype(bf16)
    slots = r0.shape[0]
    for i, block in enumerate((r0, r1, r2, r3)):
        block[...] = result[i * slots : (i + 1) * slots, :]


def grad_tokens(sum_one, grads, w_qkv, slots, after):
    count, width = sum_one.shape
    *blocks, mark = call(
        grad_tokens_kernel, "grad_tokens", [], [grads, w_qkv], [shape(slots, width)] * 4,
        [pltpu.VMEM((count, width), f32)], far=[sum_one], copies=1, room=12, after=after,
    )
    return blocks, mark


def swap(block, axis, bit):
    return lax.ppermute(block, axis, [(i, i ^ bit) for i in range(lax.axis_size(axis))])


def pick(block, index, dim=0):
    return lax.dynamic_index_in_dim(block, index, dim, keepdims=False)


def every(count, work):
    if count <= 8:
        for number in range(count):
            work(number)
    else:
        pl.loop(0, count)(work)


def cut_units(bits, units, extra, orders, flip, after):
    parts, dims = len(orders), len(orders[0])
    arrays, numbers = [], {}
    for array in [a for unit in units for terms, _ in unit for a in terms] + list(extra):
        if id(array) not in numbers:
            numbers[id(array)] = len(arrays)
            arrays.append(array)
    rows = arrays[0].shape[-2]
    size = sum({id(terms[0]): terms[0].shape[-1] for terms, _ in units[0]}.values()) // parts
    more = [extra[0].shape[-2] if extra and s == 0 else 0 for s in range(parts)]
    outs = [shape(2 ** (dims - 1), len(units) * rows + m, size) for m in more]

    def kernel(bits_ref, *refs):
        ins, results = refs[: len(arrays)], refs[len(arrays) :]

        def added(terms, at):
            total = ins[numbers[id(terms[0])]][at]
            for term in terms[1:]:
                total = total + ins[numbers[id(term)]][at]
            return total

        def work(number):
            for s, order in enumerate(orders):
                index = [None] * dims
                index[order[0]] = bits_ref[order[0]] ^ flip
                for i, n in enumerate(order[1:]):
                    index[n] = (number >> (dims - 2 - i)) & 1
                for u, unit in enumerate(units):
                    terms, column = unit[s]
                    at = (*index, slice(None), slice(column * size, (column + 1) * size))
                    results[s][number, u * rows : (u + 1) * rows] = added(terms, at)
                if more[s]:
                    results[s][number, len(units) * rows :] = added(extra, tuple(index))

        every(2 ** (dims - 1), work)

    *made, mark = call(kernel, "cut_units", [bits], arrays, outs, after=after)
    return made, mark


def halve(bits, pairs, axes, join, after=()):
    taken = pairs[0][0].shape[0] // (2 if axes else 1)
    sizes = [a.shape[1] for a, _ in pairs]
    width = pairs[0][0].shape[2]
    flips = (1, 0) if axes else (0,)
    outs = [shape(taken, sum(sizes), width)] if join else [shape(taken, n, width) for n in sizes]
    arrays = [a for pair in pairs for a in pair]

    def kernel(bits_ref, *refs):
        ins, results = refs[: len(arrays)], refs[len(arrays) :]

        def work(number):
            for f, flip in enumerate(flips):
                for s in range(len(pairs)):
                    at = number + ((bits_ref[axes[s]] ^ flip) * taken if axes else 0)
                    total = ins[2 * s][at] + ins[2 * s + 1][at]
                    if join:
                        first = sum(sizes[:s])
                        results[f][number, first : first + sizes[s]] = total
                    else:
                        results[f * len(pairs) + s][number] = total

        every(taken, work)

    *made, mark = call(kernel, "halve", [bits], arrays, outs * len(flips), room=6, after=after)
    return made[: len(outs)], made[len(outs) :], mark


class Group:
    def __init__(self, units, extra, bits, names):
        self.units, self.extra, self.bits, self.names = units, extra, bits, names
        size = len(names)
        turn = [0, size - 1, size - 2]
        rest = list(range(size - 3, 0, -1))
        self.orders = [turn[s:] + turn[:s] + rest for s in range(3)]
        self.stage = 0
        self.pairs = None

    def send(self, blocks):
        return [
            swap(block, *self.names[order[self.stage]]) for block, order in zip(blocks, self.orders)
        ]

    def begin(self, after):
        sent, mark = cut_units(self.bits, self.units, self.extra, self.orders, 1, after)
        self.arrived = self.send(sent)
        return mark

    def rest(self, after):
        keep, mark = cut_units(self.bits, self.units, self.extra, self.orders, 0, after)
        self.pairs = list(zip(keep, self.arrived))
        self.stage = 1
        return mark

    def step(self, after):
        axes = [order[self.stage] for order in self.orders]
        sent, keep, mark = halve(self.bits, self.pairs, axes, self.stage == 3, after)
        self.pairs = list(zip(keep, self.send(sent)))
        self.stage += 1
        return mark

    def finish(self, after):
        (own,), _, mark = halve(self.bits, self.pairs, None, False, after)
        across = swap(own, "blk", 2)
        return (own, swap(own, "blk", 1), across, swap(across, "blk", 1)), mark


def chosen(place, b, refs):
    relative = place[1] ^ b
    values = [ref[...] for ref in refs]
    return jnp.where(
        relative < 2,
        jnp.where(relative == 0, values[0], values[1]),
        jnp.where(relative == 2, values[2], values[3]),
    ).astype(f32)


def place_feed(place, pieces, rows, shares):
    size = pieces[0].shape[2]
    width = 3 * size

    def kernel(place_ref, p0, p1, p2, p3, down, up):
        for b in range(4):
            for s in range(3):
                at = 2 * s * rows
                columns = slice(s * size, (s + 1) * size)
                value = chosen(place_ref, b, [p.at[0, at : at + rows] for p in (p0, p1, p2, p3)])
                down[b * rows : (b + 1) * rows, columns] = value
                at = at + rows
                columns = slice(b * width + s * size, b * width + (s + 1) * size)
                value = chosen(place_ref, b, [p.at[0, at : at + rows] for p in (p0, p1, p2, p3)])
                up[:, columns] = value

    return call(
        kernel, "place_feed", [place], pieces,
        [shape(4 * rows, width, dtype=f32), shape(rows, 4 * width, dtype=f32)],
    )[:2]


def place_own(place, pieces, rows, shares):
    size = pieces[0].shape[2]
    width = 3 * size
    share = width // shares
    extra = pieces[0].shape[1] - 3 * rows

    def kernel(place_ref, p0, p1, p2, p3, qkv, out, *small):
        refs = (p0, p1, p2, p3)
        bias_qv, bias_out, gain_one, shift_one, bias_up, bias_down, gain_two, shift_two = small
        for b in range(4):
            for s in range(3):
                at = s * rows + (extra if s else 0)
                value = chosen(place_ref, b, [p.at[0, at : at + rows] for p in refs])
                columns = slice(s * size, (s + 1) * size)
                if b == 3:
                    out[:, columns] = value
                else:
                    qkv[:, b * width + s * size : b * width + (s + 1) * size] = value
            value = chosen(place_ref, b, [p.at[0, rows : rows + extra] for p in refs])
            targets = (
                ((bias_qv, 0), (bias_qv, 1), (bias_out, 0)),
                ((gain_one, 0), (shift_one, 0), (bias_down, 0)),
                ((gain_two, 0), (shift_two, 0), (bias_up, 0)),
                ((bias_up, 1), (bias_up, 2), (bias_up, 3)),
            )[b]
            for j, (ref, part) in enumerate(targets):
                ref[:, part * share : (part + 1) * share] = value[j : j + 1, 0:share]

    vectors = [shape(1, n * share, dtype=f32) for n in (2, 1, 1, 1, 4, 1, 1, 1)]
    return call(
        kernel, "place_own", [place], pieces,
        [shape(rows, 3 * width, dtype=f32), shape(rows, width, dtype=f32), *vectors],
    )[:10]


def place_rows(place, blocks, after):
    slots, width = blocks[0].shape

    def kernel(place_ref, *refs):
        for i in range(4):
            refs[4][place_ref[1] ^ i] = refs[i][...]

    return call(kernel, "place_rows", [place], blocks, [shape(4, slots, width)], after=after)


def shards(
    tokens, lengths, w_qkv, bias_qv, w_out, bias_out, norm1_gain, norm1_bias, w_up, bias_up,
    w_down, bias_down, norm2_gain, norm2_bias, cotangent,
):
    rows, slots, width = tokens.shape
    shares = lax.axis_size("dp")
    dp_bits = shares.bit_length() - 1
    position = lax.axis_index("blk").astype(jnp.int32)
    group = lax.axis_index("dp").astype(jnp.int32)
    place = jnp.stack([position % 2, position])
    names = [("blk", 2)] + [("dp", 1 << i) for i in reversed(range(dp_bits))]
    bits = jnp.stack([position // 2] + [(group >> i) % 2 for i in reversed(range(dp_bits))])

    def gather_row(array):
        return [pick(array, position)] + [
            swap(pick(array, position ^ i), "blk", i) for i in (2, 3, 1)
        ]

    def in_order(blocks):
        return [blocks[0], blocks[3], blocks[1], blocks[2]]

    def scatter_row(blocks, after=()):
        moved = [blocks[0]] + [swap(blocks[i], "blk", i) for i in range(1, rows)]
        return place_rows(place, moved, after)

    vectors = jnp.concatenate(
        [bias_qv, bias_out, norm1_gain, norm1_bias, bias_down, norm2_gain, norm2_bias, bias_up]
    ).reshape(-1, width)
    row = jnp.concatenate([pick(lengths, position), position[None]])
    blocks = gather_row(tokens)
    blocks, cotangent = lax.optimization_barrier((blocks, cotangent))
    blocks = in_order(blocks)
    cotangents = in_order(gather_row(cotangent))
    qkv_near, out_near, mask = prepare(row, w_qkv, w_out, slots, rows * slots)
    normed, inverse, q, k, v, prob, context, row_tokens = attend(
        blocks, vectors, qkv_near, out_near, mask
    )
    keep_active, send_active, slope, lowered, first, o0, o1, o2, o3, vector_two, sum_two, normed = feed(
        place, normed, vectors, cotangents, w_up, w_down, shares
    )
    got_active, got_lowered = swap(send_active, "blk", 1), swap(lowered, "blk", 1)
    keep_up, send_up, grad_bias_up, attended, vector_one, sum_one, mark = grad_up(
        place, lowered, slope, first, w_down, inverse, vectors, w_up, sum_two, normed
    )
    got_up = swap(send_up, "blk", 1)
    outputs, mark = scatter_row([o0, o1, o2, o3], [mark])
    down, mark = grad_down(keep_active, got_active, lowered, got_lowered, [mark])

    def chunks(array):
        return array.reshape((2,) * (1 + dp_bits) + (-1, array.shape[-1]))

    down, keep_up, got_up = chunks(down), chunks(keep_up), chunks(got_up)
    feed_group = Group(
        [[([down], s) for s in range(3)], [([keep_up, got_up], s) for s in range(3)]],
        (), bits, names,
    )
    mark = feed_group.begin([mark])
    keeps, sends, small_keep, small_send, grads, mark = attend_back(
        place, attended, [vector_one, vector_two, grad_bias_up],
        [row_tokens, context, prob, q, k, v, w_out], shares, [mark],
    )
    gots = [swap(send, "blk", 1) for send in sends]
    small_got = swap(small_send, "blk", 1)
    mark = feed_group.rest([mark])
    mark = feed_group.step([mark])
    own_group = Group(
        [[([chunks(keep), chunks(got)], 0) for keep, got in zip(keeps, gots)]],
        (chunks(small_keep), chunks(small_got)), bits, names,
    )
    mark = own_group.begin([mark])
    tokens_parts, mark = grad_tokens(sum_one, grads, w_qkv, slots, [mark])
    mark = own_group.rest([mark])
    for _ in range(dp_bits - 1):
        mark = feed_group.step([mark])
        mark = own_group.step([mark])
    mark = own_group.step([mark])
    feed_pieces, mark = feed_group.finish([mark])
    token_grads, mark = scatter_row(tokens_parts, [mark])
    own_pieces, mark = own_group.finish([mark])

    share = width // shares
    down, up = place_feed(place, feed_pieces, share, shares)
    (
        grad_w_qkv, grad_w_out, sum_qv, sum_out, sum_gain_one, sum_shift_one, sum_up, sum_down,
        sum_gain_two, sum_shift_two,
    ) = place_own(place, own_pieces, share, shares)
    return (
        outputs,
        token_grads,
        grad_w_qkv,
        sum_qv[0],
        grad_w_out,
        sum_out[0],
        sum_gain_one[0],
        sum_shift_one[0],
        up,
        sum_up[0],
        down,
        sum_down[0],
        sum_gain_two[0],
        sum_shift_two[0],
    )


def solution(mesh):
    row_spec = P("dp", "blk", None)
    in_specs = (row_spec, P("dp", None)) + (P(),) * 12 + (row_spec,)
    wide, flat = P("dp", None), P("dp")
    out_specs = (
        row_spec, row_spec, wide, flat, wide, flat, flat, flat, wide, flat, wide, flat, flat, flat,
    )
    return jax.shard_map(shards, mesh=mesh, in_specs=in_specs, out_specs=out_specs, check_vma=False)
```

```python
import functools
import math

import jax
import jax.numpy as jnp
from jax import lax
from jax.experimental import pallas as pl
from jax.experimental.pallas import tpu as pltpu
from jax.sharding import PartitionSpec as P

HEADS = 12
EPSILON = 1e-12
MASKED = -1e30
f32 = jnp.float32
bf16 = jnp.bfloat16
NN = (((1,), (0,)), ((), ()))
NT = (((1,), (1,)), ((), ()))
TN = (((0,), (0,)), ((), ()))
VMEM = pl.BlockSpec(memory_space=pltpu.VMEM)
SMEM = pl.BlockSpec(memory_space=pltpu.SMEM)
HBM = pl.BlockSpec(memory_space=pltpu.HBM)
ANY = pl.BlockSpec(memory_space=pl.ANY)


WEIGHTS = {
    "prepare": 60 * 10**9, "attend": 60 * 10**9, "feed": 60 * 10**9, "grad_up": 60 * 10**9,
    "grad_down": 60 * 10**9, "attend_back": 60 * 10**9, "grad_tokens": 60 * 10**9,
    "halve": 5 * 10**9, "cut_units": 5 * 10**9, "place_feed": 5 * 10**9,
}


def dot(left, right, dims=NN):
    return lax.dot_general(left, right, dims, preferred_element_type=f32)


def call(
    kernel, name, scalars, arrays, outs, scratch=(), far=(), far_outs=(), copies=0, room=10, after=()
):
    scratch = list(scratch)
    if copies:
        scratch.append(pltpu.SemaphoreType.DMA((copies,)))
    first, last = len(scalars) + len(arrays) + len(far), len(after)
    results = len(outs) + len(far_outs)
    mark = jax.ShapeDtypeStruct((8, 128), f32)

    def body(*refs):
        mine = refs[first + last :]
        mine[results][...] = jnp.zeros(mark.shape, mark.dtype)
        kernel(*refs[:first], *mine[:results], *mine[results + 1 :])

    return pl.pallas_call(
        body,
        in_specs=[SMEM] * len(scalars) + [VMEM] * len(arrays) + [HBM] * len(far) + [VMEM] * last,
        out_specs=[VMEM] * len(outs) + [HBM] * len(far_outs) + [VMEM],
        out_shape=[*outs, *[pltpu.HBM(a.shape, a.dtype) for a in far_outs], mark],
        scratch_shapes=scratch,
        compiler_params=pltpu.CompilerParams(vmem_limit_bytes=room * 2**20),
        cost_estimate=pl.CostEstimate(
            flops=WEIGHTS.get(name, 0), bytes_accessed=0, transcendentals=0
        ),
        name=name,
    )(
        *scalars, *arrays, *[pltpu.with_memory_space_constraint(a, pltpu.HBM) for a in far], *after
    )


def shape(*dims, dtype=bf16):
    return jax.ShapeDtypeStruct(dims, dtype)


def cut(i, size):
    return pl.ds(pl.multiple_of(i * size, size), size)


def copy(source, target, semaphore):
    return pltpu.make_async_copy(source, target, semaphore)


def column_sum(values):
    return jnp.sum(values, axis=0, keepdims=True)


def row_mean(values):
    return jnp.mean(values, axis=-1, keepdims=True)


def normalize(inputs):
    centre = inputs - row_mean(inputs)
    inverse = lax.rsqrt(row_mean(centre * centre) + EPSILON)
    return centre * inverse, inverse


def normalize_back(scaled, normed, inverse):
    return inverse * (scaled - row_mean(scaled) - normed * row_mean(scaled * normed))


BIAS_Q, BIAS_V, BIAS_OUT, GAIN_ONE, SHIFT_ONE, BIAS_DOWN, GAIN_TWO, SHIFT_TWO, BIAS_UP = range(9)


def vector(ref, row):
    return ref[row : row + 1, :]


def only(rows, h, height):
    parts = [jnp.zeros((height, rows.shape[1]), rows.dtype)] * (rows.shape[0] // height)
    parts[h] = rows[h * height : (h + 1) * height, :]
    return jnp.concatenate(parts)


def prepare_kernel(
    row_ref, b0, b1, b2, b3, b4, b5, b6, b7, w_qkv, w_out, qkv_near, out_near, mask, vectors, sems,
    *, pages, slots,
):
    load_qkv = copy(w_qkv, qkv_near, sems.at[0])
    load_qkv.start()
    load_out = copy(w_out, out_near, sems.at[1])
    load_out.start()
    width = vectors.shape[1]
    row = 0
    for part in (b0, b1, b2, b3, b4, b5, b6, b7):
        for i in range(part.shape[0] // width):
            vectors[row : row + 1, :] = part[i * width : (i + 1) * width].reshape(1, width)
            row += 1
    count = mask.shape[0]
    position = row_ref[pages]

    def page_of(shape, dim):
        at = lax.broadcasted_iota(jnp.int32, shape, dim)
        slot = ((at // slots) ^ position) * slots + at % slots
        page = jnp.zeros(shape, jnp.int32)
        end = 0
        for c in range(pages):
            end = end + row_ref[c]
            page = page + (slot >= end).astype(jnp.int32)
        return page

    mask[...] = jnp.where(
        page_of((count, count), 0) == page_of((1, count), 1), 0.0, MASKED
    )
    load_qkv.wait()
    load_out.wait()


def prepare(row, biases, w_qkv, w_out, slots, count):
    width = w_out.shape[0]
    rows = sum(b.shape[0] for b in biases) // width
    return call(
        functools.partial(prepare_kernel, pages=row.shape[0] - 1, slots=slots),
        "prepare", [row], biases,
        [
            shape(*w_qkv.shape), shape(*w_out.shape), shape(count, count, dtype=f32),
            shape(rows, width, dtype=f32),
        ],
        far=[w_qkv, w_out], copies=2,
    )[:4]


def attend_kernel(
    x0, x1, x2, x3, vectors, w_qkv, w_out, mask,
    normed_out, inverse_out, q_out, k_out, v_out, prob_out, context_out, tokens_out,
    tokens, q_kept, k_kept, v_kept, context_kept, probs_kept, sems, *, head_width,
):
    slots = x0.shape[0]
    count, width = tokens.shape
    wide = 4 * head_width
    groups = width // wide
    kept = ((0, q_kept, q_out), (1, k_kept, k_out), (2, v_kept, v_out), (3, context_kept, context_out))

    def keep(i, number, source, target):
        here = cut(i, wide)
        return copy(source.at[:, here], target.at[:, here], sems.at[number * groups + i])

    def keep_probs(i, h):
        return copy(
            probs_kept.at[4 * i + h], prob_out.at[4 * i + h], sems.at[4 * groups + 1 + 4 * i + h]
        )

    for i, block in enumerate((x0, x1, x2, x3)):
        tokens[i * slots : (i + 1) * slots, :] = block[...]
    keep_tokens = copy(tokens, tokens_out, sems.at[4 * groups])
    keep_tokens.start()

    @pl.loop(0, groups)
    def _(i):
        here = cut(i, wide)
        x = tokens[...]
        q = (dot(x, w_qkv[:, here]) + vectors[BIAS_Q : BIAS_Q + 1, here]).astype(bf16)
        k = dot(x, w_qkv[:, cut(i + groups, wide)]).astype(bf16)
        v = dot(x, w_qkv[:, cut(i + 2 * groups, wide)]) + vectors[BIAS_V : BIAS_V + 1, here]
        v = v.astype(bf16)
        q_kept[:, here] = q
        k_kept[:, here] = k
        v_kept[:, here] = v
        q_turned = (q * jnp.asarray(1.0 / math.sqrt(head_width), bf16)).T
        v_turned = v.T
        context = []
        for h in range(4):
            scores = dot(k, only(q_turned, h, head_width)) + mask[...]
            powers = jnp.exp(scores - jnp.max(scores, axis=0, keepdims=True))
            probs = (powers * (1.0 / jnp.sum(powers, axis=0, keepdims=True))).astype(bf16)
            probs_kept[4 * i + h] = probs
            keep_probs(i, h).start()
            context.append(dot(v_turned[h * head_width : (h + 1) * head_width, :], probs))
        context_kept[:, here] = jnp.concatenate(context).astype(bf16).T
        for number, source, target in kept:
            keep(i, number, source, target).start()

    attended = dot(context_kept[...], w_out[...]) + vector(vectors, BIAS_OUT)
    normed, inverse = normalize(tokens[...].astype(f32) + attended)
    normed_out[...] = normed
    inverse_out[...] = inverse
    for i in range(groups):
        for number, source, target in kept:
            keep(i, number, source, target).wait()
        for h in range(4):
            keep_probs(i, h).wait()
    keep_tokens.wait()


def attend(blocks, vectors, w_qkv, w_out, mask):
    slots, width = blocks[0].shape
    count = slots * len(blocks)
    groups = HEADS // 4
    narrow = shape(count, width)
    rows = pltpu.VMEM((count, width), bf16)
    return call(
        functools.partial(attend_kernel, head_width=width // HEADS),
        "attend", [], [*blocks, vectors, w_qkv, w_out, mask],
        [shape(count, width, dtype=f32), shape(count, 1, dtype=f32)],
        [rows, rows, rows, rows, rows, pltpu.VMEM((HEADS, count, count), bf16)],
        far_outs=[narrow, narrow, narrow, shape(HEADS, count, count), narrow, narrow],
        copies=4 * groups + 1 + HEADS, room=24,
    )[:8]


def feed_kernel(
    place, normed_one, vectors, c0, c1, c2, c3, w_up, w_down,
    keep_active, send_active, slope_out, lowered_out, first_out, r0, r1, r2, r3, vector_out,
    sum_out, total, *, shares,
):
    width = w_up.shape[0]
    hidden = w_up.shape[1]
    first_norm = normed_one[...] * vector(vectors, GAIN_ONE) + vector(vectors, SHIFT_ONE)
    first_out[...] = first_norm.astype(bf16)
    total[...] = first_norm + vector(vectors, BIAS_DOWN)
    odd = place[0] == 1
    rows = hidden // shares // 4
    apart = send_active is not None

    @pl.loop(0, hidden // width)
    def _(i):
        here = cut(i, width)
        raised = dot(first_out[...], w_up[:, here]) + vectors[pl.ds(BIAS_UP + i, 1), :]
        cumulative = 0.5 * (1.0 + lax.erf(raised * (1.0 / math.sqrt(2.0))))
        activated = (raised * cumulative).astype(bf16)
        bell = jnp.exp(-0.5 * raised * raised) * (1.0 / math.sqrt(2.0 * math.pi))
        slope_out[:, here] = (cumulative + raised * bell).astype(bf16)
        total[...] += dot(activated, w_down[here, :])
        turned = activated.T
        if apart:
            count = width // rows // 4
            for d in range(count):
                for x in range(2):
                    at = (d * 4 + x * 2) * rows
                    even_part = turned[at : at + rows, :]
                    odd_part = turned[at + rows : at + 2 * rows, :]
                    keep_active[x, i * count + d] = jnp.where(odd, odd_part, even_part)
                    send_active[x, i * count + d] = jnp.where(odd, even_part, odd_part)
        else:
            keep_active[here, :] = turned

    normed, inverse = normalize(total[...])
    gain = vector(vectors, GAIN_TWO)
    result = (normed * gain + vector(vectors, SHIFT_TWO)).astype(bf16)
    slots = c0.shape[0]
    for i, block in enumerate((r0, r1, r2, r3)):
        block[...] = result[i * slots : (i + 1) * slots, :]
    upstream = jnp.concatenate([c0[...], c1[...], c2[...], c3[...]]).astype(f32)
    grad_sum = normalize_back(upstream * gain, normed, inverse)
    sum_out[...] = grad_sum
    lowered = grad_sum.astype(bf16)
    lowered_out[...] = lowered
    vector_out[0:1, :] = column_sum(upstream * normed)
    vector_out[1:2, :] = column_sum(upstream)
    vector_out[2:3, :] = column_sum(lowered.astype(f32))


def feed(place, normed, vectors, cotangents, w_up, w_down, shares):
    count, width = normed.shape
    hidden = w_up.shape[1]
    rows = hidden // shares // 4
    narrow, full = shape(count, width), shape(count, width, dtype=f32)
    apart = rows % 16 == 0 and width % (4 * rows) == 0
    kernel = functools.partial(feed_kernel, shares=shares)
    if apart:
        active = [shape(2, shares, rows, count)] * 2
    else:
        active = [shape(hidden, count)]
        whole = kernel

        def kernel(*refs):
            whole(*refs[:10], None, *refs[10:])

    made = call(
        kernel, "feed", [place], [normed, vectors, *cotangents, w_up, w_down],
        active + [shape(count, hidden), narrow, narrow]
        + [shape(*cotangents[0].shape)] * 4 + [shape(8, width, dtype=f32), full],
        [pltpu.VMEM((count, width), f32)], room=14,
    )[:-1]
    if apart:
        return made
    parts = jnp.moveaxis(made[0].reshape(shares, 2, 2, rows, count), 0, 2)
    odd = place[0] == 1
    keep = jnp.where(odd, parts[:, 1], parts[:, 0])
    send = jnp.where(odd, parts[:, 0], parts[:, 1])
    return [keep, send, *made[1:]]


def grad_up_kernel(
    place, lowered, slope, first, w_down, inverse_one, vectors, sum_two, normed, w_up,
    keep, send, bias_out, attended_out, vector_out, sum_out, turned, raised_kept, weights, sems,
):
    width = lowered.shape[1]
    load = copy(w_up, weights, sems.at[0])
    load.start()
    turned[...] = first[...].T

    def work(b):
        here = cut(b, width)
        raised = dot(lowered[...], w_down[here, :], NT) * slope[:, here].astype(f32)
        raised = raised.astype(bf16)
        raised_kept[:, here] = raised
        bias_out[pl.ds(b, 1), :] = column_sum(raised.astype(f32))
        return dot(turned[...], raised).astype(bf16)

    @pl.loop(0, 2)
    def _(x):
        send[x] = work(2 * x + 1 - place[0])
        keep[x] = work(2 * x + place[0])

    load.wait()
    upstream = sum_two[...] + dot(raised_kept[...], weights[...], NT)
    grad_sum = normalize_back(
        upstream * vector(vectors, GAIN_ONE), normed[...], inverse_one[...]
    )
    sum_out[...] = grad_sum
    attended = grad_sum.astype(bf16)
    attended_out[...] = attended
    vector_out[0:1, :] = column_sum(upstream * normed[...])
    vector_out[1:2, :] = column_sum(upstream)
    vector_out[2:3, :] = column_sum(attended.astype(f32))


def grad_up(place, lowered, slope, first, w_down, inverse, vectors, w_up, sum_two, normed):
    count, width = lowered.shape
    hidden = w_down.shape[0]
    return call(
        grad_up_kernel, "grad_up", [place],
        [lowered, slope, first, w_down, inverse, vectors, sum_two, normed],
        [shape(2, width, width)] * 2
        + [shape(hidden // width, width, dtype=f32), shape(count, width)]
        + [shape(8, width, dtype=f32), shape(count, width, dtype=f32)],
        [
            pltpu.VMEM((width, count), bf16), pltpu.VMEM((count, hidden), bf16),
            pltpu.VMEM((width, hidden), bf16),
        ],
        far=[w_up], copies=1, room=28,
    )


def place_rows(place, blocks, rows, sems):
    copies = [copy(block, rows.at[place[1] ^ i], sems.at[i]) for i, block in enumerate(blocks)]
    for one in copies:
        one.start()
    return copies


def grad_down_kernel(
    place, active, other_active, lowered, other_lowered, r0, r1, r2, r3, down, rows_out, sems
):
    copies = place_rows(place, (r0, r1, r2, r3), rows_out, sems)
    _, shares, rows, count = active.shape
    width = lowered.shape[1]

    for x in range(2):

        @pl.loop(0, shares, step=2)
        def _(d):
            mine = active[x, pl.ds(d, 2)].reshape(2 * rows, count)
            other = other_active[x, pl.ds(d, 2)].reshape(2 * rows, count)
            value = dot(mine, lowered[...]) + dot(other, other_lowered[...])
            down[x, pl.ds(d, 2)] = value.astype(bf16).reshape(2, rows, width)

    for one in copies:
        one.wait()


def grad_down(place, active, other_active, lowered, other_lowered, blocks, after):
    _, shares, rows, _ = active.shape
    slots, width = blocks[0].shape
    return call(
        grad_down_kernel, "grad_down", [place],
        [active, other_active, lowered, other_lowered, *blocks],
        [shape(2, shares, rows, width)], far_outs=[shape(4, slots, width)], copies=4, after=after,
    )


def small_pieces(shares, width):
    q, v, gain_one, shift_one, out, gain_two, shift_two, down, up = range(9)
    share = width // shares

    def flat(row, first):
        return row + first // width, first % width

    def pieces(d):
        at = d * share
        return (
            (flat(q, 2 * at), flat(q, 2 * at + share), (out, at)),
            ((gain_one, at), (shift_one, at), (down, at)),
            ((gain_two, at), (shift_two, at), flat(up, 4 * at)),
            tuple(flat(up, 4 * at + j * share) for j in (1, 2, 3)),
        )

    return [pieces(d) for d in range(shares)]


def attend_back_kernel(
    place, attended, vector_one, vector_two, bias_up, tokens, context, prob, q_ref, k_ref, v_ref, w_out,
    grads_out, keep_0, keep_1, keep_2, send_0, send_1, send_2, small_keep, small_send,
    rows_kept, turned, turned_context, probs_kept, q_kept, k_kept, v_kept, weights, sums, small, sems,
    *, head_width,
):
    count, width = attended.shape
    wide = 4 * head_width
    groups = width // wide
    shares = small_keep.shape[1]

    def load(i):
        here = cut(i, wide)
        pairs = [
            (w_out.at[here, :], weights.at[here, :]),
            (v_ref.at[:, here], v_kept.at[:, here]),
            (q_ref.at[:, here], q_kept.at[:, here]),
            (k_ref.at[:, here], k_kept.at[:, here]),
        ]
        pairs = pairs + [(prob.at[4 * i + h], probs_kept.at[4 * i + h]) for h in range(4)]
        return [copy(s, t, sems.at[8 * i + n]) for n, (s, t) in enumerate(pairs)]

    load_tokens = copy(tokens, rows_kept.at[0], sems.at[8 * groups])
    load_context = copy(context, rows_kept.at[1], sems.at[8 * groups + 1])
    for one in load(0):
        one.start()
    load_tokens.start()
    load_context.start()
    head = lax.broadcasted_iota(jnp.int32, (count, wide), 1) // head_width
    none = jnp.zeros((count, wide), bf16)
    odd = place[0] == 1

    @pl.loop(0, groups)
    def _(i):
        here = cut(i, wide)

        @pl.when(i + 1 < groups)
        def _():
            for one in load(i + 1):
                one.start()

        waits = load(i)
        waits[0].wait()
        grad_context = dot(attended[...], weights[here, :], NT).astype(bf16)
        context_turned = grad_context.T
        scaling = jnp.asarray(1.0 / math.sqrt(head_width), bf16)
        for one in waits[1:4]:
            one.wait()
        scaled_q = q_kept[:, here] * scaling
        k_turned = (k_kept[:, here] * scaling).T
        v = v_kept[:, here]

        @pl.when(i == 0)
        def _():
            load_tokens.wait()
            turned[...] = rows_kept[0].T
            load_context.wait()
            turned_context[...] = rows_kept[1].T

        for one in waits[4:]:
            one.wait()
        grad_k = jnp.zeros((count, wide), f32)
        grad_v = grad_k
        grad_q = []
        for h in range(4):
            mine = head == h
            probs = probs_kept[4 * i + h]
            wider = probs.astype(f32)
            weighted = wider * dot(v, only(context_turned, h, head_width))
            balance = jnp.sum(weighted, axis=0, keepdims=True)
            grad_scores = (weighted - wider * balance).astype(bf16)
            grad_v = grad_v + dot(probs, jnp.where(mine, grad_context, none))
            grad_k = grad_k + dot(grad_scores, jnp.where(mine, scaled_q, none))
            grad_q.append(dot(k_turned[h * head_width : (h + 1) * head_width, :], grad_scores))
        grad_q = jnp.concatenate(grad_q).astype(bf16).T
        grad_k = grad_k.astype(bf16)
        grad_v = grad_v.astype(bf16)
        grads_out[:, here] = grad_q
        grads_out[:, cut(i + groups, wide)] = grad_k
        grads_out[:, cut(i + 2 * groups, wide)] = grad_v
        sums[0:1, here] = column_sum(grad_q.astype(f32))
        sums[1:2, here] = column_sum(grad_v.astype(f32))
        pieces = (
            dot(turned[...], grad_q).astype(bf16),
            dot(turned[...], grad_k).astype(bf16),
            dot(turned[...], grad_v).astype(bf16),
            dot(turned_context[...], attended[:, here]).astype(bf16),
        )
        for s, (keep, send) in enumerate(((keep_0, send_0), (keep_1, send_1), (keep_2, send_2))):

            @pl.when(i == s)
            def _(keep=keep, send=send):
                for x in range(2):
                    keep[x] = jnp.where(odd, pieces[2 * x + 1], pieces[2 * x])
                    send[x] = jnp.where(odd, pieces[2 * x], pieces[2 * x + 1])

    sums[2:5, :] = vector_one[0:3, :]
    sums[5:8, :] = vector_two[0:3, :]
    sums[8:12, :] = bias_up[...]
    share = width // shares
    small[...] = jnp.zeros_like(small)
    for d, by_blk in enumerate(small_pieces(shares, width)):
        for b, three in enumerate(by_blk):
            for j, (row, column) in enumerate(three):
                small[b, d, j : j + 1, 0:share] = sums[row : row + 1, column : column + share]
    for x in range(2):
        even_part = small[2 * x].astype(bf16)
        odd_part = small[2 * x + 1].astype(bf16)
        small_keep[x] = jnp.where(odd, odd_part, even_part)
        small_send[x] = jnp.where(odd, even_part, odd_part)


def attend_back(place, attended, small, far, shares, after):
    count, width = attended.shape
    wide = 4 * (width // HEADS)
    groups = width // wide
    rows, turned = pltpu.VMEM((count, width), bf16), pltpu.VMEM((width, count), bf16)
    grads, keep_0, keep_1, keep_2, send_0, send_1, send_2, small_keep, small_send, mark = call(
        functools.partial(attend_back_kernel, head_width=width // HEADS),
        "attend_back", [place], [attended, *small],
        [shape(count, 3 * width)] + [shape(2, width, wide)] * 6 + [shape(2, shares, 16, wide)] * 2,
        [
            pltpu.VMEM((2, count, width), bf16), turned, turned,
            pltpu.VMEM((HEADS, count, count), bf16), rows, rows, rows,
            pltpu.VMEM((width, width), bf16),
            pltpu.VMEM((16, width), f32), pltpu.VMEM((4, shares, 16, wide), f32),
        ],
        far=far, copies=8 * groups + 2, room=26, after=after,
    )
    return [keep_0, keep_1, keep_2], [send_0, send_1, send_2], small_keep, small_send, grads, mark


def grad_tokens_kernel(grads, w_qkv, sum_one, r0, r1, r2, r3):
    result = (sum_one[...] + dot(grads[...], w_qkv[...], NT)).astype(bf16)
    slots = r0.shape[0]
    for i, block in enumerate((r0, r1, r2, r3)):
        block[...] = result[i * slots : (i + 1) * slots, :]


def grad_tokens(sum_one, grads, w_qkv, slots, after):
    count, width = sum_one.shape
    *blocks, mark = call(
        grad_tokens_kernel, "grad_tokens", [], [grads, w_qkv, sum_one], [shape(slots, width)] * 4,
        room=12, after=after,
    )
    return blocks, mark


def swap(block, axis, bit):
    return lax.ppermute(block, axis, [(i, i ^ bit) for i in range(lax.axis_size(axis))])


def pick(block, index, dim=0):
    return lax.dynamic_index_in_dim(block, index, dim, keepdims=False)


def every(count, work):
    if count <= 8:
        for number in range(count):
            work(number)
    else:
        pl.loop(0, count)(work)


def cut_units(bits, units, extra, orders, flip, after):
    parts, dims = len(orders), len(orders[0])
    arrays, numbers = [], {}
    for array in [a for unit in units for terms, _ in unit for a in terms] + list(extra):
        if id(array) not in numbers:
            numbers[id(array)] = len(arrays)
            arrays.append(array)
    rows = arrays[0].shape[-2]
    size = sum({id(terms[0]): terms[0].shape[-1] for terms, _ in units[0]}.values()) // parts
    more = [extra[0].shape[-2] if extra and s == 0 else 0 for s in range(parts)]
    outs = [shape(2 ** (dims - 1), len(units) * rows + m, size) for m in more]

    def kernel(bits_ref, *refs):
        ins, results = refs[: len(arrays)], refs[len(arrays) :]

        def added(terms, at):
            total = ins[numbers[id(terms[0])]][at]
            for term in terms[1:]:
                total = total + ins[numbers[id(term)]][at]
            return total

        def work(number):
            for s, order in enumerate(orders):
                index = [None] * dims
                index[order[0]] = bits_ref[order[0]] ^ flip
                for i, n in enumerate(order[1:]):
                    index[n] = (number >> (dims - 2 - i)) & 1
                for u, unit in enumerate(units):
                    terms, column = unit[s]
                    at = (*index, slice(None), slice(column * size, (column + 1) * size))
                    results[s][number, u * rows : (u + 1) * rows] = added(terms, at)
                if more[s]:
                    results[s][number, len(units) * rows :] = added(extra, tuple(index))

        every(2 ** (dims - 1), work)

    *made, mark = call(kernel, "cut_units", [bits], arrays, outs, after=after)
    return made, mark


def halve(bits, pairs, axes, join, after=()):
    taken = pairs[0][0].shape[0] // (2 if axes else 1)
    sizes = [a.shape[1] for a, _ in pairs]
    width = pairs[0][0].shape[2]
    flips = (1, 0) if axes else (0,)
    outs = [shape(taken, sum(sizes), width)] if join else [shape(taken, n, width) for n in sizes]
    arrays = [a for pair in pairs for a in pair]

    def kernel(bits_ref, *refs):
        ins, results = refs[: len(arrays)], refs[len(arrays) :]

        def work(number):
            for f, flip in enumerate(flips):
                for s in range(len(pairs)):
                    at = number + ((bits_ref[axes[s]] ^ flip) * taken if axes else 0)
                    total = ins[2 * s][at] + ins[2 * s + 1][at]
                    if join:
                        first = sum(sizes[:s])
                        results[f][number, first : first + sizes[s]] = total
                    else:
                        results[f * len(pairs) + s][number] = total

        every(taken, work)

    *made, mark = call(kernel, "halve", [bits], arrays, outs * len(flips), room=6, after=after)
    return made[: len(outs)], made[len(outs) :], mark


class Group:
    def __init__(self, units, extra, bits, names):
        self.units, self.extra, self.bits, self.names = units, extra, bits, names
        size = len(names)
        turn = [0, size - 1, size - 2]
        rest = list(range(size - 3, 0, -1))
        self.orders = [turn[s:] + turn[:s] + rest for s in range(3)]
        self.stage = 0
        self.pairs = None

    def send(self, blocks):
        return [
            swap(block, *self.names[order[self.stage]]) for block, order in zip(blocks, self.orders)
        ]

    def begin(self, after):
        sent, mark = cut_units(self.bits, self.units, self.extra, self.orders, 1, after)
        self.arrived = self.send(sent)
        return mark

    def rest(self, after):
        keep, mark = cut_units(self.bits, self.units, self.extra, self.orders, 0, after)
        self.pairs = list(zip(keep, self.arrived))
        self.stage = 1
        return mark

    def step(self, after):
        axes = [order[self.stage] for order in self.orders]
        sent, keep, mark = halve(self.bits, self.pairs, axes, self.stage == 3, after)
        self.pairs = list(zip(keep, self.send(sent)))
        self.stage += 1
        return mark

    def finish(self, after):
        (own,), _, mark = halve(self.bits, self.pairs, None, False, after)
        across = swap(own, "blk", 2)
        return (own, swap(own, "blk", 1), across, swap(across, "blk", 1)), mark


def chosen(place, b, refs):
    relative = place[1] ^ b
    values = [ref[...] for ref in refs]
    return jnp.where(
        relative < 2,
        jnp.where(relative == 0, values[0], values[1]),
        jnp.where(relative == 2, values[2], values[3]),
    ).astype(f32)


def place_feed(place, pieces, rows, blocks, after):
    size = pieces[0].shape[2]
    width = 3 * size

    def kernel(place_ref, p0, p1, p2, p3, r0, r1, r2, r3, down, up, rows_out, sems):
        copies = place_rows(place_ref, (r0, r1, r2, r3), rows_out, sems)
        for b in range(4):
            for s in range(3):
                at = 2 * s * rows
                columns = slice(s * size, (s + 1) * size)
                value = chosen(place_ref, b, [p.at[0, at : at + rows] for p in (p0, p1, p2, p3)])
                down[b * rows : (b + 1) * rows, columns] = value
                at = at + rows
                columns = slice(b * width + s * size, b * width + (s + 1) * size)
                value = chosen(place_ref, b, [p.at[0, at : at + rows] for p in (p0, p1, p2, p3)])
                up[:, columns] = value
        for one in copies:
            one.wait()

    return call(
        kernel, "place_feed", [place], [*pieces, *blocks],
        [shape(4 * rows, width, dtype=f32), shape(rows, 4 * width, dtype=f32)],
        far_outs=[shape(4, *blocks[0].shape)], copies=4, after=after,
    )


def place_own(place, pieces, rows, shares, after):
    size = pieces[0].shape[2]
    width = 3 * size
    share = width // shares
    extra = pieces[0].shape[1] - 3 * rows

    def kernel(place_ref, p0, p1, p2, p3, qkv, out, *small):
        refs = (p0, p1, p2, p3)
        bias_qv, bias_out, gain_one, shift_one, bias_up, bias_down, gain_two, shift_two = small
        for b in range(4):
            for s in range(3):
                at = s * rows + (extra if s else 0)
                value = chosen(place_ref, b, [p.at[0, at : at + rows] for p in refs])
                columns = slice(s * size, (s + 1) * size)
                if b == 3:
                    out[:, columns] = value
                else:
                    qkv[:, b * width + s * size : b * width + (s + 1) * size] = value
            value = chosen(place_ref, b, [p.at[0, rows : rows + extra] for p in refs])
            targets = (
                ((bias_qv, 0), (bias_qv, 1), (bias_out, 0)),
                ((gain_one, 0), (shift_one, 0), (bias_down, 0)),
                ((gain_two, 0), (shift_two, 0), (bias_up, 0)),
                ((bias_up, 1), (bias_up, 2), (bias_up, 3)),
            )[b]
            for j, (ref, part) in enumerate(targets):
                ref[:, part * share : (part + 1) * share] = value[j : j + 1, 0:share]

    vectors = [shape(1, n * share, dtype=f32) for n in (2, 1, 1, 1, 4, 1, 1, 1)]
    return call(
        kernel, "place_own", [place], pieces,
        [shape(rows, 3 * width, dtype=f32), shape(rows, width, dtype=f32), *vectors],
        after=after,
    )[:10]


def shards(
    tokens, lengths, w_qkv, bias_qv, w_out, bias_out, norm1_gain, norm1_bias, w_up, bias_up,
    w_down, bias_down, norm2_gain, norm2_bias, cotangent,
):
    rows, slots, width = tokens.shape
    shares = lax.axis_size("dp")
    dp_bits = shares.bit_length() - 1
    position = lax.axis_index("blk").astype(jnp.int32)
    group = lax.axis_index("dp").astype(jnp.int32)
    place = jnp.stack([position % 2, position])
    names = [("blk", 2)] + [("dp", 1 << i) for i in reversed(range(dp_bits))]
    bits = jnp.stack([position // 2] + [(group >> i) % 2 for i in reversed(range(dp_bits))])

    def gather_row(array):
        return [pick(array, position)] + [
            swap(pick(array, position ^ i), "blk", i) for i in (2, 3, 1)
        ]

    def in_order(blocks):
        return [blocks[0], blocks[3], blocks[1], blocks[2]]

    def scatter_row(blocks):
        return [blocks[0]] + [swap(blocks[i], "blk", i) for i in range(1, rows)]

    biases = [
        bias_qv, bias_out, norm1_gain, norm1_bias, bias_down, norm2_gain, norm2_bias, bias_up
    ]
    row = jnp.concatenate([pick(lengths, position), position[None]])
    blocks = gather_row(tokens)
    blocks, cotangent = lax.optimization_barrier((blocks, cotangent))
    blocks = in_order(blocks)
    cotangents = in_order(gather_row(cotangent))
    qkv_near, out_near, mask, vectors = prepare(
        row, biases, w_qkv, w_out, slots, rows * slots
    )
    normed, inverse, q, k, v, prob, context, row_tokens = attend(
        blocks, vectors, qkv_near, out_near, mask
    )
    keep_active, send_active, slope, lowered, first, o0, o1, o2, o3, vector_two, sum_two = feed(
        place, normed, vectors, cotangents, w_up, w_down, shares
    )
    got_active, got_lowered = swap(send_active, "blk", 1), swap(lowered, "blk", 1)
    keep_up, send_up, grad_bias_up, attended, vector_one, sum_one, mark = grad_up(
        place, lowered, slope, first, w_down, inverse, vectors, w_up, sum_two, normed
    )
    got_up = swap(send_up, "blk", 1)
    down, outputs, mark = grad_down(
        place, keep_active, got_active, lowered, got_lowered, scatter_row([o0, o1, o2, o3]), [mark]
    )

    def chunks(array):
        return array.reshape((2,) * (1 + dp_bits) + (-1, array.shape[-1]))

    down, keep_up, got_up = chunks(down), chunks(keep_up), chunks(got_up)
    feed_group = Group(
        [[([down], s) for s in range(3)], [([keep_up, got_up], s) for s in range(3)]],
        (), bits, names,
    )
    mark = feed_group.begin([mark])
    keeps, sends, small_keep, small_send, grads, mark = attend_back(
        place, attended, [vector_one, vector_two, grad_bias_up],
        [row_tokens, context, prob, q, k, v, w_out], shares, [mark],
    )
    gots = [swap(send, "blk", 1) for send in sends]
    small_got = swap(small_send, "blk", 1)
    mark = feed_group.rest([mark])
    mark = feed_group.step([mark])
    own_group = Group(
        [[([chunks(keep), chunks(got)], 0) for keep, got in zip(keeps, gots)]],
        (chunks(small_keep), chunks(small_got)), bits, names,
    )
    mark = own_group.begin([mark])
    tokens_parts, mark = grad_tokens(sum_one, grads, w_qkv, slots, [mark])
    mark = own_group.rest([mark])
    for _ in range(dp_bits - 1):
        mark = feed_group.step([mark])
        mark = own_group.step([mark])
    share = width // shares
    feed_pieces, mark = feed_group.finish([mark])
    mark = own_group.step([mark])
    own_pieces, mark = own_group.finish([mark])
    down, up, token_grads, mark = place_feed(
        place, feed_pieces, share, scatter_row(tokens_parts), [mark]
    )
    (
        grad_w_qkv, grad_w_out, sum_qv, sum_out, sum_gain_one, sum_shift_one, sum_up, sum_down,
        sum_gain_two, sum_shift_two,
    ) = place_own(place, own_pieces, share, shares, [mark])
    return (
        outputs,
        token_grads,
        grad_w_qkv,
        sum_qv[0],
        grad_w_out,
        sum_out[0],
        sum_gain_one[0],
        sum_shift_one[0],
        up,
        sum_up[0],
        down,
        sum_down[0],
        sum_gain_two[0],
        sum_shift_two[0],
    )


def solution(mesh):
    row_spec = P("dp", "blk", None)
    in_specs = (row_spec, P("dp", None)) + (P(),) * 12 + (row_spec,)
    wide, flat = P("dp", None), P("dp")
    out_specs = (
        row_spec, row_spec, wide, flat, wide, flat, flat, flat, wide, flat, wide, flat, flat, flat,
    )
    return jax.shard_map(shards, mesh=mesh, in_specs=in_specs, out_specs=out_specs, check_vma=False)
```

```python
import functools
import math

import jax
import jax.numpy as jnp
from jax import lax
from jax.experimental import pallas as pl
from jax.experimental.pallas import tpu as pltpu
from jax.sharding import PartitionSpec as P

HEADS = 12
EPSILON = 1e-12
MASKED = -1e30
f32 = jnp.float32
bf16 = jnp.bfloat16
NN = (((1,), (0,)), ((), ()))
NT = (((1,), (1,)), ((), ()))
TN = (((0,), (0,)), ((), ()))
VMEM = pl.BlockSpec(memory_space=pltpu.VMEM)
SMEM = pl.BlockSpec(memory_space=pltpu.SMEM)
HBM = pl.BlockSpec(memory_space=pltpu.HBM)
ANY = pl.BlockSpec(memory_space=pl.ANY)


WEIGHTS = {
    "prepare": 60 * 10**9, "attend": 60 * 10**9, "feed": 60 * 10**9, "grad_up": 60 * 10**9,
    "grad_down": 60 * 10**9, "attend_back": 60 * 10**9, "grad_tokens": 60 * 10**8,
    "halve": 200 * 10**7, "cut_units": 200 * 10**7, "place_feed": 200 * 10**7,
}


def dot(left, right, dims=NN):
    return lax.dot_general(left, right, dims, preferred_element_type=f32)


def call(
    kernel, name, scalars, arrays, outs, scratch=(), far=(), far_outs=(), copies=0, room=10, after=()
):
    scratch = list(scratch)
    if copies:
        scratch.append(pltpu.SemaphoreType.DMA((copies,)))
    first, last = len(scalars) + len(arrays) + len(far), len(after)
    results = len(outs) + len(far_outs)
    mark = jax.ShapeDtypeStruct((8, 128), f32)

    def body(*refs):
        mine = refs[first + last :]
        mine[results][...] = jnp.zeros(mark.shape, mark.dtype)
        kernel(*refs[:first], *mine[:results], *mine[results + 1 :])

    return pl.pallas_call(
        body,
        in_specs=[SMEM] * len(scalars) + [VMEM] * len(arrays) + [HBM] * len(far) + [VMEM] * last,
        out_specs=[VMEM] * len(outs) + [HBM] * len(far_outs) + [VMEM],
        out_shape=[*outs, *[pltpu.HBM(a.shape, a.dtype) for a in far_outs], mark],
        scratch_shapes=scratch,
        compiler_params=pltpu.CompilerParams(vmem_limit_bytes=room * 2**20),
        cost_estimate=pl.CostEstimate(
            flops=WEIGHTS.get(name, 0), bytes_accessed=0, transcendentals=0
        ),
        name=name,
    )(
        *scalars, *arrays, *[pltpu.with_memory_space_constraint(a, pltpu.HBM) for a in far], *after
    )


def shape(*dims, dtype=bf16):
    return jax.ShapeDtypeStruct(dims, dtype)


def cut(i, size):
    return pl.ds(pl.multiple_of(i * size, size), size)


def copy(source, target, semaphore):
    return pltpu.make_async_copy(source, target, semaphore)


def column_sum(values):
    return jnp.sum(values, axis=0, keepdims=True)


def row_mean(values):
    return jnp.mean(values, axis=-1, keepdims=True)


def normalize(inputs):
    centre = inputs - row_mean(inputs)
    inverse = lax.rsqrt(row_mean(centre * centre) + EPSILON)
    return centre * inverse, inverse


def normalize_back(scaled, normed, inverse):
    return inverse * (scaled - row_mean(scaled) - normed * row_mean(scaled * normed))


BIAS_Q, BIAS_V, BIAS_OUT, GAIN_ONE, SHIFT_ONE, BIAS_DOWN, GAIN_TWO, SHIFT_TWO, BIAS_UP = range(9)


def vector(ref, row):
    return ref[row : row + 1, :]


def only(rows, h, height):
    parts = [jnp.zeros((height, rows.shape[1]), rows.dtype)] * (rows.shape[0] // height)
    parts[h] = rows[h * height : (h + 1) * height, :]
    return jnp.concatenate(parts)


def prepare_kernel(
    row_ref, b0, b1, b2, b3, b4, b5, b6, b7, w_qkv, w_out, qkv_near, out_near, mask, vectors, sems,
    *, pages, slots,
):
    load_qkv = copy(w_qkv, qkv_near, sems.at[0])
    load_qkv.start()
    load_out = copy(w_out, out_near, sems.at[1])
    load_out.start()
    width = vectors.shape[1]
    row = 0
    for part in (b0, b1, b2, b3, b4, b5, b6, b7):
        for i in range(part.shape[0] // width):
            vectors[row : row + 1, :] = part[i * width : (i + 1) * width].reshape(1, width)
            row += 1
    count = mask.shape[0]
    position = row_ref[pages]

    def page_of(shape, dim):
        at = lax.broadcasted_iota(jnp.int32, shape, dim)
        slot = ((at // slots) ^ position) * slots + at % slots
        page = jnp.zeros(shape, jnp.int32)
        end = 0
        for c in range(pages):
            end = end + row_ref[c]
            page = page + (slot >= end).astype(jnp.int32)
        return page

    mask[...] = jnp.where(
        page_of((count, count), 0) == page_of((1, count), 1), 0.0, MASKED
    )
    load_qkv.wait()
    load_out.wait()


def prepare(row, biases, w_qkv, w_out, slots, count):
    width = w_out.shape[0]
    rows = sum(b.shape[0] for b in biases) // width
    return call(
        functools.partial(prepare_kernel, pages=row.shape[0] - 1, slots=slots),
        "prepare", [row], biases,
        [
            shape(*w_qkv.shape), shape(*w_out.shape), shape(count, count, dtype=f32),
            shape(rows, width, dtype=f32),
        ],
        far=[w_qkv, w_out], copies=2,
    )[:4]


def attend_kernel(
    x0, x1, x2, x3, vectors, w_qkv, w_out, mask,
    normed_out, inverse_out, q_out, k_out, v_out, prob_out, context_out, tokens_out,
    tokens, q_kept, k_kept, v_kept, context_kept, probs_kept, sems, *, head_width,
):
    slots = x0.shape[0]
    count, width = tokens.shape
    wide = 4 * head_width
    groups = width // wide
    kept = ((0, q_kept, q_out), (1, k_kept, k_out), (2, v_kept, v_out), (3, context_kept, context_out))

    def keep(i, number, source, target):
        here = cut(i, wide)
        return copy(source.at[:, here], target.at[:, here], sems.at[number * groups + i])

    def keep_probs(i, h):
        return copy(
            probs_kept.at[4 * i + h], prob_out.at[4 * i + h], sems.at[4 * groups + 1 + 4 * i + h]
        )

    for i, block in enumerate((x0, x1, x2, x3)):
        tokens[i * slots : (i + 1) * slots, :] = block[...]
    keep_tokens = copy(tokens, tokens_out, sems.at[4 * groups])
    keep_tokens.start()

    @pl.loop(0, groups)
    def _(i):
        here = cut(i, wide)
        x = tokens[...]
        q = (dot(x, w_qkv[:, here]) + vectors[BIAS_Q : BIAS_Q + 1, here]).astype(bf16)
        k = dot(x, w_qkv[:, cut(i + groups, wide)]).astype(bf16)
        v = dot(x, w_qkv[:, cut(i + 2 * groups, wide)]) + vectors[BIAS_V : BIAS_V + 1, here]
        v = v.astype(bf16)
        q_kept[:, here] = q
        k_kept[:, here] = k
        v_kept[:, here] = v
        q_turned = (q * jnp.asarray(1.0 / math.sqrt(head_width), bf16)).T
        v_turned = v.T
        context = []
        for h in range(4):
            scores = dot(k, only(q_turned, h, head_width)) + mask[...]
            powers = jnp.exp(scores - jnp.max(scores, axis=0, keepdims=True))
            probs = (powers * (1.0 / jnp.sum(powers, axis=0, keepdims=True))).astype(bf16)
            probs_kept[4 * i + h] = probs
            keep_probs(i, h).start()
            context.append(dot(v_turned[h * head_width : (h + 1) * head_width, :], probs))
        context_kept[:, here] = jnp.concatenate(context).astype(bf16).T
        for number, source, target in kept:
            keep(i, number, source, target).start()

    attended = dot(context_kept[...], w_out[...]) + vector(vectors, BIAS_OUT)
    normed, inverse = normalize(tokens[...].astype(f32) + attended)
    normed_out[...] = normed
    inverse_out[...] = inverse
    for i in range(groups):
        for number, source, target in kept:
            keep(i, number, source, target).wait()
        for h in range(4):
            keep_probs(i, h).wait()
    keep_tokens.wait()


def attend(blocks, vectors, w_qkv, w_out, mask):
    slots, width = blocks[0].shape
    count = slots * len(blocks)
    groups = HEADS // 4
    narrow = shape(count, width)
    rows = pltpu.VMEM((count, width), bf16)
    return call(
        functools.partial(attend_kernel, head_width=width // HEADS),
        "attend", [], [*blocks, vectors, w_qkv, w_out, mask],
        [shape(count, width, dtype=f32), shape(count, 1, dtype=f32)],
        [rows, rows, rows, rows, rows, pltpu.VMEM((HEADS, count, count), bf16)],
        far_outs=[narrow, narrow, narrow, shape(HEADS, count, count), narrow, narrow],
        copies=4 * groups + 1 + HEADS, room=24,
    )[:8]


def feed_kernel(
    place, normed_one, vectors, c0, c1, c2, c3, w_up, w_down,
    keep_active, send_active, slope_out, lowered_out, first_out, r0, r1, r2, r3, vector_out,
    sum_out, total, *, shares,
):
    width = w_up.shape[0]
    hidden = w_up.shape[1]
    first_norm = normed_one[...] * vector(vectors, GAIN_ONE) + vector(vectors, SHIFT_ONE)
    first_out[...] = first_norm.astype(bf16)
    total[...] = first_norm + vector(vectors, BIAS_DOWN)
    odd = place[0] == 1
    rows = hidden // shares // 4
    apart = send_active is not None

    @pl.loop(0, hidden // width, unroll=True)
    def _(i):
        here = cut(i, width)
        raised = dot(first_out[...], w_up[:, here]) + vectors[pl.ds(BIAS_UP + i, 1), :]
        cumulative = 0.5 * (1.0 + lax.erf(raised * (1.0 / math.sqrt(2.0))))
        activated = (raised * cumulative).astype(bf16)
        bell = jnp.exp(-0.5 * raised * raised) * (1.0 / math.sqrt(2.0 * math.pi))
        slope_out[:, here] = (cumulative + raised * bell).astype(bf16)
        total[...] += dot(activated, w_down[here, :])
        turned = activated.T
        if apart:
            count = width // rows // 4
            for d in range(count):
                for x in range(2):
                    at = (d * 4 + x * 2) * rows
                    even_part = turned[at : at + rows, :]
                    odd_part = turned[at + rows : at + 2 * rows, :]
                    keep_active[x, i * count + d] = jnp.where(odd, odd_part, even_part)
                    send_active[x, i * count + d] = jnp.where(odd, even_part, odd_part)
        else:
            keep_active[here, :] = turned

    normed, inverse = normalize(total[...])
    gain = vector(vectors, GAIN_TWO)
    result = (normed * gain + vector(vectors, SHIFT_TWO)).astype(bf16)
    slots = c0.shape[0]
    for i, block in enumerate((r0, r1, r2, r3)):
        block[...] = result[i * slots : (i + 1) * slots, :]
    upstream = jnp.concatenate([c0[...], c1[...], c2[...], c3[...]]).astype(f32)
    grad_sum = normalize_back(upstream * gain, normed, inverse)
    sum_out[...] = grad_sum
    lowered = grad_sum.astype(bf16)
    lowered_out[...] = lowered
    vector_out[0:1, :] = column_sum(upstream * normed)
    vector_out[1:2, :] = column_sum(upstream)
    vector_out[2:3, :] = column_sum(lowered.astype(f32))


def feed(place, normed, vectors, cotangents, w_up, w_down, shares):
    count, width = normed.shape
    hidden = w_up.shape[1]
    rows = hidden // shares // 4
    narrow, full = shape(count, width), shape(count, width, dtype=f32)
    apart = rows % 16 == 0 and width % (4 * rows) == 0
    kernel = functools.partial(feed_kernel, shares=shares)
    if apart:
        active = [shape(2, shares, rows, count)] * 2
    else:
        active = [shape(hidden, count)]
        whole = kernel

        def kernel(*refs):
            whole(*refs[:10], None, *refs[10:])

    made = call(
        kernel, "feed", [place], [normed, vectors, *cotangents, w_up, w_down],
        active + [shape(count, hidden), narrow, narrow]
        + [shape(*cotangents[0].shape)] * 4 + [shape(8, width, dtype=f32), full],
        [pltpu.VMEM((count, width), f32)], room=14,
    )[:-1]
    if apart:
        return made
    parts = jnp.moveaxis(made[0].reshape(shares, 2, 2, rows, count), 0, 2)
    odd = place[0] == 1
    keep = jnp.where(odd, parts[:, 1], parts[:, 0])
    send = jnp.where(odd, parts[:, 0], parts[:, 1])
    return [keep, send, *made[1:]]


def grad_up_kernel(
    place, lowered, slope, first, w_down, inverse_one, vectors, sum_two, normed, w_up,
    keep, send, bias_out, attended_out, vector_out, sum_out, turned, raised_kept, weights, sems,
):
    width = lowered.shape[1]
    load = copy(w_up, weights, sems.at[0])
    load.start()
    turned[...] = first[...].T

    def work(b):
        here = cut(b, width)
        raised = dot(lowered[...], w_down[here, :], NT) * slope[:, here].astype(f32)
        raised = raised.astype(bf16)
        raised_kept[:, here] = raised
        bias_out[pl.ds(b, 1), :] = column_sum(raised.astype(f32))
        return dot(turned[...], raised).astype(bf16)

    @pl.loop(0, 2)
    def _(x):
        send[x] = work(2 * x + 1 - place[0])
        keep[x] = work(2 * x + place[0])

    load.wait()
    upstream = sum_two[...] + dot(raised_kept[...], weights[...], NT)
    grad_sum = normalize_back(
        upstream * vector(vectors, GAIN_ONE), normed[...], inverse_one[...]
    )
    sum_out[...] = grad_sum
    attended = grad_sum.astype(bf16)
    attended_out[...] = attended
    vector_out[0:1, :] = column_sum(upstream * normed[...])
    vector_out[1:2, :] = column_sum(upstream)
    vector_out[2:3, :] = column_sum(attended.astype(f32))


def grad_up(place, lowered, slope, first, w_down, inverse, vectors, w_up, sum_two, normed):
    count, width = lowered.shape
    hidden = w_down.shape[0]
    return call(
        grad_up_kernel, "grad_up", [place],
        [lowered, slope, first, w_down, inverse, vectors, sum_two, normed],
        [shape(2, width, width)] * 2
        + [shape(hidden // width, width, dtype=f32), shape(count, width)]
        + [shape(8, width, dtype=f32), shape(count, width, dtype=f32)],
        [
            pltpu.VMEM((width, count), bf16), pltpu.VMEM((count, hidden), bf16),
            pltpu.VMEM((width, hidden), bf16),
        ],
        far=[w_up], copies=1, room=28,
    )


def place_rows(place, blocks, rows, sems):
    copies = [copy(block, rows.at[place[1] ^ i], sems.at[i]) for i, block in enumerate(blocks)]
    for one in copies:
        one.start()
    return copies


def grad_down_kernel(
    place, active, other_active, lowered, other_lowered, r0, r1, r2, r3, down, rows_out, sems
):
    copies = place_rows(place, (r0, r1, r2, r3), rows_out, sems)
    _, shares, rows, count = active.shape
    width = lowered.shape[1]

    for x in range(2):

        @pl.loop(0, shares, step=2, unroll=shares <= 8)
        def _(d):
            mine = active[x, pl.ds(d, 2)].reshape(2 * rows, count)
            other = other_active[x, pl.ds(d, 2)].reshape(2 * rows, count)
            value = dot(mine, lowered[...]) + dot(other, other_lowered[...])
            down[x, pl.ds(d, 2)] = value.astype(bf16).reshape(2, rows, width)

    for one in copies:
        one.wait()


def grad_down(place, active, other_active, lowered, other_lowered, blocks, after):
    _, shares, rows, _ = active.shape
    slots, width = blocks[0].shape
    return call(
        grad_down_kernel, "grad_down", [place],
        [active, other_active, lowered, other_lowered, *blocks],
        [shape(2, shares, rows, width)], far_outs=[shape(4, slots, width)], copies=4, after=after,
    )


def small_pieces(shares, width):
    q, v, gain_one, shift_one, out, gain_two, shift_two, down, up = range(9)
    share = width // shares

    def flat(row, first):
        return row + first // width, first % width

    def pieces(d):
        at = d * share
        return (
            (flat(q, 2 * at), flat(q, 2 * at + share), (out, at)),
            ((gain_one, at), (shift_one, at), (down, at)),
            ((gain_two, at), (shift_two, at), flat(up, 4 * at)),
            tuple(flat(up, 4 * at + j * share) for j in (1, 2, 3)),
        )

    return [pieces(d) for d in range(shares)]


def attend_back_kernel(
    place, attended, vector_one, vector_two, bias_up, tokens, context, prob, q_ref, k_ref, v_ref, w_out,
    grads_out, keep_0, keep_1, keep_2, send_0, send_1, send_2, small_keep, small_send,
    rows_kept, turned, turned_context, probs_kept, q_kept, k_kept, v_kept, weights, sums, small, sems,
    *, head_width,
):
    count, width = attended.shape
    wide = 4 * head_width
    groups = width // wide
    shares = small.shape[1]
    rows = width // shares
    joined = small_keep is None

    def load(i):
        here = cut(i, wide)
        pairs = [
            (w_out.at[here, :], weights.at[here, :]),
            (v_ref.at[:, here], v_kept.at[:, here]),
            (q_ref.at[:, here], q_kept.at[:, here]),
            (k_ref.at[:, here], k_kept.at[:, here]),
        ]
        pairs = pairs + [(prob.at[4 * i + h], probs_kept.at[4 * i + h]) for h in range(4)]
        return [copy(s, t, sems.at[8 * i + n]) for n, (s, t) in enumerate(pairs)]

    load_tokens = copy(tokens, rows_kept.at[0], sems.at[8 * groups])
    load_context = copy(context, rows_kept.at[1], sems.at[8 * groups + 1])
    for one in load(0):
        one.start()
    load_tokens.start()
    load_context.start()
    head = lax.broadcasted_iota(jnp.int32, (count, wide), 1) // head_width
    none = jnp.zeros((count, wide), bf16)
    odd = place[0] == 1

    @pl.loop(0, groups, unroll=True)
    def _(i):
        here = cut(i, wide)

        @pl.when(i + 1 < groups)
        def _():
            for one in load(i + 1):
                one.start()

        waits = load(i)
        waits[0].wait()
        grad_context = dot(attended[...], weights[here, :], NT).astype(bf16)
        context_turned = grad_context.T
        scaling = jnp.asarray(1.0 / math.sqrt(head_width), bf16)
        for one in waits[1:4]:
            one.wait()
        scaled_q = q_kept[:, here] * scaling
        k_turned = (k_kept[:, here] * scaling).T
        v = v_kept[:, here]

        @pl.when(i == 0)
        def _():
            load_tokens.wait()
            turned[...] = rows_kept[0].T
            load_context.wait()
            turned_context[...] = rows_kept[1].T

        for one in waits[4:]:
            one.wait()
        grad_k = jnp.zeros((count, wide), f32)
        grad_v = grad_k
        grad_q = []
        for h in range(4):
            mine = head == h
            probs = probs_kept[4 * i + h]
            wider = probs.astype(f32)
            lines = slice(h * head_width, (h + 1) * head_width)
            balance = column_sum(
                context_turned[lines, :].astype(f32)
                * turned_context[pl.ds(i * wide + h * head_width, head_width), :].astype(f32)
            )
            weighted = dot(v, only(context_turned, h, head_width)) - balance
            grad_scores = (wider * weighted).astype(bf16)
            grad_v = grad_v + dot(probs, jnp.where(mine, grad_context, none))
            grad_k = grad_k + dot(grad_scores, jnp.where(mine, scaled_q, none))
            grad_q.append(dot(k_turned[h * head_width : (h + 1) * head_width, :], grad_scores))
        grad_q = jnp.concatenate(grad_q).astype(bf16).T
        grad_k = grad_k.astype(bf16)
        grad_v = grad_v.astype(bf16)
        grads_out[:, here] = grad_q
        grads_out[:, cut(i + groups, wide)] = grad_k
        grads_out[:, cut(i + 2 * groups, wide)] = grad_v
        sums[0:1, here] = column_sum(grad_q.astype(f32))
        sums[1:2, here] = column_sum(grad_v.astype(f32))
        pieces = (
            dot(turned[...], grad_q).astype(bf16),
            dot(turned[...], grad_k).astype(bf16),
            dot(turned[...], grad_v).astype(bf16),
            dot(turned_context[...], attended[:, here]).astype(bf16),
        )
        for s, (keep, send) in enumerate(((keep_0, send_0), (keep_1, send_1), (keep_2, send_2))):

            @pl.when(i == s)
            def _(s=s, keep=keep, send=send):
                for x in range(2):
                    kept = jnp.where(odd, pieces[2 * x + 1], pieces[2 * x])
                    sent = jnp.where(odd, pieces[2 * x], pieces[2 * x + 1])
                    if s or not joined:
                        keep[x] = kept
                        send[x] = sent
                    else:
                        for d in range(shares):
                            keep[x, d, 0:rows, :] = kept[d * rows : (d + 1) * rows, :]
                            send[x, d, 0:rows, :] = sent[d * rows : (d + 1) * rows, :]

    sums[2:5, :] = vector_one[0:3, :]
    sums[5:8, :] = vector_two[0:3, :]
    sums[8:12, :] = bias_up[...]
    share = width // shares
    small[...] = jnp.zeros_like(small)
    for d, by_blk in enumerate(small_pieces(shares, width)):
        for b, three in enumerate(by_blk):
            for j, (row, column) in enumerate(three):
                small[b, d, j : j + 1, 0:share] = sums[row : row + 1, column : column + share]
    for x in range(2):
        even_part = small[2 * x].astype(bf16)
        odd_part = small[2 * x + 1].astype(bf16)
        kept = jnp.where(odd, odd_part, even_part)
        sent = jnp.where(odd, even_part, odd_part)
        if joined:
            keep_0[x, :, rows:, :] = kept
            send_0[x, :, rows:, :] = sent
        else:
            small_keep[x] = kept
            small_send[x] = sent


def attend_back(place, attended, small, far, shares, after):
    count, width = attended.shape
    wide = 4 * (width // HEADS)
    groups = width // wide
    rows, turned = pltpu.VMEM((count, width), bf16), pltpu.VMEM((width, count), bf16)
    share = width // shares
    joined = share % 16 == 0
    plain, extra = shape(2, width, wide), [shape(2, shares, 16, wide)] * 2
    first = shape(2, shares, share + 16, wide) if joined else plain
    inner = functools.partial(attend_back_kernel, head_width=width // HEADS)

    def kernel(*refs):
        if joined:
            refs = (*refs[:19], None, None, *refs[19:])
        inner(*refs)

    grads, keep_0, keep_1, keep_2, send_0, send_1, send_2, *small, mark = call(
        kernel, "attend_back", [place], [attended, *small],
        [shape(count, 3 * width)] + [first, plain, plain] * 2 + ([] if joined else extra),
        [
            pltpu.VMEM((2, count, width), bf16), turned, turned,
            pltpu.VMEM((HEADS, count, count), bf16), rows, rows, rows,
            pltpu.VMEM((width, width), bf16),
            pltpu.VMEM((16, width), f32), pltpu.VMEM((4, shares, 16, wide), f32),
        ],
        far=far, copies=8 * groups + 2, room=26, after=after,
    )
    return [keep_0, keep_1, keep_2], [send_0, send_1, send_2], small, grads, mark


def grad_tokens_kernel(grads, w_qkv, sum_one, r0, r1, r2, r3):
    result = (sum_one[...] + dot(grads[...], w_qkv[...], NT)).astype(bf16)
    slots = r0.shape[0]
    for i, block in enumerate((r0, r1, r2, r3)):
        block[...] = result[i * slots : (i + 1) * slots, :]


def grad_tokens(sum_one, grads, w_qkv, slots, after):
    count, width = sum_one.shape
    *blocks, mark = call(
        grad_tokens_kernel, "grad_tokens", [], [grads, w_qkv, sum_one], [shape(slots, width)] * 4,
        room=12, after=after,
    )
    return blocks, mark


def swap(block, axis, bit):
    return lax.ppermute(block, axis, [(i, i ^ bit) for i in range(lax.axis_size(axis))])


def pick(block, index, dim=0):
    return lax.dynamic_index_in_dim(block, index, dim, keepdims=False)


def every(count, work):
    if count <= 8:
        for number in range(count):
            work(number)
    else:
        pl.loop(0, count)(work)


def cut_units(bits, units, extra, orders, flip, after):
    parts, dims = len(orders), len(orders[0])
    arrays, numbers = [], {}
    for array in [a for unit in units for terms, _ in unit for a in terms] + list(extra):
        if id(array) not in numbers:
            numbers[id(array)] = len(arrays)
            arrays.append(array)
    rows = [units[0][s][0][0].shape[-2] for s in range(parts)]
    size = sum({id(terms[0]): terms[0].shape[-1] for terms, _ in units[0]}.values()) // parts
    more = [extra[0].shape[-2] if extra and s == 0 else 0 for s in range(parts)]
    outs = [shape(2 ** (dims - 1), len(units) * r + m, size) for r, m in zip(rows, more)]

    def kernel(bits_ref, *refs):
        ins, results = refs[: len(arrays)], refs[len(arrays) :]

        def added(terms, at):
            total = ins[numbers[id(terms[0])]][at]
            for term in terms[1:]:
                total = total + ins[numbers[id(term)]][at]
            return total

        def work(number):
            for s, order in enumerate(orders):
                index = [None] * dims
                index[order[0]] = bits_ref[order[0]] ^ flip
                for i, n in enumerate(order[1:]):
                    index[n] = (number >> (dims - 2 - i)) & 1
                for u, unit in enumerate(units):
                    terms, column = unit[s]
                    at = (*index, slice(None), slice(column * size, (column + 1) * size))
                    results[s][number, u * rows[s] : (u + 1) * rows[s]] = added(terms, at)
                if more[s]:
                    results[s][number, len(units) * rows[s] :] = added(extra, tuple(index))

        every(2 ** (dims - 1), work)

    *made, mark = call(kernel, "cut_units", [bits], arrays, outs, after=after)
    return made, mark


def halve(bits, pairs, axes, join, after=(), place=None, blocks=()):
    taken = pairs[0][0].shape[0] // (2 if axes else 1)
    sizes = [a.shape[1] for a, _ in pairs]
    width = pairs[0][0].shape[2]
    flips = (1, 0) if axes else (0,)
    outs = [shape(taken, sum(sizes), width)] if join else [shape(taken, n, width) for n in sizes]
    outs = outs * len(flips)
    arrays = [a for pair in pairs for a in pair]

    def kernel(*refs):
        copies = []
        if blocks:
            place_ref, *refs, sems = refs
            copies = place_rows(place_ref, refs[1 + len(arrays) : 5 + len(arrays)], refs[-1], sems)
        bits_ref, ins, results = refs[0], refs[1 : 1 + len(arrays)], refs[1 + len(arrays) + len(blocks) :]

        def work(number):
            for f, flip in enumerate(flips):
                for s in range(len(pairs)):
                    at = number + ((bits_ref[axes[s]] ^ flip) * taken if axes else 0)
                    total = ins[2 * s][at] + ins[2 * s + 1][at]
                    if join:
                        first = sum(sizes[:s])
                        results[f][number, first : first + sizes[s]] = total
                    else:
                        results[f * len(pairs) + s][number] = total

        every(taken, work)
        for one in copies:
            one.wait()

    far_outs = [shape(4, *blocks[0].shape)] if blocks else []
    *made, mark = call(
        kernel, "halve", [place, bits] if blocks else [bits], arrays + list(blocks), outs,
        far_outs=far_outs, copies=len(blocks), room=6, after=after,
    )
    made, rows = made[: len(outs)], made[len(outs) :]
    half = len(outs) // len(flips)
    return made[:half], made[half:], mark, *rows


class Group:
    def __init__(self, units, extra, bits, names):
        self.units, self.extra, self.bits, self.names = units, extra, bits, names
        size = len(names)
        turn = [0, size - 1, size - 2]
        rest = list(range(size - 3, 0, -1))
        self.orders = [turn[s:] + turn[:s] + rest for s in range(3)]
        self.stage = 0
        self.pairs = None

    def send(self, blocks):
        return [
            swap(block, *self.names[order[self.stage]]) for block, order in zip(blocks, self.orders)
        ]

    def begin(self, after):
        sent, mark = cut_units(self.bits, self.units, self.extra, self.orders, 1, after)
        self.arrived = self.send(sent)
        return mark

    def rest(self, after):
        keep, mark = cut_units(self.bits, self.units, self.extra, self.orders, 0, after)
        self.pairs = list(zip(keep, self.arrived))
        self.stage = 1
        return mark

    def step(self, after, place=None, blocks=()):
        axes = [order[self.stage] for order in self.orders]
        sent, keep, mark, *rows = halve(
            self.bits, self.pairs, axes, self.stage == 3, after, place, blocks
        )
        self.pairs = list(zip(keep, self.send(sent)))
        self.stage += 1
        return (mark, *rows) if rows else mark

    def finish(self, after):
        (own,), _, mark = halve(self.bits, self.pairs, None, False, after)
        across = swap(own, "blk", 2)
        return (own, swap(own, "blk", 1), across, swap(across, "blk", 1)), mark


def chosen(place, b, refs):
    relative = place[1] ^ b
    values = [ref[...] for ref in refs]
    return jnp.where(
        relative < 2,
        jnp.where(relative == 0, values[0], values[1]),
        jnp.where(relative == 2, values[2], values[3]),
    ).astype(f32)


def place_feed(place, pieces, rows, after):
    size = pieces[0].shape[2]
    width = 3 * size

    def kernel(place_ref, p0, p1, p2, p3, down, up):
        for b in range(4):
            for s in range(3):
                at = 2 * s * rows
                columns = slice(s * size, (s + 1) * size)
                value = chosen(place_ref, b, [p.at[0, at : at + rows] for p in (p0, p1, p2, p3)])
                down[b * rows : (b + 1) * rows, columns] = value
                at = at + rows
                columns = slice(b * width + s * size, b * width + (s + 1) * size)
                value = chosen(place_ref, b, [p.at[0, at : at + rows] for p in (p0, p1, p2, p3)])
                up[:, columns] = value

    return call(
        kernel, "place_feed", [place], pieces,
        [shape(4 * rows, width, dtype=f32), shape(rows, 4 * width, dtype=f32)], after=after,
    )


def place_own(place, pieces, rows, shares, after):
    size = pieces[0].shape[2]
    width = 3 * size
    share = width // shares
    extra = pieces[0].shape[1] - 3 * rows

    def kernel(place_ref, p0, p1, p2, p3, qkv, out, *small):
        refs = (p0, p1, p2, p3)
        bias_qv, bias_out, gain_one, shift_one, bias_up, bias_down, gain_two, shift_two = small
        for b in range(4):
            for s in range(3):
                at = s * rows + (extra if s else 0)
                value = chosen(place_ref, b, [p.at[0, at : at + rows] for p in refs])
                columns = slice(s * size, (s + 1) * size)
                if b == 3:
                    out[:, columns] = value
                else:
                    qkv[:, b * width + s * size : b * width + (s + 1) * size] = value
            value = chosen(place_ref, b, [p.at[0, rows : rows + extra] for p in refs])
            targets = (
                ((bias_qv, 0), (bias_qv, 1), (bias_out, 0)),
                ((gain_one, 0), (shift_one, 0), (bias_down, 0)),
                ((gain_two, 0), (shift_two, 0), (bias_up, 0)),
                ((bias_up, 1), (bias_up, 2), (bias_up, 3)),
            )[b]
            for j, (ref, part) in enumerate(targets):
                ref[:, part * share : (part + 1) * share] = value[j : j + 1, 0:share]

    vectors = [shape(1, n * share, dtype=f32) for n in (2, 1, 1, 1, 4, 1, 1, 1)]
    return call(
        kernel, "place_own", [place], pieces,
        [shape(rows, 3 * width, dtype=f32), shape(rows, width, dtype=f32), *vectors],
        after=after,
    )[:10]


def shards(
    tokens, lengths, w_qkv, bias_qv, w_out, bias_out, norm1_gain, norm1_bias, w_up, bias_up,
    w_down, bias_down, norm2_gain, norm2_bias, cotangent,
):
    rows, slots, width = tokens.shape
    shares = lax.axis_size("dp")
    dp_bits = shares.bit_length() - 1
    position = lax.axis_index("blk").astype(jnp.int32)
    group = lax.axis_index("dp").astype(jnp.int32)
    place = jnp.stack([position % 2, position])
    names = [("blk", 2)] + [("dp", 1 << i) for i in reversed(range(dp_bits))]
    bits = jnp.stack([position // 2] + [(group >> i) % 2 for i in reversed(range(dp_bits))])

    def gather_row(array):
        return [pick(array, position)] + [
            swap(pick(array, position ^ i), "blk", i) for i in (2, 3, 1)
        ]

    def in_order(blocks):
        return [blocks[0], blocks[3], blocks[1], blocks[2]]

    def scatter_row(blocks):
        return [blocks[0]] + [swap(blocks[i], "blk", i) for i in range(1, rows)]

    biases = [
        bias_qv, bias_out, norm1_gain, norm1_bias, bias_down, norm2_gain, norm2_bias, bias_up
    ]
    row = jnp.concatenate([pick(lengths, position), position[None]])
    blocks = gather_row(tokens)
    blocks, cotangent = lax.optimization_barrier((blocks, cotangent))
    blocks = in_order(blocks)
    cotangents = in_order(gather_row(cotangent))
    qkv_near, out_near, mask, vectors = prepare(
        row, biases, w_qkv, w_out, slots, rows * slots
    )
    normed, inverse, q, k, v, prob, context, row_tokens = attend(
        blocks, vectors, qkv_near, out_near, mask
    )
    keep_active, send_active, slope, lowered, first, o0, o1, o2, o3, vector_two, sum_two = feed(
        place, normed, vectors, cotangents, w_up, w_down, shares
    )
    got_active, got_lowered = swap(send_active, "blk", 1), swap(lowered, "blk", 1)
    keep_up, send_up, grad_bias_up, attended, vector_one, sum_one, mark = grad_up(
        place, lowered, slope, first, w_down, inverse, vectors, w_up, sum_two, normed
    )
    got_up = swap(send_up, "blk", 1)
    down, outputs, mark = grad_down(
        place, keep_active, got_active, lowered, got_lowered, scatter_row([o0, o1, o2, o3]), [mark]
    )

    def chunks(array):
        return array.reshape((2,) * (1 + dp_bits) + (-1, array.shape[-1]))

    down, keep_up, got_up = chunks(down), chunks(keep_up), chunks(got_up)
    feed_group = Group(
        [[([down], s) for s in range(3)], [([keep_up, got_up], s) for s in range(3)]],
        (), bits, names,
    )
    mark = feed_group.begin([mark])
    keeps, sends, small, grads, mark = attend_back(
        place, attended, [vector_one, vector_two, grad_bias_up],
        [row_tokens, context, prob, q, k, v, w_out], shares, [mark],
    )
    gots = [swap(send, "blk", 1) for send in sends]
    small = [chunks(small[0]), chunks(swap(small[1], "blk", 1))] if small else ()
    own_group = Group(
        [[([chunks(keep), chunks(got)], 0) for keep, got in zip(keeps, gots)]], small, bits, names
    )
    share = width // shares
    mark = feed_group.rest([mark])
    mark = feed_group.step([mark])
    mark = own_group.begin([mark])
    tokens_parts, mark = grad_tokens(sum_one, grads, w_qkv, slots, [mark])
    mark = own_group.rest([mark])
    for _ in range(dp_bits - 3):
        mark = feed_group.step([mark])
        mark = own_group.step([mark])
    mark = feed_group.step([mark])
    mark = own_group.step([mark])
    mark = feed_group.step([mark])
    mark = own_group.step([mark])
    feed_pieces, mark = feed_group.finish([mark])
    mark, token_grads = own_group.step([mark], place, scatter_row(tokens_parts))
    own_pieces, mark = own_group.finish([mark])
    down, up, mark = place_feed(place, feed_pieces, share, [mark])
    (
        grad_w_qkv, grad_w_out, sum_qv, sum_out, sum_gain_one, sum_shift_one, sum_up, sum_down,
        sum_gain_two, sum_shift_two,
    ) = place_own(place, own_pieces, share, shares, [mark])
    return (
        outputs,
        token_grads,
        grad_w_qkv,
        sum_qv.reshape(-1),
        grad_w_out,
        sum_out.reshape(-1),
        sum_gain_one.reshape(-1),
        sum_shift_one.reshape(-1),
        up,
        sum_up.reshape(-1),
        down,
        sum_down.reshape(-1),
        sum_gain_two.reshape(-1),
        sum_shift_two.reshape(-1),
    )


def solution(mesh):
    row_spec = P("dp", "blk", None)
    in_specs = (row_spec, P("dp", None)) + (P(),) * 12 + (row_spec,)
    wide, flat = P("dp", None), P("dp")
    out_specs = (
        row_spec, row_spec, wide, flat, wide, flat, flat, flat, wide, flat, wide, flat, flat, flat,
    )
    return jax.shard_map(shards, mesh=mesh, in_specs=in_specs, out_specs=out_specs, check_vma=False)
```

```python
import functools
import math

import jax
import jax.numpy as jnp
from jax import lax
from jax.experimental import pallas as pl
from jax.experimental.pallas import tpu as pltpu
from jax.sharding import PartitionSpec as P

HEADS = 12
EPSILON = 1e-12
MASKED = -1e30
f32 = jnp.float32
bf16 = jnp.bfloat16
NN = (((1,), (0,)), ((), ()))
NT = (((1,), (1,)), ((), ()))
TN = (((0,), (0,)), ((), ()))
VMEM = pl.BlockSpec(memory_space=pltpu.VMEM)
SMEM = pl.BlockSpec(memory_space=pltpu.SMEM)
HBM = pl.BlockSpec(memory_space=pltpu.HBM)
ANY = pl.BlockSpec(memory_space=pl.ANY)


WEIGHTS = {
    "prepare": 60 * 10**9, "attend": 60 * 10**9, "feed": 60 * 10**9, "grad_up": 60 * 10**9,
    "grad_down": 60 * 10**9, "attend_back": 60 * 10**9, "grad_tokens": 60 * 10**8,
    "halve": 200 * 10**7, "cut_units": 200 * 10**7, "place_all": 200 * 10**7,
}


def dot(left, right, dims=NN):
    return lax.dot_general(left, right, dims, preferred_element_type=f32)


def call(
    kernel, name, scalars, arrays, outs, scratch=(), far=(), far_outs=(), copies=0, room=10, after=()
):
    scratch = list(scratch)
    if copies:
        scratch.append(pltpu.SemaphoreType.DMA((copies,)))
    first, last = len(scalars) + len(arrays) + len(far), len(after)
    results = len(outs) + len(far_outs)
    mark = jax.ShapeDtypeStruct((8, 128), f32)

    def body(*refs):
        mine = refs[first + last :]
        mine[results][...] = jnp.zeros(mark.shape, mark.dtype)
        kernel(*refs[:first], *mine[:results], *mine[results + 1 :])

    return pl.pallas_call(
        body,
        in_specs=[SMEM] * len(scalars) + [VMEM] * len(arrays) + [HBM] * len(far) + [VMEM] * last,
        out_specs=[VMEM] * len(outs) + [HBM] * len(far_outs) + [VMEM],
        out_shape=[*outs, *[pltpu.HBM(a.shape, a.dtype) for a in far_outs], mark],
        scratch_shapes=scratch,
        compiler_params=pltpu.CompilerParams(vmem_limit_bytes=room * 2**20),
        cost_estimate=pl.CostEstimate(
            flops=WEIGHTS.get(name, 0), bytes_accessed=0, transcendentals=0
        ),
        name=name,
    )(
        *scalars, *arrays, *[pltpu.with_memory_space_constraint(a, pltpu.HBM) for a in far], *after
    )


def shape(*dims, dtype=bf16):
    return jax.ShapeDtypeStruct(dims, dtype)


def cut(i, size):
    return pl.ds(pl.multiple_of(i * size, size), size)


def copy(source, target, semaphore):
    return pltpu.make_async_copy(source, target, semaphore)


def column_sum(values):
    return jnp.sum(values, axis=0, keepdims=True)


def row_mean(values):
    return jnp.mean(values, axis=-1, keepdims=True)


def normalize(inputs):
    centre = inputs - row_mean(inputs)
    inverse = lax.rsqrt(row_mean(centre * centre) + EPSILON)
    return centre * inverse, inverse


def normalize_back(scaled, normed, inverse):
    return inverse * (scaled - row_mean(scaled) - normed * row_mean(scaled * normed))


BIAS_Q, BIAS_V, BIAS_OUT, GAIN_ONE, SHIFT_ONE, BIAS_DOWN, GAIN_TWO, SHIFT_TWO, BIAS_UP = range(9)


def vector(ref, row):
    return ref[row : row + 1, :]


def only(rows, h, height):
    parts = [jnp.zeros((height, rows.shape[1]), rows.dtype)] * (rows.shape[0] // height)
    parts[h] = rows[h * height : (h + 1) * height, :]
    return jnp.concatenate(parts)


def prepare_kernel(
    row_ref, w_qkv, w_out, b0, b1, b2, b3, b4, b5, b6, b7,
    qkv_near, out_near, mask, vectors, s0, s1, s2, s3, s4, s5, s6, s7, sems, *, pages, slots,
):
    pairs = zip((b0, b1, b2, b3, b4, b5, b6, b7), (s0, s1, s2, s3, s4, s5, s6, s7))
    loads = [copy(a, b, sems.at[2 + i]) for i, (a, b) in enumerate(pairs)]
    for one in loads:
        one.start()
    load_qkv = copy(w_qkv, qkv_near, sems.at[0])
    load_qkv.start()
    load_out = copy(w_out, out_near, sems.at[1])
    load_out.start()
    count = mask.shape[0]
    position = row_ref[pages]

    def page_of(shape, dim):
        at = lax.broadcasted_iota(jnp.int32, shape, dim)
        slot = ((at // slots) ^ position) * slots + at % slots
        page = jnp.zeros(shape, jnp.int32)
        end = 0
        for c in range(pages):
            end = end + row_ref[c]
            page = page + (slot >= end).astype(jnp.int32)
        return page

    mask[...] = jnp.where(
        page_of((count, count), 0) == page_of((1, count), 1), 0.0, MASKED
    )
    for one in loads:
        one.wait()
    width = vectors.shape[1]
    row = 0
    for part in (s0, s1, s2, s3, s4, s5, s6, s7):
        for i in range(part.shape[0] // width):
            vectors[row : row + 1, :] = part[i * width : (i + 1) * width].reshape(1, width)
            row += 1
    load_qkv.wait()
    load_out.wait()


def prepare(row, biases, w_qkv, w_out, slots, count):
    width = w_out.shape[0]
    rows = sum(b.shape[0] for b in biases) // width
    return call(
        functools.partial(prepare_kernel, pages=row.shape[0] - 1, slots=slots),
        "prepare", [row], [],
        [
            shape(*w_qkv.shape), shape(*w_out.shape), shape(count, count, dtype=f32),
            shape(rows, width, dtype=f32),
        ],
        [pltpu.VMEM(b.shape, f32) for b in biases],
        far=[w_qkv, w_out, *biases], copies=2 + len(biases),
    )


def attend_kernel(
    x0, x1, x2, x3, vectors, w_qkv, w_out, mask,
    normed_out, inverse_out, q_out, k_out, v_out, prob_out, context_out, tokens_out,
    tokens, q_kept, k_kept, v_kept, context_kept, probs_kept, sems, *, head_width,
):
    slots = x0.shape[0]
    count, width = tokens.shape
    wide = 4 * head_width
    groups = width // wide
    kept = ((0, q_kept, q_out), (1, k_kept, k_out), (2, v_kept, v_out), (3, context_kept, context_out))

    def keep(i, number, source, target):
        here = cut(i, wide)
        return copy(source.at[:, here], target.at[:, here], sems.at[number * groups + i])

    def keep_probs(i, h):
        return copy(
            probs_kept.at[4 * i + h], prob_out.at[4 * i + h], sems.at[4 * groups + 1 + 4 * i + h]
        )

    for i, block in enumerate((x0, x1, x2, x3)):
        tokens[i * slots : (i + 1) * slots, :] = block[...]
    keep_tokens = copy(tokens, tokens_out, sems.at[4 * groups])
    keep_tokens.start()

    @pl.loop(0, groups)
    def _(i):
        here = cut(i, wide)
        x = tokens[...]
        q = (dot(x, w_qkv[:, here]) + vectors[BIAS_Q : BIAS_Q + 1, here]).astype(bf16)
        k = dot(x, w_qkv[:, cut(i + groups, wide)]).astype(bf16)
        v = dot(x, w_qkv[:, cut(i + 2 * groups, wide)]) + vectors[BIAS_V : BIAS_V + 1, here]
        v = v.astype(bf16)
        q_kept[:, here] = q
        k_kept[:, here] = k
        v_kept[:, here] = v
        q_turned = (q * jnp.asarray(1.0 / math.sqrt(head_width), bf16)).T
        v_turned = v.T
        context = []
        for h in range(4):
            scores = dot(k, only(q_turned, h, head_width)) + mask[...]
            powers = jnp.exp(scores - jnp.max(scores, axis=0, keepdims=True))
            probs = (powers * (1.0 / jnp.sum(powers, axis=0, keepdims=True))).astype(bf16)
            probs_kept[4 * i + h] = probs
            keep_probs(i, h).start()
            context.append(dot(v_turned[h * head_width : (h + 1) * head_width, :], probs))
        context_kept[:, here] = jnp.concatenate(context).astype(bf16).T
        for number, source, target in kept:
            keep(i, number, source, target).start()

    attended = dot(context_kept[...], w_out[...]) + vector(vectors, BIAS_OUT)
    normed, inverse = normalize(tokens[...].astype(f32) + attended)
    normed_out[...] = normed
    inverse_out[...] = inverse
    for i in range(groups):
        for number, source, target in kept:
            keep(i, number, source, target).wait()
        for h in range(4):
            keep_probs(i, h).wait()
    keep_tokens.wait()


def attend(blocks, vectors, w_qkv, w_out, mask):
    slots, width = blocks[0].shape
    count = slots * len(blocks)
    groups = HEADS // 4
    narrow = shape(count, width)
    rows = pltpu.VMEM((count, width), bf16)
    return call(
        functools.partial(attend_kernel, head_width=width // HEADS),
        "attend", [], [*blocks, vectors, w_qkv, w_out, mask],
        [shape(count, width, dtype=f32), shape(count, 1, dtype=f32)],
        [rows, rows, rows, rows, rows, pltpu.VMEM((HEADS, count, count), bf16)],
        far_outs=[narrow, narrow, narrow, shape(HEADS, count, count), narrow, narrow],
        copies=4 * groups + 1 + HEADS, room=24,
    )[:8]


def feed_kernel(
    place, normed_one, vectors, c0, c1, c2, c3, w_up, w_down,
    keep_active, send_active, slope_out, lowered_out, first_out, r0, r1, r2, r3, vector_out,
    sum_out, total, *, shares,
):
    width = w_up.shape[0]
    hidden = w_up.shape[1]
    first_norm = normed_one[...] * vector(vectors, GAIN_ONE) + vector(vectors, SHIFT_ONE)
    first_out[...] = first_norm.astype(bf16)
    total[...] = first_norm + vector(vectors, BIAS_DOWN)
    odd = place[0] == 1
    rows = hidden // shares // 4
    apart = send_active is not None

    @pl.loop(0, hidden // width, unroll=True)
    def _(i):
        here = cut(i, width)
        raised = dot(first_out[...], w_up[:, here]) + vectors[pl.ds(BIAS_UP + i, 1), :]
        cumulative = 0.5 * (1.0 + lax.erf(raised * (1.0 / math.sqrt(2.0))))
        activated = (raised * cumulative).astype(bf16)
        bell = jnp.exp(-0.5 * raised * raised) * (1.0 / math.sqrt(2.0 * math.pi))
        slope_out[:, here] = (cumulative + raised * bell).astype(bf16)
        total[...] += dot(activated, w_down[here, :])
        turned = activated.T
        if apart:
            count = width // rows // 4
            for d in range(count):
                for x in range(2):
                    at = (d * 4 + x * 2) * rows
                    even_part = turned[at : at + rows, :]
                    odd_part = turned[at + rows : at + 2 * rows, :]
                    keep_active[x, i * count + d] = jnp.where(odd, odd_part, even_part)
                    send_active[x, i * count + d] = jnp.where(odd, even_part, odd_part)
        else:
            keep_active[here, :] = turned

    normed, inverse = normalize(total[...])
    gain = vector(vectors, GAIN_TWO)
    result = (normed * gain + vector(vectors, SHIFT_TWO)).astype(bf16)
    slots = c0.shape[0]
    for i, block in enumerate((r0, r1, r2, r3)):
        block[...] = result[i * slots : (i + 1) * slots, :]
    upstream = jnp.concatenate([c0[...], c1[...], c2[...], c3[...]]).astype(f32)
    grad_sum = normalize_back(upstream * gain, normed, inverse)
    sum_out[...] = grad_sum
    lowered = grad_sum.astype(bf16)
    lowered_out[...] = lowered
    vector_out[0:1, :] = column_sum(upstream * normed)
    vector_out[1:2, :] = column_sum(upstream)
    vector_out[2:3, :] = column_sum(lowered.astype(f32))


def feed(place, normed, vectors, cotangents, w_up, w_down, shares):
    count, width = normed.shape
    hidden = w_up.shape[1]
    rows = hidden // shares // 4
    narrow, full = shape(count, width), shape(count, width, dtype=f32)
    apart = rows % 16 == 0 and width % (4 * rows) == 0
    kernel = functools.partial(feed_kernel, shares=shares)
    if apart:
        active = [shape(2, shares, rows, count)] * 2
    else:
        active = [shape(hidden, count)]
        whole = kernel

        def kernel(*refs):
            whole(*refs[:10], None, *refs[10:])

    made = call(
        kernel, "feed", [place], [normed, vectors, *cotangents, w_up, w_down],
        active + [shape(count, hidden), narrow, narrow]
        + [shape(*cotangents[0].shape)] * 4 + [shape(8, width, dtype=f32), full],
        [pltpu.VMEM((count, width), f32)], room=14,
    )[:-1]
    if apart:
        return made
    parts = jnp.moveaxis(made[0].reshape(shares, 2, 2, rows, count), 0, 2)
    odd = place[0] == 1
    keep = jnp.where(odd, parts[:, 1], parts[:, 0])
    send = jnp.where(odd, parts[:, 0], parts[:, 1])
    return [keep, send, *made[1:]]


def grad_up_kernel(
    place, lowered, slope, first, w_down, inverse_one, vectors, sum_two, normed, w_up,
    keep, send, bias_out, attended_out, vector_out, sum_out, turned, raised_kept, weights, sems,
):
    width = lowered.shape[1]
    load = copy(w_up, weights, sems.at[0])
    load.start()
    turned[...] = first[...].T

    def work(b):
        here = cut(b, width)
        raised = dot(lowered[...], w_down[here, :], NT) * slope[:, here].astype(f32)
        raised = raised.astype(bf16)
        raised_kept[:, here] = raised
        bias_out[pl.ds(b, 1), :] = column_sum(raised.astype(f32))
        return dot(turned[...], raised).astype(bf16)

    @pl.loop(0, 2)
    def _(x):
        send[x] = work(2 * x + 1 - place[0])
        keep[x] = work(2 * x + place[0])

    load.wait()
    upstream = sum_two[...] + dot(raised_kept[...], weights[...], NT)
    grad_sum = normalize_back(
        upstream * vector(vectors, GAIN_ONE), normed[...], inverse_one[...]
    )
    sum_out[...] = grad_sum
    attended = grad_sum.astype(bf16)
    attended_out[...] = attended
    vector_out[0:1, :] = column_sum(upstream * normed[...])
    vector_out[1:2, :] = column_sum(upstream)
    vector_out[2:3, :] = column_sum(attended.astype(f32))


def grad_up(place, lowered, slope, first, w_down, inverse, vectors, w_up, sum_two, normed):
    count, width = lowered.shape
    hidden = w_down.shape[0]
    return call(
        grad_up_kernel, "grad_up", [place],
        [lowered, slope, first, w_down, inverse, vectors, sum_two, normed],
        [shape(2, width, width)] * 2
        + [shape(hidden // width, width, dtype=f32), shape(count, width)]
        + [shape(8, width, dtype=f32), shape(count, width, dtype=f32)],
        [
            pltpu.VMEM((width, count), bf16), pltpu.VMEM((count, hidden), bf16),
            pltpu.VMEM((width, hidden), bf16),
        ],
        far=[w_up], copies=1, room=28,
    )


def place_rows(place, blocks, rows, sems):
    if len(blocks[2].shape) == 3:
        blocks = (*blocks[:2], blocks[2].at[0], blocks[3].at[1])
    copies = [copy(block, rows.at[place[1] ^ i], sems.at[i]) for i, block in enumerate(blocks)]
    for one in copies:
        one.start()
    return copies


def grad_down_kernel(
    place, active, other_active, lowered, other_lowered, r0, r1, r2, r3, down, rows_out, sems
):
    copies = place_rows(place, (r0, r1, r2, r3), rows_out, sems)
    _, shares, rows, count = active.shape
    width = lowered.shape[1]

    for x in range(2):

        @pl.loop(0, shares, step=2, unroll=shares <= 8)
        def _(d):
            mine = active[x, pl.ds(d, 2)].reshape(2 * rows, count)
            other = other_active[x, pl.ds(d, 2)].reshape(2 * rows, count)
            value = dot(mine, lowered[...]) + dot(other, other_lowered[...])
            down[x, pl.ds(d, 2)] = value.astype(bf16).reshape(2, rows, width)

    for one in copies:
        one.wait()


def grad_down(place, active, other_active, lowered, other_lowered, blocks, after):
    _, shares, rows, _ = active.shape
    slots, width = blocks[0].shape
    return call(
        grad_down_kernel, "grad_down", [place],
        [active, other_active, lowered, other_lowered, *blocks],
        [shape(2, shares, rows, width)], far_outs=[shape(4, slots, width)], copies=4, after=after,
    )


def small_pieces(shares, width):
    q, v, gain_one, shift_one, out, gain_two, shift_two, down, up = range(9)
    share = width // shares

    def flat(row, first):
        return row + first // width, first % width

    def pieces(d):
        at = d * share
        return (
            (flat(q, 2 * at), flat(q, 2 * at + share), (out, at)),
            ((gain_one, at), (shift_one, at), (down, at)),
            ((gain_two, at), (shift_two, at), flat(up, 4 * at)),
            tuple(flat(up, 4 * at + j * share) for j in (1, 2, 3)),
        )

    return [pieces(d) for d in range(shares)]


def attend_back_kernel(
    place, attended, vector_one, vector_two, bias_up, tokens, context, prob, q_ref, k_ref, v_ref, w_out,
    grads_out, keep_0, keep_1, keep_2, send_0, send_1, send_2, small_keep, small_send,
    rows_kept, turned, turned_context, probs_kept, q_kept, k_kept, v_kept, weights, sums, small, sems,
    *, head_width,
):
    count, width = attended.shape
    wide = 4 * head_width
    groups = width // wide
    shares = small.shape[1]
    rows = width // shares
    joined = small_keep is None

    def load(i):
        here = cut(i, wide)
        pairs = [
            (w_out.at[here, :], weights.at[here, :]),
            (v_ref.at[:, here], v_kept.at[:, here]),
            (q_ref.at[:, here], q_kept.at[:, here]),
            (k_ref.at[:, here], k_kept.at[:, here]),
        ]
        pairs = pairs + [(prob.at[4 * i + h], probs_kept.at[4 * i + h]) for h in range(4)]
        return [copy(s, t, sems.at[8 * i + n]) for n, (s, t) in enumerate(pairs)]

    load_tokens = copy(tokens, rows_kept.at[0], sems.at[8 * groups])
    load_context = copy(context, rows_kept.at[1], sems.at[8 * groups + 1])
    for one in load(0):
        one.start()
    load_tokens.start()
    load_context.start()
    head = lax.broadcasted_iota(jnp.int32, (count, wide), 1) // head_width
    none = jnp.zeros((count, wide), bf16)
    odd = place[0] == 1

    @pl.loop(0, groups, unroll=True)
    def _(i):
        here = cut(i, wide)

        @pl.when(i + 1 < groups)
        def _():
            for one in load(i + 1):
                one.start()

        waits = load(i)
        waits[0].wait()
        grad_context = dot(attended[...], weights[here, :], NT).astype(bf16)
        context_turned = grad_context.T
        scaling = jnp.asarray(1.0 / math.sqrt(head_width), bf16)
        for one in waits[1:4]:
            one.wait()
        scaled_q = q_kept[:, here] * scaling
        k_turned = (k_kept[:, here] * scaling).T
        v = v_kept[:, here]

        @pl.when(i == 0)
        def _():
            load_tokens.wait()
            turned[...] = rows_kept[0].T
            load_context.wait()
            turned_context[...] = rows_kept[1].T

        for one in waits[4:]:
            one.wait()
        grad_k = jnp.zeros((count, wide), f32)
        grad_v = grad_k
        grad_q = []
        for h in range(4):
            mine = head == h
            probs = probs_kept[4 * i + h]
            wider = probs.astype(f32)
            lines = slice(h * head_width, (h + 1) * head_width)
            balance = column_sum(
                context_turned[lines, :].astype(f32)
                * turned_context[pl.ds(i * wide + h * head_width, head_width), :].astype(f32)
            )
            weighted = dot(v, only(context_turned, h, head_width)) - balance
            grad_scores = (wider * weighted).astype(bf16)
            grad_v = grad_v + dot(probs, jnp.where(mine, grad_context, none))
            grad_k = grad_k + dot(grad_scores, jnp.where(mine, scaled_q, none))
            grad_q.append(dot(k_turned[h * head_width : (h + 1) * head_width, :], grad_scores))
        grad_q = jnp.concatenate(grad_q).astype(bf16).T
        grad_k = grad_k.astype(bf16)
        grad_v = grad_v.astype(bf16)
        grads_out[:, here] = grad_q
        grads_out[:, cut(i + groups, wide)] = grad_k
        grads_out[:, cut(i + 2 * groups, wide)] = grad_v
        sums[0:1, here] = column_sum(grad_q.astype(f32))
        sums[1:2, here] = column_sum(grad_v.astype(f32))
        pieces = (
            dot(turned[...], grad_q).astype(bf16),
            dot(turned[...], grad_k).astype(bf16),
            dot(turned[...], grad_v).astype(bf16),
            dot(turned_context[...], attended[:, here]).astype(bf16),
        )
        for s, (keep, send) in enumerate(((keep_0, send_0), (keep_1, send_1), (keep_2, send_2))):

            @pl.when(i == s)
            def _(s=s, keep=keep, send=send):
                for x in range(2):
                    kept = jnp.where(odd, pieces[2 * x + 1], pieces[2 * x])
                    sent = jnp.where(odd, pieces[2 * x], pieces[2 * x + 1])
                    if s or not joined:
                        keep[x] = kept
                        send[x] = sent
                    else:
                        for d in range(shares):
                            keep[x, d, 0:rows, :] = kept[d * rows : (d + 1) * rows, :]
                            send[x, d, 0:rows, :] = sent[d * rows : (d + 1) * rows, :]

    sums[2:5, :] = vector_one[0:3, :]
    sums[5:8, :] = vector_two[0:3, :]
    sums[8:12, :] = bias_up[...]
    share = width // shares
    small[...] = jnp.zeros_like(small)
    for d, by_blk in enumerate(small_pieces(shares, width)):
        for b, three in enumerate(by_blk):
            for j, (row, column) in enumerate(three):
                small[b, d, j : j + 1, 0:share] = sums[row : row + 1, column : column + share]
    for x in range(2):
        even_part = small[2 * x].astype(bf16)
        odd_part = small[2 * x + 1].astype(bf16)
        kept = jnp.where(odd, odd_part, even_part)
        sent = jnp.where(odd, even_part, odd_part)
        if joined:
            keep_0[x, :, rows:, :] = kept
            send_0[x, :, rows:, :] = sent
        else:
            small_keep[x] = kept
            small_send[x] = sent


def attend_back(place, attended, small, far, shares, after):
    count, width = attended.shape
    wide = 4 * (width // HEADS)
    groups = width // wide
    rows, turned = pltpu.VMEM((count, width), bf16), pltpu.VMEM((width, count), bf16)
    share = width // shares
    joined = share % 16 == 0
    plain, extra = shape(2, width, wide), [shape(2, shares, 16, wide)] * 2
    first = shape(2, shares, share + 16, wide) if joined else plain
    inner = functools.partial(attend_back_kernel, head_width=width // HEADS)

    def kernel(*refs):
        if joined:
            refs = (*refs[:19], None, None, *refs[19:])
        inner(*refs)

    grads, keep_0, keep_1, keep_2, send_0, send_1, send_2, *small, mark = call(
        kernel, "attend_back", [place], [attended, *small],
        [shape(count, 3 * width)] + [first, plain, plain] * 2 + ([] if joined else extra),
        [
            pltpu.VMEM((2, count, width), bf16), turned, turned,
            pltpu.VMEM((HEADS, count, count), bf16), rows, rows, rows,
            pltpu.VMEM((width, width), bf16),
            pltpu.VMEM((16, width), f32), pltpu.VMEM((4, shares, 16, wide), f32),
        ],
        far=far, copies=8 * groups + 2, room=26, after=after,
    )
    return [keep_0, keep_1, keep_2], [send_0, send_1, send_2], small, grads, mark


def grad_tokens_kernel(grads, w_qkv, sum_one, own, beside, across):
    result = (sum_one[...] + dot(grads[...], w_qkv[...], NT)).astype(bf16)
    slots = own.shape[0]
    for i, block in enumerate((own, beside, across.at[0], across.at[1])):
        block[...] = result[i * slots : (i + 1) * slots, :]


def grad_tokens(sum_one, grads, w_qkv, slots, after):
    count, width = sum_one.shape
    *blocks, mark = call(
        grad_tokens_kernel, "grad_tokens", [], [grads, w_qkv, sum_one],
        [shape(slots, width)] * 2 + [shape(2, slots, width)],
        room=12, after=after,
    )
    return blocks, mark


def swap(block, axis, bit):
    return lax.ppermute(block, axis, [(i, i ^ bit) for i in range(lax.axis_size(axis))])


def pick(block, index, dim=0):
    return lax.dynamic_index_in_dim(block, index, dim, keepdims=False)


def every(count, work):
    if count <= 8:
        for number in range(count):
            work(number)
    else:
        pl.loop(0, count)(work)


def cut_units(bits, units, extra, orders, flip, after):
    parts, dims = len(orders), len(orders[0])
    arrays, numbers = [], {}
    for array in [a for unit in units for terms, _ in unit for a in terms] + list(extra):
        if id(array) not in numbers:
            numbers[id(array)] = len(arrays)
            arrays.append(array)
    rows = [units[0][s][0][0].shape[-2] for s in range(parts)]
    size = sum({id(terms[0]): terms[0].shape[-1] for terms, _ in units[0]}.values()) // parts
    more = [extra[0].shape[-2] if extra and s == 0 else 0 for s in range(parts)]
    outs = [shape(2 ** (dims - 1), len(units) * r + m, size) for r, m in zip(rows, more)]

    def kernel(bits_ref, *refs):
        ins, results = refs[: len(arrays)], refs[len(arrays) :]

        def added(terms, at):
            total = ins[numbers[id(terms[0])]][at]
            for term in terms[1:]:
                total = total + ins[numbers[id(term)]][at]
            return total

        def work(number):
            for s, order in enumerate(orders):
                index = [None] * dims
                index[order[0]] = bits_ref[order[0]] ^ flip
                for i, n in enumerate(order[1:]):
                    index[n] = (number >> (dims - 2 - i)) & 1
                for u, unit in enumerate(units):
                    terms, column = unit[s]
                    at = (*index, slice(None), slice(column * size, (column + 1) * size))
                    results[s][number, u * rows[s] : (u + 1) * rows[s]] = added(terms, at)
                if more[s]:
                    results[s][number, len(units) * rows[s] :] = added(extra, tuple(index))

        every(2 ** (dims - 1), work)

    *made, mark = call(kernel, "cut_units", [bits], arrays, outs, after=after)
    return made, mark


def halve(bits, pairs, axes, join, after=(), place=None, blocks=()):
    taken = pairs[0][0].shape[0] // (2 if axes else 1)
    sizes = [a.shape[1] for a, _ in pairs]
    width = pairs[0][0].shape[2]
    flips = (1, 0) if axes else (0,)
    outs = [shape(taken, sum(sizes), width)] if join else [shape(taken, n, width) for n in sizes]
    outs = outs * len(flips)
    arrays = [a for pair in pairs for a in pair]

    def kernel(*refs):
        copies = []
        if blocks:
            place_ref, *refs, sems = refs
            copies = place_rows(place_ref, refs[1 + len(arrays) : 5 + len(arrays)], refs[-1], sems)
        bits_ref, ins, results = refs[0], refs[1 : 1 + len(arrays)], refs[1 + len(arrays) + len(blocks) :]

        def work(number):
            for f, flip in enumerate(flips):
                for s in range(len(pairs)):
                    at = number + ((bits_ref[axes[s]] ^ flip) * taken if axes else 0)
                    total = ins[2 * s][at] + ins[2 * s + 1][at]
                    if join:
                        first = sum(sizes[:s])
                        results[f][number, first : first + sizes[s]] = total
                    else:
                        results[f * len(pairs) + s][number] = total

        every(taken, work)
        for one in copies:
            one.wait()

    far_outs = [shape(4, *blocks[0].shape)] if blocks else []
    *made, mark = call(
        kernel, "halve", [place, bits] if blocks else [bits], arrays + list(blocks), outs,
        far_outs=far_outs, copies=len(blocks), room=6, after=after,
    )
    made, rows = made[: len(outs)], made[len(outs) :]
    half = len(outs) // len(flips)
    return made[:half], made[half:], mark, *rows


class Group:
    def __init__(self, units, extra, bits, names):
        self.units, self.extra, self.bits, self.names = units, extra, bits, names
        size = len(names)
        turn = [0, size - 1, size - 2]
        rest = list(range(size - 3, 0, -1))
        self.orders = [turn[s:] + turn[:s] + rest for s in range(3)]
        self.stage = 0
        self.pairs = None

    def send(self, blocks):
        return [
            swap(block, *self.names[order[self.stage]]) for block, order in zip(blocks, self.orders)
        ]

    def begin(self, after):
        sent, mark = cut_units(self.bits, self.units, self.extra, self.orders, 1, after)
        self.arrived = self.send(sent)
        return mark

    def rest(self, after):
        keep, mark = cut_units(self.bits, self.units, self.extra, self.orders, 0, after)
        self.pairs = list(zip(keep, self.arrived))
        self.stage = 1
        return mark

    def step(self, after, place=None, blocks=()):
        axes = [order[self.stage] for order in self.orders]
        sent, keep, mark, *rows = halve(
            self.bits, self.pairs, axes, self.stage == 3, after, place, blocks
        )
        self.pairs = list(zip(keep, self.send(sent)))
        self.stage += 1
        return (mark, *rows) if rows else mark

    def finish(self, after, place=None, blocks=()):
        (own,), _, mark, *rows = halve(self.bits, self.pairs, None, False, after, place, blocks)
        across = swap(own, "blk", 2)
        return (own, swap(own, "blk", 1), across, swap(across, "blk", 1)), mark, *rows


def chosen(place, b, refs):
    relative = place[1] ^ b
    values = [ref[...] for ref in refs]
    return jnp.where(
        relative < 2,
        jnp.where(relative == 0, values[0], values[1]),
        jnp.where(relative == 2, values[2], values[3]),
    ).astype(f32)


def place_all(place, feed_pieces, own_pieces, rows, shares, blocks, after):
    size = own_pieces[0].shape[2]
    width = 3 * size
    share = width // shares
    extra = own_pieces[0].shape[1] - 3 * rows
    count = 8 + len(blocks)

    def kernel(place_ref, *refs):
        feed_refs, own_refs = refs[:4], refs[4:8]
        down, up, qkv, out, bias_qv, bias_out, gain_one, shift_one, bias_up, bias_down, gain_two, shift_two = (
            refs[count : count + 12]
        )
        copies = place_rows(place_ref, refs[8:12], refs[count + 12], refs[-1]) if blocks else []
        for b in range(4):
            for s in range(3):
                columns = slice(s * size, (s + 1) * size)
                wider = slice(b * width + s * size, b * width + (s + 1) * size)
                at = 2 * s * rows
                value = chosen(place_ref, b, [p.at[0, at : at + rows] for p in feed_refs])
                down[b * rows : (b + 1) * rows, columns] = value
                at = at + rows
                up[:, wider] = chosen(place_ref, b, [p.at[0, at : at + rows] for p in feed_refs])
                at = s * rows + (extra if s else 0)
                value = chosen(place_ref, b, [p.at[0, at : at + rows] for p in own_refs])
                if b == 3:
                    out[:, columns] = value
                else:
                    qkv[:, wider] = value
            value = chosen(place_ref, b, [p.at[0, rows : rows + extra] for p in own_refs])
            targets = (
                ((bias_qv, 0), (bias_qv, 1), (bias_out, 0)),
                ((gain_one, 0), (shift_one, 0), (bias_down, 0)),
                ((gain_two, 0), (shift_two, 0), (bias_up, 0)),
                ((bias_up, 1), (bias_up, 2), (bias_up, 3)),
            )[b]
            for j, (ref, part) in enumerate(targets):
                ref[part * share : (part + 1) * share] = value[j, 0:share]
        for one in copies:
            one.wait()

    vectors = [shape(n * share, dtype=f32) for n in (2, 1, 1, 1, 4, 1, 1, 1)]
    return call(
        kernel, "place_all", [place], [*feed_pieces, *own_pieces, *blocks],
        [
            shape(4 * rows, width, dtype=f32), shape(rows, 4 * width, dtype=f32),
            shape(rows, 3 * width, dtype=f32), shape(rows, width, dtype=f32), *vectors,
        ],
        far_outs=[shape(4, *blocks[0].shape)] if blocks else [], copies=len(blocks), room=16, after=after,
    )[:-1]


def shards(
    tokens, lengths, w_qkv, bias_qv, w_out, bias_out, norm1_gain, norm1_bias, w_up, bias_up,
    w_down, bias_down, norm2_gain, norm2_bias, cotangent,
):
    rows, slots, width = tokens.shape
    shares = lax.axis_size("dp")
    dp_bits = shares.bit_length() - 1
    position = lax.axis_index("blk").astype(jnp.int32)
    group = lax.axis_index("dp").astype(jnp.int32)
    place = jnp.stack([position % 2, position])
    names = [("blk", 2)] + [("dp", 1 << i) for i in reversed(range(dp_bits))]
    bits = jnp.stack([position // 2] + [(group >> i) % 2 for i in reversed(range(dp_bits))])

    def gather_row(array):
        return [pick(array, position)] + [
            swap(pick(array, position ^ i), "blk", i) for i in (2, 3, 1)
        ]

    def in_order(blocks):
        return [blocks[0], blocks[3], blocks[1], blocks[2]]

    def scatter_pairs(blocks):
        own, beside, pair = blocks
        arrived = swap(pair, "blk", 2)
        return [own, swap(beside, "blk", 1), arrived, swap(arrived, "blk", 1)]

    def scatter_row(blocks):
        return [blocks[0]] + [swap(blocks[i], "blk", i) for i in range(1, rows)]

    biases = [
        bias_qv, bias_out, norm1_gain, norm1_bias, bias_down, norm2_gain, norm2_bias, bias_up
    ]
    row = jnp.concatenate([pick(lengths, position), position[None]])
    blocks = in_order(gather_row(tokens))
    qkv_near, out_near, mask, vectors, mark = prepare(
        row, biases, w_qkv, w_out, slots, rows * slots
    )
    cotangent, _ = lax.optimization_barrier((cotangent, blocks[1]))
    cotangents = in_order(gather_row(cotangent))
    normed, inverse, q, k, v, prob, context, row_tokens = attend(
        blocks, vectors, qkv_near, out_near, mask
    )
    keep_active, send_active, slope, lowered, first, o0, o1, o2, o3, vector_two, sum_two = feed(
        place, normed, vectors, cotangents, w_up, w_down, shares
    )
    got_active, got_lowered = swap(send_active, "blk", 1), swap(lowered, "blk", 1)
    keep_up, send_up, grad_bias_up, attended, vector_one, sum_one, mark = grad_up(
        place, lowered, slope, first, w_down, inverse, vectors, w_up, sum_two, normed
    )
    got_up = swap(send_up, "blk", 1)
    down, outputs, mark = grad_down(
        place, keep_active, got_active, lowered, got_lowered, scatter_row([o0, o1, o2, o3]), [mark]
    )

    def chunks(array):
        return array.reshape((2,) * (1 + dp_bits) + (-1, array.shape[-1]))

    down, keep_up, got_up = chunks(down), chunks(keep_up), chunks(got_up)
    feed_group = Group(
        [[([down], s) for s in range(3)], [([keep_up, got_up], s) for s in range(3)]],
        (), bits, names,
    )
    mark = feed_group.begin([mark])
    keeps, sends, small, grads, mark = attend_back(
        place, attended, [vector_one, vector_two, grad_bias_up],
        [row_tokens, context, prob, q, k, v, w_out], shares, [mark],
    )
    gots = [swap(send, "blk", 1) for send in sends]
    small = [chunks(small[0]), chunks(swap(small[1], "blk", 1))] if small else ()
    own_group = Group(
        [[([chunks(keep), chunks(got)], 0) for keep, got in zip(keeps, gots)]], small, bits, names
    )
    share = width // shares
    mark = feed_group.rest([mark])
    mark = feed_group.step([mark])
    mark = own_group.begin([mark])
    tokens_parts, mark = grad_tokens(sum_one, grads, w_qkv, slots, [mark])
    mark = own_group.rest([mark])
    for _ in range(dp_bits - 3):
        mark = feed_group.step([mark])
        mark = own_group.step([mark])
    mark = feed_group.step([mark])
    mark = own_group.step([mark])
    mark = feed_group.step([mark])
    mark = own_group.step([mark])
    feed_pieces, mark = feed_group.finish([mark])
    mark = own_group.step([mark])
    own_pieces, mark = own_group.finish([mark])
    (
        down, up, grad_w_qkv, grad_w_out, sum_qv, sum_out, sum_gain_one, sum_shift_one, sum_up, sum_down,
        sum_gain_two, sum_shift_two, token_grads,
    ) = place_all(place, feed_pieces, own_pieces, share, shares, scatter_pairs(tokens_parts), [mark])
    return (
        outputs,
        token_grads,
        grad_w_qkv,
        sum_qv,
        grad_w_out,
        sum_out,
        sum_gain_one,
        sum_shift_one,
        up,
        sum_up,
        down,
        sum_down,
        sum_gain_two,
        sum_shift_two,
    )


def solution(mesh):
    row_spec = P("dp", "blk", None)
    in_specs = (row_spec, P("dp", None)) + (P(),) * 12 + (row_spec,)
    wide, flat = P("dp", None), P("dp")
    out_specs = (
        row_spec, row_spec, wide, flat, wide, flat, flat, flat, wide, flat, wide, flat, flat, flat,
    )
    return jax.shard_map(shards, mesh=mesh, in_specs=in_specs, out_specs=out_specs, check_vma=False)
```

```python
import functools
import math

import jax
import jax.numpy as jnp
from jax import lax
from jax.experimental import pallas as pl
from jax.experimental.pallas import tpu as pltpu
from jax.sharding import PartitionSpec as P

HEADS = 12
EPSILON = 1e-12
MASKED = -1e30
f32 = jnp.float32
bf16 = jnp.bfloat16
NN = (((1,), (0,)), ((), ()))
NT = (((1,), (1,)), ((), ()))
TN = (((0,), (0,)), ((), ()))
VMEM = pl.BlockSpec(memory_space=pltpu.VMEM)
SMEM = pl.BlockSpec(memory_space=pltpu.SMEM)
HBM = pl.BlockSpec(memory_space=pltpu.HBM)
ANY = pl.BlockSpec(memory_space=pl.ANY)


WEIGHTS = {
    "prepare": 60 * 10**9, "attend": 60 * 10**9, "feed": 60 * 10**9, "grad_up": 60 * 10**9,
    "grad_down": 60 * 10**9, "attend_back": 60 * 10**9, "grad_tokens": 60 * 10**8,
    "halve": 150 * 10**7, "cut_units": 150 * 10**7, "place_all": 150 * 10**7,
}


def dot(left, right, dims=NN):
    return lax.dot_general(left, right, dims, preferred_element_type=f32)


def call(
    kernel, name, scalars, arrays, outs, scratch=(), far=(), far_outs=(), copies=0, room=10, after=()
):
    scratch = list(scratch)
    if copies:
        scratch.append(pltpu.SemaphoreType.DMA((copies,)))
    first, last = len(scalars) + len(arrays) + len(far), len(after)
    results = len(outs) + len(far_outs)
    mark = jax.ShapeDtypeStruct((8, 128), f32)

    def body(*refs):
        mine = refs[first + last :]
        mine[results][...] = jnp.zeros(mark.shape, mark.dtype)
        kernel(*refs[:first], *mine[:results], *mine[results + 1 :])

    return pl.pallas_call(
        body,
        in_specs=[SMEM] * len(scalars) + [VMEM] * len(arrays) + [HBM] * len(far) + [VMEM] * last,
        out_specs=[VMEM] * len(outs) + [HBM] * len(far_outs) + [VMEM],
        out_shape=[*outs, *[pltpu.HBM(a.shape, a.dtype) for a in far_outs], mark],
        scratch_shapes=scratch,
        compiler_params=pltpu.CompilerParams(vmem_limit_bytes=room * 2**20),
        cost_estimate=pl.CostEstimate(
            flops=WEIGHTS.get(name, 0), bytes_accessed=0, transcendentals=0
        ),
        name=name,
    )(
        *scalars, *arrays, *[pltpu.with_memory_space_constraint(a, pltpu.HBM) for a in far], *after
    )


def shape(*dims, dtype=bf16):
    return jax.ShapeDtypeStruct(dims, dtype)


def cut(i, size):
    return pl.ds(pl.multiple_of(i * size, size), size)


def copy(source, target, semaphore):
    return pltpu.make_async_copy(source, target, semaphore)


def column_sum(values):
    return jnp.sum(values, axis=0, keepdims=True)


def row_mean(values):
    return jnp.mean(values, axis=-1, keepdims=True)


def normalize(inputs):
    centre = inputs - row_mean(inputs)
    inverse = lax.rsqrt(row_mean(centre * centre) + EPSILON)
    return centre * inverse, inverse


def normalize_back(scaled, normed, inverse):
    return inverse * (scaled - row_mean(scaled) - normed * row_mean(scaled * normed))


BIAS_Q, BIAS_V, BIAS_OUT, GAIN_ONE, SHIFT_ONE, BIAS_DOWN, GAIN_TWO, SHIFT_TWO, BIAS_UP = range(9)


def vector(ref, row):
    return ref[row : row + 1, :]


def only(rows, h, height):
    parts = [jnp.zeros((height, rows.shape[1]), rows.dtype)] * (rows.shape[0] // height)
    parts[h] = rows[h * height : (h + 1) * height, :]
    return jnp.concatenate(parts)


def prepare_kernel(
    row_ref, w_qkv, w_out, b0, b1, b2, b3, b4, b5, b6, b7,
    qkv_near, out_near, mask, vectors, s0, s1, s2, s3, s4, s5, s6, s7, sems, *, pages, slots,
):
    pairs = zip((b0, b1, b2, b3, b4, b5, b6, b7), (s0, s1, s2, s3, s4, s5, s6, s7))
    loads = [copy(a, b, sems.at[2 + i]) for i, (a, b) in enumerate(pairs)]
    for one in loads:
        one.start()
    load_qkv = copy(w_qkv, qkv_near, sems.at[0])
    load_qkv.start()
    load_out = copy(w_out, out_near, sems.at[1])
    load_out.start()
    count = mask.shape[0]
    position = row_ref[pages]

    def page_of(shape, dim):
        at = lax.broadcasted_iota(jnp.int32, shape, dim)
        slot = ((at // slots) ^ position) * slots + at % slots
        page = jnp.zeros(shape, jnp.int32)
        end = 0
        for c in range(pages):
            end = end + row_ref[c]
            page = page + (slot >= end).astype(jnp.int32)
        return page

    mask[...] = jnp.where(
        page_of((count, count), 0) == page_of((1, count), 1), 0.0, MASKED
    )
    for one in loads:
        one.wait()
    width = vectors.shape[1]
    row = 0
    for part in (s0, s1, s2, s3, s4, s5, s6, s7):
        for i in range(part.shape[0] // width):
            vectors[row : row + 1, :] = part[i * width : (i + 1) * width].reshape(1, width)
            row += 1
    load_qkv.wait()
    load_out.wait()


def prepare(row, biases, w_qkv, w_out, slots, count):
    width = w_out.shape[0]
    rows = sum(b.shape[0] for b in biases) // width
    return call(
        functools.partial(prepare_kernel, pages=row.shape[0] - 1, slots=slots),
        "prepare", [row], [],
        [
            shape(*w_qkv.shape), shape(*w_out.shape), shape(count, count, dtype=f32),
            shape(rows, width, dtype=f32),
        ],
        [pltpu.VMEM(b.shape, f32) for b in biases],
        far=[w_qkv, w_out, *biases], copies=2 + len(biases),
    )


def attend_kernel(
    x0, x1, x2, x3, vectors, w_qkv, w_out, mask,
    normed_out, inverse_out, q_out, k_out, v_out, prob_out, context_out, tokens_out,
    tokens, q_kept, k_kept, v_kept, context_kept, probs_kept, sems, *, head_width,
):
    slots = x0.shape[0]
    count, width = tokens.shape
    wide = 4 * head_width
    groups = width // wide
    kept = ((0, q_kept, q_out), (1, k_kept, k_out), (2, v_kept, v_out), (3, context_kept, context_out))

    def keep(i, number, source, target):
        here = cut(i, wide)
        return copy(source.at[:, here], target.at[:, here], sems.at[number * groups + i])

    def keep_probs(i, h):
        return copy(
            probs_kept.at[4 * i + h], prob_out.at[4 * i + h], sems.at[4 * groups + 1 + 4 * i + h]
        )

    for i, block in enumerate((x0, x1, x2, x3)):
        tokens[i * slots : (i + 1) * slots, :] = block[...]
    keep_tokens = copy(tokens, tokens_out, sems.at[4 * groups])
    keep_tokens.start()

    @pl.loop(0, groups)
    def _(i):
        here = cut(i, wide)
        x = tokens[...]
        q = (dot(x, w_qkv[:, here]) + vectors[BIAS_Q : BIAS_Q + 1, here]).astype(bf16)
        k = dot(x, w_qkv[:, cut(i + groups, wide)]).astype(bf16)
        v = dot(x, w_qkv[:, cut(i + 2 * groups, wide)]) + vectors[BIAS_V : BIAS_V + 1, here]
        v = v.astype(bf16)
        q_kept[:, here] = q
        k_kept[:, here] = k
        v_kept[:, here] = v
        q_turned = (q * jnp.asarray(1.0 / math.sqrt(head_width), bf16)).T
        v_turned = v.T
        context = []
        for h in range(4):
            scores = dot(k, only(q_turned, h, head_width)) + mask[...]
            powers = jnp.exp(scores - jnp.max(scores, axis=0, keepdims=True))
            probs = (powers * (1.0 / jnp.sum(powers, axis=0, keepdims=True))).astype(bf16)
            probs_kept[4 * i + h] = probs
            keep_probs(i, h).start()
            context.append(dot(v_turned[h * head_width : (h + 1) * head_width, :], probs))
        context_kept[:, here] = jnp.concatenate(context).astype(bf16).T
        for number, source, target in kept:
            keep(i, number, source, target).start()

    attended = dot(context_kept[...], w_out[...]) + vector(vectors, BIAS_OUT)
    normed, inverse = normalize(tokens[...].astype(f32) + attended)
    normed_out[...] = normed
    inverse_out[...] = inverse
    for i in range(groups):
        for number, source, target in kept:
            keep(i, number, source, target).wait()
        for h in range(4):
            keep_probs(i, h).wait()
    keep_tokens.wait()


def attend(blocks, vectors, w_qkv, w_out, mask):
    slots, width = blocks[0].shape
    count = slots * len(blocks)
    groups = HEADS // 4
    narrow = shape(count, width)
    rows = pltpu.VMEM((count, width), bf16)
    return call(
        functools.partial(attend_kernel, head_width=width // HEADS),
        "attend", [], [*blocks, vectors, w_qkv, w_out, mask],
        [shape(count, width, dtype=f32), shape(count, 1, dtype=f32)],
        [rows, rows, rows, rows, rows, pltpu.VMEM((HEADS, count, count), bf16)],
        far_outs=[narrow, narrow, narrow, shape(HEADS, count, count), narrow, narrow],
        copies=4 * groups + 1 + HEADS, room=24,
    )[:8]


def feed_kernel(
    place, normed_one, vectors, c0, c1, c2, c3, w_up, w_down,
    keep_active, send_active, slope_out, lowered_out, first_out, r0, r1, r2, r3, vector_out,
    sum_out, total, *, shares,
):
    width = w_up.shape[0]
    hidden = w_up.shape[1]
    first_norm = normed_one[...] * vector(vectors, GAIN_ONE) + vector(vectors, SHIFT_ONE)
    first_out[...] = first_norm.astype(bf16)
    total[...] = first_norm + vector(vectors, BIAS_DOWN)
    odd = place[0] == 1
    rows = hidden // shares // 4
    apart = send_active is not None

    @pl.loop(0, hidden // width, unroll=True)
    def _(i):
        here = cut(i, width)
        raised = dot(first_out[...], w_up[:, here]) + vectors[pl.ds(BIAS_UP + i, 1), :]
        cumulative = 0.5 * (1.0 + lax.erf(raised * (1.0 / math.sqrt(2.0))))
        activated = (raised * cumulative).astype(bf16)
        bell = jnp.exp(-0.5 * raised * raised) * (1.0 / math.sqrt(2.0 * math.pi))
        slope_out[:, here] = (cumulative + raised * bell).astype(bf16)
        total[...] += dot(activated, w_down[here, :])
        turned = activated.T
        if apart:
            count = width // rows // 4
            for d in range(count):
                for x in range(2):
                    at = (d * 4 + x * 2) * rows
                    even_part = turned[at : at + rows, :]
                    odd_part = turned[at + rows : at + 2 * rows, :]
                    keep_active[x, i * count + d] = jnp.where(odd, odd_part, even_part)
                    send_active[x, i * count + d] = jnp.where(odd, even_part, odd_part)
        else:
            keep_active[here, :] = turned

    normed, inverse = normalize(total[...])
    gain = vector(vectors, GAIN_TWO)
    result = (normed * gain + vector(vectors, SHIFT_TWO)).astype(bf16)
    slots = c0.shape[0]
    for i, block in enumerate((r0, r1, r2, r3)):
        block[...] = result[i * slots : (i + 1) * slots, :]
    upstream = jnp.concatenate([c0[...], c1[...], c2[...], c3[...]]).astype(f32)
    grad_sum = normalize_back(upstream * gain, normed, inverse)
    sum_out[...] = grad_sum
    lowered = grad_sum.astype(bf16)
    lowered_out[...] = lowered
    vector_out[0:1, :] = column_sum(upstream * normed)
    vector_out[1:2, :] = column_sum(upstream)
    vector_out[2:3, :] = column_sum(lowered.astype(f32))


def feed(place, normed, vectors, cotangents, w_up, w_down, shares):
    count, width = normed.shape
    hidden = w_up.shape[1]
    rows = hidden // shares // 4
    narrow, full = shape(count, width), shape(count, width, dtype=f32)
    apart = rows % 16 == 0 and width % (4 * rows) == 0
    kernel = functools.partial(feed_kernel, shares=shares)
    if apart:
        active = [shape(2, shares, rows, count)] * 2
    else:
        active = [shape(hidden, count)]
        whole = kernel

        def kernel(*refs):
            whole(*refs[:10], None, *refs[10:])

    made = call(
        kernel, "feed", [place], [normed, vectors, *cotangents, w_up, w_down],
        active + [shape(count, hidden), narrow, narrow]
        + [shape(*cotangents[0].shape)] * 4 + [shape(8, width, dtype=f32), full],
        [pltpu.VMEM((count, width), f32)], room=14,
    )[:-1]
    if apart:
        return made
    parts = jnp.moveaxis(made[0].reshape(shares, 2, 2, rows, count), 0, 2)
    odd = place[0] == 1
    keep = jnp.where(odd, parts[:, 1], parts[:, 0])
    send = jnp.where(odd, parts[:, 0], parts[:, 1])
    return [keep, send, *made[1:]]


def grad_up_kernel(
    place, lowered, slope, first, w_down, inverse_one, vectors, sum_two, normed, w_up,
    keep, send, bias_out, attended_out, vector_out, sum_out, turned, raised_kept, weights, sems,
):
    width = lowered.shape[1]
    load = copy(w_up, weights, sems.at[0])
    load.start()
    turned[...] = first[...].T

    def work(b):
        here = cut(b, width)
        raised = dot(lowered[...], w_down[here, :], NT) * slope[:, here].astype(f32)
        raised = raised.astype(bf16)
        raised_kept[:, here] = raised
        bias_out[pl.ds(b, 1), :] = column_sum(raised.astype(f32))
        return dot(turned[...], raised).astype(bf16)

    @pl.loop(0, 2)
    def _(x):
        send[x] = work(2 * x + 1 - place[0])
        keep[x] = work(2 * x + place[0])

    load.wait()
    upstream = sum_two[...] + dot(raised_kept[...], weights[...], NT)
    grad_sum = normalize_back(
        upstream * vector(vectors, GAIN_ONE), normed[...], inverse_one[...]
    )
    sum_out[...] = grad_sum
    attended = grad_sum.astype(bf16)
    attended_out[...] = attended
    vector_out[0:1, :] = column_sum(upstream * normed[...])
    vector_out[1:2, :] = column_sum(upstream)
    vector_out[2:3, :] = column_sum(attended.astype(f32))


def grad_up(place, lowered, slope, first, w_down, inverse, vectors, w_up, sum_two, normed):
    count, width = lowered.shape
    hidden = w_down.shape[0]
    return call(
        grad_up_kernel, "grad_up", [place],
        [lowered, slope, first, w_down, inverse, vectors, sum_two, normed],
        [shape(2, width, width)] * 2
        + [shape(hidden // width, width, dtype=f32), shape(count, width)]
        + [shape(8, width, dtype=f32), shape(count, width, dtype=f32)],
        [
            pltpu.VMEM((width, count), bf16), pltpu.VMEM((count, hidden), bf16),
            pltpu.VMEM((width, hidden), bf16),
        ],
        far=[w_up], copies=1, room=28,
    )


def place_rows(place, blocks, rows, sems):
    if len(blocks[2].shape) == 3:
        blocks = (*blocks[:2], blocks[2].at[0], blocks[3].at[1])
    copies = [copy(block, rows.at[place[1] ^ i], sems.at[i]) for i, block in enumerate(blocks)]
    for one in copies:
        one.start()
    return copies


def grad_down_kernel(
    place, active, other_active, lowered, other_lowered, r0, r1, r2, r3, down, rows_out, sems
):
    copies = place_rows(place, (r0, r1, r2, r3), rows_out, sems)
    _, shares, rows, count = active.shape
    width = lowered.shape[1]

    for x in range(2):

        @pl.loop(0, shares, step=2, unroll=shares <= 8)
        def _(d):
            mine = active[x, pl.ds(d, 2)].reshape(2 * rows, count)
            other = other_active[x, pl.ds(d, 2)].reshape(2 * rows, count)
            value = dot(mine, lowered[...]) + dot(other, other_lowered[...])
            down[x, pl.ds(d, 2)] = value.astype(bf16).reshape(2, rows, width)

    for one in copies:
        one.wait()


def grad_down(place, active, other_active, lowered, other_lowered, blocks, after):
    _, shares, rows, _ = active.shape
    slots, width = blocks[0].shape
    return call(
        grad_down_kernel, "grad_down", [place],
        [active, other_active, lowered, other_lowered, *blocks],
        [shape(2, shares, rows, width)], far_outs=[shape(4, slots, width)], copies=4, after=after,
    )


def small_pieces(shares, width):
    q, v, gain_one, shift_one, out, gain_two, shift_two, down, up = range(9)
    share = width // shares

    def flat(row, first):
        return row + first // width, first % width

    def pieces(d):
        at = d * share
        return (
            (flat(q, 2 * at), flat(q, 2 * at + share), (out, at)),
            ((gain_one, at), (shift_one, at), (down, at)),
            ((gain_two, at), (shift_two, at), flat(up, 4 * at)),
            tuple(flat(up, 4 * at + j * share) for j in (1, 2, 3)),
        )

    return [pieces(d) for d in range(shares)]


def attend_back_kernel(
    place, attended, vector_one, vector_two, bias_up, tokens, context, prob, q_ref, k_ref, v_ref, w_out,
    grads_out, keep_0, keep_1, keep_2, send_0, send_1, send_2, small_keep, small_send,
    rows_kept, turned, turned_context, probs_kept, q_kept, k_kept, v_kept, weights, sums, small, sems,
    *, head_width,
):
    count, width = attended.shape
    wide = 4 * head_width
    groups = width // wide
    shares = small.shape[1]
    rows = width // shares
    joined = small_keep is None

    def load(i):
        here = cut(i, wide)
        pairs = [
            (w_out.at[here, :], weights.at[here, :]),
            (v_ref.at[:, here], v_kept.at[:, here]),
            (q_ref.at[:, here], q_kept.at[:, here]),
            (k_ref.at[:, here], k_kept.at[:, here]),
        ]
        pairs = pairs + [(prob.at[4 * i + h], probs_kept.at[4 * i + h]) for h in range(4)]
        return [copy(s, t, sems.at[8 * i + n]) for n, (s, t) in enumerate(pairs)]

    load_tokens = copy(tokens, rows_kept.at[0], sems.at[8 * groups])
    load_context = copy(context, rows_kept.at[1], sems.at[8 * groups + 1])
    for one in load(0):
        one.start()
    load_tokens.start()
    load_context.start()
    head = lax.broadcasted_iota(jnp.int32, (count, wide), 1) // head_width
    none = jnp.zeros((count, wide), bf16)
    odd = place[0] == 1

    @pl.loop(0, groups, unroll=True)
    def _(i):
        here = cut(i, wide)

        @pl.when(i + 1 < groups)
        def _():
            for one in load(i + 1):
                one.start()

        waits = load(i)
        waits[0].wait()
        grad_context = dot(attended[...], weights[here, :], NT).astype(bf16)
        context_turned = grad_context.T
        scaling = jnp.asarray(1.0 / math.sqrt(head_width), bf16)
        for one in waits[1:4]:
            one.wait()
        scaled_q = q_kept[:, here] * scaling
        k_turned = (k_kept[:, here] * scaling).T
        v = v_kept[:, here]

        @pl.when(i == 0)
        def _():
            load_tokens.wait()
            turned[...] = rows_kept[0].T
            load_context.wait()
            turned_context[...] = rows_kept[1].T

        for one in waits[4:]:
            one.wait()
        grad_k = jnp.zeros((count, wide), f32)
        grad_v = grad_k
        grad_q = []
        for h in range(4):
            mine = head == h
            probs = probs_kept[4 * i + h]
            wider = probs.astype(f32)
            lines = slice(h * head_width, (h + 1) * head_width)
            balance = column_sum(
                context_turned[lines, :].astype(f32)
                * turned_context[pl.ds(i * wide + h * head_width, head_width), :].astype(f32)
            )
            weighted = dot(v, only(context_turned, h, head_width)) - balance
            grad_scores = (wider * weighted).astype(bf16)
            grad_v = grad_v + dot(probs, jnp.where(mine, grad_context, none))
            grad_k = grad_k + dot(grad_scores, jnp.where(mine, scaled_q, none))
            grad_q.append(dot(k_turned[h * head_width : (h + 1) * head_width, :], grad_scores))
        grad_q = jnp.concatenate(grad_q).astype(bf16).T
        grad_k = grad_k.astype(bf16)
        grad_v = grad_v.astype(bf16)
        grads_out[:, here] = grad_q
        grads_out[:, cut(i + groups, wide)] = grad_k
        grads_out[:, cut(i + 2 * groups, wide)] = grad_v
        sums[0:1, here] = column_sum(grad_q.astype(f32))
        sums[1:2, here] = column_sum(grad_v.astype(f32))
        pieces = (
            dot(turned[...], grad_q).astype(bf16),
            dot(turned[...], grad_k).astype(bf16),
            dot(turned[...], grad_v).astype(bf16),
            dot(turned_context[...], attended[:, here]).astype(bf16),
        )
        for s, (keep, send) in enumerate(((keep_0, send_0), (keep_1, send_1), (keep_2, send_2))):

            @pl.when(i == s)
            def _(s=s, keep=keep, send=send):
                for x in range(2):
                    kept = jnp.where(odd, pieces[2 * x + 1], pieces[2 * x])
                    sent = jnp.where(odd, pieces[2 * x], pieces[2 * x + 1])
                    if s or not joined:
                        keep[x] = kept
                        send[x] = sent
                    else:
                        for d in range(shares):
                            keep[x, d, 0:rows, :] = kept[d * rows : (d + 1) * rows, :]
                            send[x, d, 0:rows, :] = sent[d * rows : (d + 1) * rows, :]

    sums[2:5, :] = vector_one[0:3, :]
    sums[5:8, :] = vector_two[0:3, :]
    sums[8:12, :] = bias_up[...]
    share = width // shares
    small[...] = jnp.zeros_like(small)
    for d, by_blk in enumerate(small_pieces(shares, width)):
        for b, three in enumerate(by_blk):
            for j, (row, column) in enumerate(three):
                small[b, d, j : j + 1, 0:share] = sums[row : row + 1, column : column + share]
    for x in range(2):
        even_part = small[2 * x].astype(bf16)
        odd_part = small[2 * x + 1].astype(bf16)
        kept = jnp.where(odd, odd_part, even_part)
        sent = jnp.where(odd, even_part, odd_part)
        if joined:
            keep_0[x, :, rows:, :] = kept
            send_0[x, :, rows:, :] = sent
        else:
            small_keep[x] = kept
            small_send[x] = sent


def attend_back(place, attended, small, far, shares, after):
    count, width = attended.shape
    wide = 4 * (width // HEADS)
    groups = width // wide
    rows, turned = pltpu.VMEM((count, width), bf16), pltpu.VMEM((width, count), bf16)
    share = width // shares
    joined = share % 16 == 0
    plain, extra = shape(2, width, wide), [shape(2, shares, 16, wide)] * 2
    first = shape(2, shares, share + 16, wide) if joined else plain
    inner = functools.partial(attend_back_kernel, head_width=width // HEADS)

    def kernel(*refs):
        if joined:
            refs = (*refs[:19], None, None, *refs[19:])
        inner(*refs)

    grads, keep_0, keep_1, keep_2, send_0, send_1, send_2, *small, mark = call(
        kernel, "attend_back", [place], [attended, *small],
        [shape(count, 3 * width)] + [first, plain, plain] * 2 + ([] if joined else extra),
        [
            pltpu.VMEM((2, count, width), bf16), turned, turned,
            pltpu.VMEM((HEADS, count, count), bf16), rows, rows, rows,
            pltpu.VMEM((width, width), bf16),
            pltpu.VMEM((16, width), f32), pltpu.VMEM((4, shares, 16, wide), f32),
        ],
        far=far, copies=8 * groups + 2, room=26, after=after,
    )
    return [keep_0, keep_1, keep_2], [send_0, send_1, send_2], small, grads, mark


def grad_tokens_kernel(grads, w_qkv, sum_one, own, beside, across):
    result = (sum_one[...] + dot(grads[...], w_qkv[...], NT)).astype(bf16)
    slots = own.shape[0]
    for i, block in enumerate((own, beside, across.at[0], across.at[1])):
        block[...] = result[i * slots : (i + 1) * slots, :]


def grad_tokens(sum_one, grads, w_qkv, slots, after):
    count, width = sum_one.shape
    *blocks, mark = call(
        grad_tokens_kernel, "grad_tokens", [], [grads, w_qkv, sum_one],
        [shape(slots, width)] * 2 + [shape(2, slots, width)],
        room=12, after=after,
    )
    return blocks, mark


def swap(block, axis, bit):
    return lax.ppermute(block, axis, [(i, i ^ bit) for i in range(lax.axis_size(axis))])


def pick(block, index, dim=0):
    return lax.dynamic_index_in_dim(block, index, dim, keepdims=False)


def every(count, work):
    if count <= 8:
        for number in range(count):
            work(number)
    else:
        pl.loop(0, count)(work)


def cut_units(bits, units, extra, orders, flip, after):
    parts, dims = len(orders), len(orders[0])
    arrays, numbers = [], {}
    for array in [a for unit in units for terms, _ in unit for a in terms] + list(extra):
        if id(array) not in numbers:
            numbers[id(array)] = len(arrays)
            arrays.append(array)
    rows = [units[0][s][0][0].shape[-2] for s in range(parts)]
    size = sum({id(terms[0]): terms[0].shape[-1] for terms, _ in units[0]}.values()) // parts
    more = [extra[0].shape[-2] if extra and s == 0 else 0 for s in range(parts)]
    outs = [shape(2 ** (dims - 1), len(units) * r + m, size) for r, m in zip(rows, more)]

    def kernel(bits_ref, *refs):
        ins, results = refs[: len(arrays)], refs[len(arrays) :]

        def added(terms, at):
            total = ins[numbers[id(terms[0])]][at]
            for term in terms[1:]:
                total = total + ins[numbers[id(term)]][at]
            return total

        def work(number):
            for s, order in enumerate(orders):
                index = [None] * dims
                index[order[0]] = bits_ref[order[0]] ^ flip
                for i, n in enumerate(order[1:]):
                    index[n] = (number >> (dims - 2 - i)) & 1
                for u, unit in enumerate(units):
                    terms, column = unit[s]
                    at = (*index, slice(None), slice(column * size, (column + 1) * size))
                    results[s][number, u * rows[s] : (u + 1) * rows[s]] = added(terms, at)
                if more[s]:
                    results[s][number, len(units) * rows[s] :] = added(extra, tuple(index))

        every(2 ** (dims - 1), work)

    *made, mark = call(kernel, "cut_units", [bits], arrays, outs, after=after)
    return made, mark


def halve(bits, pairs, axes, join, after=(), place=None, blocks=()):
    taken = pairs[0][0].shape[0] // (2 if axes else 1)
    sizes = [a.shape[1] for a, _ in pairs]
    width = pairs[0][0].shape[2]
    flips = (1, 0) if axes else (0,)
    outs = [shape(taken, sum(sizes), width)] if join else [shape(taken, n, width) for n in sizes]
    outs = outs * len(flips)
    arrays = [a for pair in pairs for a in pair]

    def kernel(*refs):
        copies = []
        if blocks:
            place_ref, *refs, sems = refs
            copies = place_rows(place_ref, refs[1 + len(arrays) : 5 + len(arrays)], refs[-1], sems)
        bits_ref, ins, results = refs[0], refs[1 : 1 + len(arrays)], refs[1 + len(arrays) + len(blocks) :]

        def work(number):
            for f, flip in enumerate(flips):
                for s in range(len(pairs)):
                    at = number + ((bits_ref[axes[s]] ^ flip) * taken if axes else 0)
                    total = ins[2 * s][at] + ins[2 * s + 1][at]
                    if join:
                        first = sum(sizes[:s])
                        results[f][number, first : first + sizes[s]] = total
                    else:
                        results[f * len(pairs) + s][number] = total

        every(taken, work)
        for one in copies:
            one.wait()

    far_outs = [shape(4, *blocks[0].shape)] if blocks else []
    *made, mark = call(
        kernel, "halve", [place, bits] if blocks else [bits], arrays + list(blocks), outs,
        far_outs=far_outs, copies=len(blocks), room=6, after=after,
    )
    made, rows = made[: len(outs)], made[len(outs) :]
    half = len(outs) // len(flips)
    return made[:half], made[half:], mark, *rows


class Group:
    def __init__(self, units, extra, bits, names):
        self.units, self.extra, self.bits, self.names = units, extra, bits, names
        size = len(names)
        turn = [0, size - 1, size - 2]
        rest = list(range(size - 3, 0, -1))
        self.orders = [turn[s:] + turn[:s] + rest for s in range(3)]
        self.stage = 0
        self.pairs = None

    def send(self, blocks):
        return [
            swap(block, *self.names[order[self.stage]]) for block, order in zip(blocks, self.orders)
        ]

    def begin(self, after):
        sent, mark = cut_units(self.bits, self.units, self.extra, self.orders, 1, after)
        self.arrived = self.send(sent)
        return mark

    def rest(self, after):
        keep, mark = cut_units(self.bits, self.units, self.extra, self.orders, 0, after)
        self.pairs = list(zip(keep, self.arrived))
        self.stage = 1
        return mark

    def step(self, after, place=None, blocks=()):
        axes = [order[self.stage] for order in self.orders]
        sent, keep, mark, *rows = halve(
            self.bits, self.pairs, axes, self.stage == 3, after, place, blocks
        )
        self.pairs = list(zip(keep, self.send(sent)))
        self.stage += 1
        return (mark, *rows) if rows else mark

    def finish(self, after, place=None, blocks=()):
        (own,), _, mark, *rows = halve(self.bits, self.pairs, None, False, after, place, blocks)
        across = swap(own, "blk", 2)
        return (own, swap(own, "blk", 1), across, swap(across, "blk", 1)), mark, *rows


def chosen(place, b, refs):
    relative = place[1] ^ b
    values = [ref[...] for ref in refs]
    return jnp.where(
        relative < 2,
        jnp.where(relative == 0, values[0], values[1]),
        jnp.where(relative == 2, values[2], values[3]),
    ).astype(f32)


def place_all(place, feed_pieces, own_pieces, rows, shares, blocks, after):
    size = own_pieces[0].shape[2]
    width = 3 * size
    share = width // shares
    extra = own_pieces[0].shape[1] - 3 * rows
    count = 8 + len(blocks)

    def kernel(place_ref, *refs):
        feed_refs, own_refs = refs[:4], refs[4:8]
        down, up, qkv, out, bias_qv, bias_out, gain_one, shift_one, bias_up, bias_down, gain_two, shift_two = (
            refs[count : count + 12]
        )
        copies = place_rows(place_ref, refs[8:12], refs[count + 12], refs[-1]) if blocks else []
        for b in range(4):
            for s in range(3):
                columns = slice(s * size, (s + 1) * size)
                wider = slice(b * width + s * size, b * width + (s + 1) * size)
                at = 2 * s * rows
                value = chosen(place_ref, b, [p.at[0, at : at + rows] for p in feed_refs])
                down[b * rows : (b + 1) * rows, columns] = value
                at = at + rows
                up[:, wider] = chosen(place_ref, b, [p.at[0, at : at + rows] for p in feed_refs])
                at = s * rows + (extra if s else 0)
                value = chosen(place_ref, b, [p.at[0, at : at + rows] for p in own_refs])
                if b == 3:
                    out[:, columns] = value
                else:
                    qkv[:, wider] = value
            value = chosen(place_ref, b, [p.at[0, rows : rows + extra] for p in own_refs])
            targets = (
                ((bias_qv, 0), (bias_qv, 1), (bias_out, 0)),
                ((gain_one, 0), (shift_one, 0), (bias_down, 0)),
                ((gain_two, 0), (shift_two, 0), (bias_up, 0)),
                ((bias_up, 1), (bias_up, 2), (bias_up, 3)),
            )[b]
            for j, (ref, part) in enumerate(targets):
                ref[part * share : (part + 1) * share] = value[j, 0:share]
        for one in copies:
            one.wait()

    vectors = [shape(n * share, dtype=f32) for n in (2, 1, 1, 1, 4, 1, 1, 1)]
    return call(
        kernel, "place_all", [place], [*feed_pieces, *own_pieces, *blocks],
        [
            shape(4 * rows, width, dtype=f32), shape(rows, 4 * width, dtype=f32),
            shape(rows, 3 * width, dtype=f32), shape(rows, width, dtype=f32), *vectors,
        ],
        far_outs=[shape(4, *blocks[0].shape)] if blocks else [], copies=len(blocks), room=16, after=after,
    )[:-1]


def shards(
    tokens, lengths, w_qkv, bias_qv, w_out, bias_out, norm1_gain, norm1_bias, w_up, bias_up,
    w_down, bias_down, norm2_gain, norm2_bias, cotangent,
):
    rows, slots, width = tokens.shape
    shares = lax.axis_size("dp")
    dp_bits = shares.bit_length() - 1
    position = lax.axis_index("blk").astype(jnp.int32)
    group = lax.axis_index("dp").astype(jnp.int32)
    place = jnp.stack([position % 2, position])
    names = [("blk", 2)] + [("dp", 1 << i) for i in reversed(range(dp_bits))]
    bits = jnp.stack([position // 2] + [(group >> i) % 2 for i in reversed(range(dp_bits))])

    def gather_row(array):
        return [pick(array, position)] + [
            swap(pick(array, position ^ i), "blk", i) for i in (2, 3, 1)
        ]

    def in_order(blocks):
        return [blocks[0], blocks[3], blocks[1], blocks[2]]

    def scatter_pairs(blocks):
        own, beside, pair = blocks
        arrived = swap(pair, "blk", 2)
        return [own, swap(beside, "blk", 1), arrived, swap(arrived, "blk", 1)]

    def scatter_row(blocks):
        return [blocks[0]] + [swap(blocks[i], "blk", i) for i in range(1, rows)]

    biases = [
        bias_qv, bias_out, norm1_gain, norm1_bias, bias_down, norm2_gain, norm2_bias, bias_up
    ]
    row = jnp.concatenate([pick(lengths, position), position[None]])
    blocks = in_order(gather_row(tokens))
    qkv_near, out_near, mask, vectors, mark = prepare(
        row, biases, w_qkv, w_out, slots, rows * slots
    )
    cotangent, _ = lax.optimization_barrier((cotangent, blocks[1]))
    cotangents = in_order(gather_row(cotangent))
    normed, inverse, q, k, v, prob, context, row_tokens = attend(
        blocks, vectors, qkv_near, out_near, mask
    )
    keep_active, send_active, slope, lowered, first, o0, o1, o2, o3, vector_two, sum_two = feed(
        place, normed, vectors, cotangents, w_up, w_down, shares
    )
    got_active, got_lowered = swap(send_active, "blk", 1), swap(lowered, "blk", 1)
    keep_up, send_up, grad_bias_up, attended, vector_one, sum_one, mark = grad_up(
        place, lowered, slope, first, w_down, inverse, vectors, w_up, sum_two, normed
    )
    got_up = swap(send_up, "blk", 1)
    down, outputs, mark = grad_down(
        place, keep_active, got_active, lowered, got_lowered, scatter_row([o0, o1, o2, o3]), [mark]
    )

    def chunks(array):
        return array.reshape((2,) * (1 + dp_bits) + (-1, array.shape[-1]))

    down, keep_up, got_up = chunks(down), chunks(keep_up), chunks(got_up)
    feed_group = Group(
        [[([down], s) for s in range(3)], [([keep_up, got_up], s) for s in range(3)]],
        (), bits, names,
    )
    mark = feed_group.begin([mark])
    keeps, sends, small, grads, mark = attend_back(
        place, attended, [vector_one, vector_two, grad_bias_up],
        [row_tokens, context, prob, q, k, v, w_out], shares, [mark],
    )
    gots = [swap(send, "blk", 1) for send in sends]
    small = [chunks(small[0]), chunks(swap(small[1], "blk", 1))] if small else ()
    own_group = Group(
        [[([chunks(keep), chunks(got)], 0) for keep, got in zip(keeps, gots)]], small, bits, names
    )
    share = width // shares
    mark = feed_group.rest([mark])
    mark = feed_group.step([mark])
    mark = own_group.begin([mark])
    tokens_parts, mark = grad_tokens(sum_one, grads, w_qkv, slots, [mark])
    mark = own_group.rest([mark])
    for _ in range(dp_bits - 3):
        mark = feed_group.step([mark])
        mark = own_group.step([mark])
    mark = feed_group.step([mark])
    mark = own_group.step([mark])
    mark = feed_group.step([mark])
    mark = own_group.step([mark])
    mark = own_group.step([mark])
    feed_pieces, mark = feed_group.finish([mark])
    own_pieces, mark = own_group.finish([mark])
    (
        down, up, grad_w_qkv, grad_w_out, sum_qv, sum_out, sum_gain_one, sum_shift_one, sum_up, sum_down,
        sum_gain_two, sum_shift_two, token_grads,
    ) = place_all(place, feed_pieces, own_pieces, share, shares, scatter_pairs(tokens_parts), [mark])
    return (
        outputs,
        token_grads,
        grad_w_qkv,
        sum_qv,
        grad_w_out,
        sum_out,
        sum_gain_one,
        sum_shift_one,
        up,
        sum_up,
        down,
        sum_down,
        sum_gain_two,
        sum_shift_two,
    )


def solution(mesh):
    row_spec = P("dp", "blk", None)
    in_specs = (row_spec, P("dp", None)) + (P(),) * 12 + (row_spec,)
    wide, flat = P("dp", None), P("dp")
    out_specs = (
        row_spec, row_spec, wide, flat, wide, flat, flat, flat, wide, flat, wide, flat, flat, flat,
    )
    return jax.shard_map(shards, mesh=mesh, in_specs=in_specs, out_specs=out_specs, check_vma=False)
```

```python
import functools
import math

import jax
import jax.numpy as jnp
from jax import lax
from jax.experimental import pallas as pl
from jax.experimental.pallas import tpu as pltpu
from jax.sharding import PartitionSpec as P

HEADS = 12
EPSILON = 1e-12
MASKED = -1e30
f32 = jnp.float32
bf16 = jnp.bfloat16
NN = (((1,), (0,)), ((), ()))
NT = (((1,), (1,)), ((), ()))
TN = (((0,), (0,)), ((), ()))
VMEM = pl.BlockSpec(memory_space=pltpu.VMEM)
SMEM = pl.BlockSpec(memory_space=pltpu.SMEM)
HBM = pl.BlockSpec(memory_space=pltpu.HBM)
ANY = pl.BlockSpec(memory_space=pl.ANY)


WEIGHTS = {
    "prepare": 60 * 10**9, "attend": 60 * 10**9, "feed": 60 * 10**9, "grad_up": 60 * 10**9,
    "grad_down": 60 * 10**9, "attend_back": 60 * 10**9, "grad_tokens": 60 * 10**8,
    "halve": 150 * 10**7, "cut_units": 150 * 10**7, "place_all": 150 * 10**7,
}


def dot(left, right, dims=NN):
    return lax.dot_general(left, right, dims, preferred_element_type=f32)


def call(
    kernel, name, scalars, arrays, outs, scratch=(), far=(), far_outs=(), copies=0, room=10, after=()
):
    scratch = list(scratch)
    if copies:
        scratch.append(pltpu.SemaphoreType.DMA((copies,)))
    first, last = len(scalars) + len(arrays) + len(far), len(after)
    results = len(outs) + len(far_outs)
    mark = jax.ShapeDtypeStruct((8, 128), f32)

    def body(*refs):
        mine = refs[first + last :]
        mine[results][...] = jnp.zeros(mark.shape, mark.dtype)
        kernel(*refs[:first], *mine[:results], *mine[results + 1 :])

    return pl.pallas_call(
        body,
        in_specs=[SMEM] * len(scalars) + [VMEM] * len(arrays) + [HBM] * len(far) + [VMEM] * last,
        out_specs=[VMEM] * len(outs) + [HBM] * len(far_outs) + [VMEM],
        out_shape=[*outs, *[pltpu.HBM(a.shape, a.dtype) for a in far_outs], mark],
        scratch_shapes=scratch,
        compiler_params=pltpu.CompilerParams(vmem_limit_bytes=room * 2**20),
        cost_estimate=pl.CostEstimate(
            flops=WEIGHTS.get(name, 0), bytes_accessed=0, transcendentals=0
        ),
        name=name,
    )(
        *scalars, *arrays, *[pltpu.with_memory_space_constraint(a, pltpu.HBM) for a in far], *after
    )


def shape(*dims, dtype=bf16):
    return jax.ShapeDtypeStruct(dims, dtype)


def cut(i, size):
    return pl.ds(pl.multiple_of(i * size, size), size)


def copy(source, target, semaphore):
    return pltpu.make_async_copy(source, target, semaphore)


def column_sum(values):
    return jnp.sum(values, axis=0, keepdims=True)


def row_mean(values):
    return jnp.mean(values, axis=-1, keepdims=True)


def normalize(inputs):
    centre = inputs - row_mean(inputs)
    inverse = lax.rsqrt(row_mean(centre * centre) + EPSILON)
    return centre * inverse, inverse


def normalize_back(scaled, normed, inverse):
    return inverse * (scaled - row_mean(scaled) - normed * row_mean(scaled * normed))


BIAS_Q, BIAS_V, BIAS_OUT, GAIN_ONE, SHIFT_ONE, BIAS_DOWN, GAIN_TWO, SHIFT_TWO, BIAS_UP = range(9)


def vector(ref, row):
    return ref[row : row + 1, :]


def only(rows, h, height):
    parts = [jnp.zeros((height, rows.shape[1]), rows.dtype)] * (rows.shape[0] // height)
    parts[h] = rows[h * height : (h + 1) * height, :]
    return jnp.concatenate(parts)


def prepare_kernel(
    row_ref, w_qkv, w_out, b0, b1, b2, b3, b4, b5, b6, b7,
    qkv_near, out_near, mask, vectors, s0, s1, s2, s3, s4, s5, s6, s7, sems, *, pages, slots,
):
    pairs = zip((b0, b1, b2, b3, b4, b5, b6, b7), (s0, s1, s2, s3, s4, s5, s6, s7))
    loads = [copy(a, b, sems.at[2 + i]) for i, (a, b) in enumerate(pairs)]
    for one in loads:
        one.start()
    load_qkv = copy(w_qkv, qkv_near, sems.at[0])
    load_qkv.start()
    load_out = copy(w_out, out_near, sems.at[1])
    load_out.start()
    count = mask.shape[0]
    position = row_ref[pages]

    def page_of(shape, dim):
        at = lax.broadcasted_iota(jnp.int32, shape, dim)
        slot = ((at // slots) ^ position) * slots + at % slots
        page = jnp.zeros(shape, jnp.int32)
        end = 0
        for c in range(pages):
            end = end + row_ref[c]
            page = page + (slot >= end).astype(jnp.int32)
        return page

    mask[...] = jnp.where(
        page_of((count, count), 0) == page_of((1, count), 1), 0.0, MASKED
    )
    for one in loads:
        one.wait()
    width = vectors.shape[1]
    row = 0
    for part in (s0, s1, s2, s3, s4, s5, s6, s7):
        for i in range(part.shape[0] // width):
            vectors[row : row + 1, :] = part[i * width : (i + 1) * width].reshape(1, width)
            row += 1
    load_qkv.wait()
    load_out.wait()


def prepare(row, biases, w_qkv, w_out, slots, count):
    width = w_out.shape[0]
    rows = sum(b.shape[0] for b in biases) // width
    return call(
        functools.partial(prepare_kernel, pages=row.shape[0] - 1, slots=slots),
        "prepare", [row], [],
        [
            shape(*w_qkv.shape), shape(*w_out.shape), shape(count, count, dtype=f32),
            shape(rows, width, dtype=f32),
        ],
        [pltpu.VMEM(b.shape, f32) for b in biases],
        far=[w_qkv, w_out, *biases], copies=2 + len(biases),
    )


def attend_kernel(
    place, x0, x1, x2, x3, vectors, w_qkv, w_out, mask,
    normed_out, inverse_out, q_out, k_out, v_out, prob_out, context_out, tokens_out,
    tokens, q_kept, k_kept, v_kept, context_kept, probs_kept, sems, *, head_width,
):
    slots = x1.shape[0]
    count, width = tokens.shape
    wide = 4 * head_width
    groups = width // wide
    kept = ((0, q_kept, q_out), (1, k_kept, k_out), (2, v_kept, v_out), (3, context_kept, context_out))

    def keep(i, number, source, target):
        here = cut(i, wide)
        return copy(source.at[:, here], target.at[:, here], sems.at[number * groups + i])

    def keep_probs(i, h):
        return copy(
            probs_kept.at[4 * i + h], prob_out.at[4 * i + h], sems.at[4 * groups + 1 + 4 * i + h]
        )

    for i, block in enumerate((x0.at[place[1]], x1, x2, x3)):
        tokens[i * slots : (i + 1) * slots, :] = block[...]
    keep_tokens = copy(tokens, tokens_out, sems.at[4 * groups])
    keep_tokens.start()

    @pl.loop(0, groups, unroll=True)
    def _(i):
        here = cut(i, wide)
        x = tokens[...]
        q = (dot(x, w_qkv[:, here]) + vectors[BIAS_Q : BIAS_Q + 1, here]).astype(bf16)
        k = dot(x, w_qkv[:, cut(i + groups, wide)]).astype(bf16)
        v = dot(x, w_qkv[:, cut(i + 2 * groups, wide)]) + vectors[BIAS_V : BIAS_V + 1, here]
        v = v.astype(bf16)
        q_kept[:, here] = q
        k_kept[:, here] = k
        v_kept[:, here] = v
        q_turned = (q * jnp.asarray(1.0 / math.sqrt(head_width), bf16)).T
        v_turned = v.T
        context = []
        for h in range(4):
            scores = dot(k, only(q_turned, h, head_width)) + mask[...]
            powers = jnp.exp(scores - jnp.max(scores, axis=0, keepdims=True))
            probs = (powers * (1.0 / jnp.sum(powers, axis=0, keepdims=True))).astype(bf16)
            probs_kept[4 * i + h] = probs
            keep_probs(i, h).start()
            context.append(dot(v_turned[h * head_width : (h + 1) * head_width, :], probs))
        context_kept[:, here] = jnp.concatenate(context).astype(bf16).T
        for number, source, target in kept:
            keep(i, number, source, target).start()

    attended = dot(context_kept[...], w_out[...]) + vector(vectors, BIAS_OUT)
    normed, inverse = normalize(tokens[...].astype(f32) + attended)
    normed_out[...] = normed
    inverse_out[...] = inverse
    for i in range(groups):
        for number, source, target in kept:
            keep(i, number, source, target).wait()
        for h in range(4):
            keep_probs(i, h).wait()
    keep_tokens.wait()


def attend(place, blocks, vectors, w_qkv, w_out, mask):
    slots, width = blocks[1].shape
    count = slots * len(blocks)
    groups = HEADS // 4
    narrow = shape(count, width)
    rows = pltpu.VMEM((count, width), bf16)
    return call(
        functools.partial(attend_kernel, head_width=width // HEADS),
        "attend", [place], [*blocks, vectors, w_qkv, w_out, mask],
        [shape(count, width, dtype=f32), shape(count, 1, dtype=f32)],
        [rows, rows, rows, rows, rows, pltpu.VMEM((HEADS, count, count), bf16)],
        far_outs=[narrow, narrow, narrow, shape(HEADS, count, count), narrow, narrow],
        copies=4 * groups + 1 + HEADS, room=24,
    )[:8]


def feed_kernel(
    place, normed_one, vectors, c0, c1, c2, c3, w_up, w_down,
    keep_active, send_active, slope_out, lowered_out, first_out, r0, r1, r2, r3, vector_out,
    sum_out, total, *, shares,
):
    width = w_up.shape[0]
    hidden = w_up.shape[1]
    first_norm = normed_one[...] * vector(vectors, GAIN_ONE) + vector(vectors, SHIFT_ONE)
    first_out[...] = first_norm.astype(bf16)
    total[...] = first_norm + vector(vectors, BIAS_DOWN)
    odd = place[0] == 1
    rows = hidden // shares // 4
    apart = send_active is not None

    @pl.loop(0, hidden // width, unroll=True)
    def _(i):
        here = cut(i, width)
        raised = dot(first_out[...], w_up[:, here]) + vectors[pl.ds(BIAS_UP + i, 1), :]
        cumulative = 0.5 * (1.0 + lax.erf(raised * (1.0 / math.sqrt(2.0))))
        activated = (raised * cumulative).astype(bf16)
        bell = jnp.exp(-0.5 * raised * raised) * (1.0 / math.sqrt(2.0 * math.pi))
        slope_out[:, here] = (cumulative + raised * bell).astype(bf16)
        total[...] += dot(activated, w_down[here, :])
        turned = activated.T
        if apart:
            count = width // rows // 4
            for d in range(count):
                for x in range(2):
                    at = (d * 4 + x * 2) * rows
                    even_part = turned[at : at + rows, :]
                    odd_part = turned[at + rows : at + 2 * rows, :]
                    keep_active[x, i * count + d] = jnp.where(odd, odd_part, even_part)
                    send_active[x, i * count + d] = jnp.where(odd, even_part, odd_part)
        else:
            keep_active[here, :] = turned

    normed, inverse = normalize(total[...])
    gain = vector(vectors, GAIN_TWO)
    result = (normed * gain + vector(vectors, SHIFT_TWO)).astype(bf16)
    slots = c0.shape[0]
    for i, block in enumerate((r0, r1, r2, r3)):
        block[...] = result[i * slots : (i + 1) * slots, :]
    upstream = jnp.concatenate([c0[...], c1[...], c2[...], c3[...]]).astype(f32)
    grad_sum = normalize_back(upstream * gain, normed, inverse)
    sum_out[...] = grad_sum
    lowered = grad_sum.astype(bf16)
    lowered_out[...] = lowered
    vector_out[0:1, :] = column_sum(upstream * normed)
    vector_out[1:2, :] = column_sum(upstream)
    vector_out[2:3, :] = column_sum(lowered.astype(f32))


def feed(place, normed, vectors, cotangents, w_up, w_down, shares):
    count, width = normed.shape
    hidden = w_up.shape[1]
    rows = hidden // shares // 4
    narrow, full = shape(count, width), shape(count, width, dtype=f32)
    apart = rows % 16 == 0 and width % (4 * rows) == 0
    kernel = functools.partial(feed_kernel, shares=shares)
    if apart:
        active = [shape(2, shares, rows, count)] * 2
    else:
        active = [shape(hidden, count)]
        whole = kernel

        def kernel(*refs):
            whole(*refs[:10], None, *refs[10:])

    made = call(
        kernel, "feed", [place], [normed, vectors, *cotangents, w_up, w_down],
        active + [shape(count, hidden), narrow, narrow]
        + [shape(*cotangents[0].shape)] * 4 + [shape(8, width, dtype=f32), full],
        [pltpu.VMEM((count, width), f32)], room=14,
    )[:-1]
    if apart:
        return made
    parts = jnp.moveaxis(made[0].reshape(shares, 2, 2, rows, count), 0, 2)
    odd = place[0] == 1
    keep = jnp.where(odd, parts[:, 1], parts[:, 0])
    send = jnp.where(odd, parts[:, 0], parts[:, 1])
    return [keep, send, *made[1:]]


def grad_up_kernel(
    place, lowered, slope, first, w_down, inverse_one, vectors, sum_two, normed, w_up,
    keep, send, bias_out, attended_out, vector_out, sum_out, turned, raised_kept, weights, sems,
):
    width = lowered.shape[1]
    load = copy(w_up, weights, sems.at[0])
    load.start()
    turned[...] = first[...].T

    def work(b):
        here = cut(b, width)
        raised = dot(lowered[...], w_down[here, :], NT) * slope[:, here].astype(f32)
        raised = raised.astype(bf16)
        raised_kept[:, here] = raised
        bias_out[pl.ds(b, 1), :] = column_sum(raised.astype(f32))
        return dot(turned[...], raised).astype(bf16)

    @pl.loop(0, 2)
    def _(x):
        send[x] = work(2 * x + 1 - place[0])
        keep[x] = work(2 * x + place[0])

    load.wait()
    upstream = sum_two[...] + dot(raised_kept[...], weights[...], NT)
    grad_sum = normalize_back(
        upstream * vector(vectors, GAIN_ONE), normed[...], inverse_one[...]
    )
    sum_out[...] = grad_sum
    attended = grad_sum.astype(bf16)
    attended_out[...] = attended
    vector_out[0:1, :] = column_sum(upstream * normed[...])
    vector_out[1:2, :] = column_sum(upstream)
    vector_out[2:3, :] = column_sum(attended.astype(f32))


def grad_up(place, lowered, slope, first, w_down, inverse, vectors, w_up, sum_two, normed):
    count, width = lowered.shape
    hidden = w_down.shape[0]
    return call(
        grad_up_kernel, "grad_up", [place],
        [lowered, slope, first, w_down, inverse, vectors, sum_two, normed],
        [shape(2, width, width)] * 2
        + [shape(hidden // width, width, dtype=f32), shape(count, width)]
        + [shape(8, width, dtype=f32), shape(count, width, dtype=f32)],
        [
            pltpu.VMEM((width, count), bf16), pltpu.VMEM((count, hidden), bf16),
            pltpu.VMEM((width, hidden), bf16),
        ],
        far=[w_up], copies=1, room=28,
    )


def place_rows(place, blocks, rows, sems):
    if len(blocks[2].shape) == 3:
        blocks = (*blocks[:2], blocks[2].at[0], blocks[3].at[1])
    copies = [copy(block, rows.at[place[1] ^ i], sems.at[i]) for i, block in enumerate(blocks)]
    for one in copies:
        one.start()
    return copies


def grad_down_kernel(
    place, active, other_active, lowered, other_lowered, r0, r1, r2, r3, down, rows_out, sems
):
    copies = place_rows(place, (r0, r1, r2, r3), rows_out, sems)
    _, shares, rows, count = active.shape
    width = lowered.shape[1]

    for x in range(2):

        @pl.loop(0, shares, step=2, unroll=shares <= 8)
        def _(d):
            mine = active[x, pl.ds(d, 2)].reshape(2 * rows, count)
            other = other_active[x, pl.ds(d, 2)].reshape(2 * rows, count)
            value = dot(mine, lowered[...]) + dot(other, other_lowered[...])
            down[x, pl.ds(d, 2)] = value.astype(bf16).reshape(2, rows, width)

    for one in copies:
        one.wait()


def grad_down(place, active, other_active, lowered, other_lowered, blocks, after):
    _, shares, rows, _ = active.shape
    slots, width = blocks[0].shape
    return call(
        grad_down_kernel, "grad_down", [place],
        [active, other_active, lowered, other_lowered, *blocks],
        [shape(2, shares, rows, width)], far_outs=[shape(4, slots, width)], copies=4, after=after,
    )


def small_pieces(shares, width):
    q, v, gain_one, shift_one, out, gain_two, shift_two, down, up = range(9)
    share = width // shares

    def flat(row, first):
        return row + first // width, first % width

    def pieces(d):
        at = d * share
        return (
            (flat(q, 2 * at), flat(q, 2 * at + share), (out, at)),
            ((gain_one, at), (shift_one, at), (down, at)),
            ((gain_two, at), (shift_two, at), flat(up, 4 * at)),
            tuple(flat(up, 4 * at + j * share) for j in (1, 2, 3)),
        )

    return [pieces(d) for d in range(shares)]


def attend_back_kernel(
    place, attended, vector_one, vector_two, bias_up, tokens, context, prob, q_ref, k_ref, v_ref, w_out,
    grads_out, keep_0, keep_1, keep_2, send_0, send_1, send_2, small_keep, small_send,
    rows_kept, turned, turned_context, probs_kept, q_kept, k_kept, v_kept, weights, sums, small, sems,
    *, head_width,
):
    count, width = attended.shape
    wide = 4 * head_width
    groups = width // wide
    shares = small.shape[1]
    rows = width // shares
    joined = small_keep is None

    def load(i):
        here = cut(i, wide)
        pairs = [
            (w_out.at[here, :], weights.at[here, :]),
            (v_ref.at[:, here], v_kept.at[:, here]),
            (q_ref.at[:, here], q_kept.at[:, here]),
            (k_ref.at[:, here], k_kept.at[:, here]),
        ]
        pairs = pairs + [(prob.at[4 * i + h], probs_kept.at[4 * i + h]) for h in range(4)]
        return [copy(s, t, sems.at[8 * i + n]) for n, (s, t) in enumerate(pairs)]

    load_tokens = copy(tokens, rows_kept.at[0], sems.at[8 * groups])
    load_context = copy(context, rows_kept.at[1], sems.at[8 * groups + 1])
    for one in load(0):
        one.start()
    load_tokens.start()
    load_context.start()
    head = lax.broadcasted_iota(jnp.int32, (count, wide), 1) // head_width
    none = jnp.zeros((count, wide), bf16)
    odd = place[0] == 1

    @pl.loop(0, groups, unroll=True)
    def _(i):
        here = cut(i, wide)

        @pl.when(i + 1 < groups)
        def _():
            for one in load(i + 1):
                one.start()

        waits = load(i)
        waits[0].wait()
        grad_context = dot(attended[...], weights[here, :], NT).astype(bf16)
        context_turned = grad_context.T
        scaling = jnp.asarray(1.0 / math.sqrt(head_width), bf16)
        for one in waits[1:4]:
            one.wait()
        scaled_q = q_kept[:, here] * scaling
        k_turned = (k_kept[:, here] * scaling).T
        v = v_kept[:, here]

        @pl.when(i == 0)
        def _():
            load_tokens.wait()
            turned[...] = rows_kept[0].T
            load_context.wait()
            turned_context[...] = rows_kept[1].T

        for one in waits[4:]:
            one.wait()
        grad_k = jnp.zeros((count, wide), f32)
        grad_v = grad_k
        grad_q = []
        for h in range(4):
            mine = head == h
            probs = probs_kept[4 * i + h]
            wider = probs.astype(f32)
            lines = slice(h * head_width, (h + 1) * head_width)
            balance = column_sum(
                context_turned[lines, :].astype(f32)
                * turned_context[pl.ds(i * wide + h * head_width, head_width), :].astype(f32)
            )
            weighted = dot(v, only(context_turned, h, head_width)) - balance
            grad_scores = (wider * weighted).astype(bf16)
            grad_v = grad_v + dot(probs, jnp.where(mine, grad_context, none))
            grad_k = grad_k + dot(grad_scores, jnp.where(mine, scaled_q, none))
            grad_q.append(dot(k_turned[h * head_width : (h + 1) * head_width, :], grad_scores))
        grad_q = jnp.concatenate(grad_q).astype(bf16).T
        grad_k = grad_k.astype(bf16)
        grad_v = grad_v.astype(bf16)
        grads_out[:, here] = grad_q
        grads_out[:, cut(i + groups, wide)] = grad_k
        grads_out[:, cut(i + 2 * groups, wide)] = grad_v
        sums[0:1, here] = column_sum(grad_q.astype(f32))
        sums[1:2, here] = column_sum(grad_v.astype(f32))
        pieces = (
            dot(turned[...], grad_q).astype(bf16),
            dot(turned[...], grad_k).astype(bf16),
            dot(turned[...], grad_v).astype(bf16),
            dot(turned_context[...], attended[:, here]).astype(bf16),
        )
        for s, (keep, send) in enumerate(((keep_0, send_0), (keep_1, send_1), (keep_2, send_2))):

            @pl.when(i == s)
            def _(s=s, keep=keep, send=send):
                for x in range(2):
                    kept = jnp.where(odd, pieces[2 * x + 1], pieces[2 * x])
                    sent = jnp.where(odd, pieces[2 * x], pieces[2 * x + 1])
                    if s or not joined:
                        keep[x] = kept
                        send[x] = sent
                    else:
                        for d in range(shares):
                            keep[x, d, 0:rows, :] = kept[d * rows : (d + 1) * rows, :]
                            send[x, d, 0:rows, :] = sent[d * rows : (d + 1) * rows, :]

    sums[2:5, :] = vector_one[0:3, :]
    sums[5:8, :] = vector_two[0:3, :]
    sums[8:12, :] = bias_up[...]
    share = width // shares
    small[...] = jnp.zeros_like(small)
    for d, by_blk in enumerate(small_pieces(shares, width)):
        for b, three in enumerate(by_blk):
            for j, (row, column) in enumerate(three):
                small[b, d, j : j + 1, 0:share] = sums[row : row + 1, column : column + share]
    for x in range(2):
        even_part = small[2 * x].astype(bf16)
        odd_part = small[2 * x + 1].astype(bf16)
        kept = jnp.where(odd, odd_part, even_part)
        sent = jnp.where(odd, even_part, odd_part)
        if joined:
            keep_0[x, :, rows:, :] = kept
            send_0[x, :, rows:, :] = sent
        else:
            small_keep[x] = kept
            small_send[x] = sent


def attend_back(place, attended, small, far, shares, after):
    count, width = attended.shape
    wide = 4 * (width // HEADS)
    groups = width // wide
    rows, turned = pltpu.VMEM((count, width), bf16), pltpu.VMEM((width, count), bf16)
    share = width // shares
    joined = share % 16 == 0
    plain, extra = shape(2, width, wide), [shape(2, shares, 16, wide)] * 2
    first = shape(2, shares, share + 16, wide) if joined else plain
    inner = functools.partial(attend_back_kernel, head_width=width // HEADS)

    def kernel(*refs):
        if joined:
            refs = (*refs[:19], None, None, *refs[19:])
        inner(*refs)

    grads, keep_0, keep_1, keep_2, send_0, send_1, send_2, *small, mark = call(
        kernel, "attend_back", [place], [attended, *small],
        [shape(count, 3 * width)] + [first, plain, plain] * 2 + ([] if joined else extra),
        [
            pltpu.VMEM((2, count, width), bf16), turned, turned,
            pltpu.VMEM((HEADS, count, count), bf16), rows, rows, rows,
            pltpu.VMEM((width, width), bf16),
            pltpu.VMEM((16, width), f32), pltpu.VMEM((4, shares, 16, wide), f32),
        ],
        far=far, copies=8 * groups + 2, room=26, after=after,
    )
    return [keep_0, keep_1, keep_2], [send_0, send_1, send_2], small, grads, mark


def grad_tokens_kernel(grads, w_qkv, sum_one, own, beside, across):
    result = (sum_one[...] + dot(grads[...], w_qkv[...], NT)).astype(bf16)
    slots = own.shape[0]
    for i, block in enumerate((own, beside, across.at[0], across.at[1])):
        block[...] = result[i * slots : (i + 1) * slots, :]


def grad_tokens(sum_one, grads, w_qkv, slots, after):
    count, width = sum_one.shape
    *blocks, mark = call(
        grad_tokens_kernel, "grad_tokens", [], [grads, w_qkv, sum_one],
        [shape(slots, width)] * 2 + [shape(2, slots, width)],
        room=12, after=after,
    )
    return blocks, mark


def swap(block, axis, bit):
    return lax.ppermute(block, axis, [(i, i ^ bit) for i in range(lax.axis_size(axis))])


def pick(block, index, dim=0):
    return lax.dynamic_index_in_dim(block, index, dim, keepdims=False)


def every(count, work):
    if count <= 8:
        for number in range(count):
            work(number)
    else:
        pl.loop(0, count)(work)


def cut_units(bits, units, extra, orders, flip, after):
    parts, dims = len(orders), len(orders[0])
    arrays, numbers = [], {}
    for array in [a for unit in units for terms, _ in unit for a in terms] + list(extra):
        if id(array) not in numbers:
            numbers[id(array)] = len(arrays)
            arrays.append(array)
    rows = [units[0][s][0][0].shape[-2] for s in range(parts)]
    size = sum({id(terms[0]): terms[0].shape[-1] for terms, _ in units[0]}.values()) // parts
    more = [extra[0].shape[-2] if extra and s == 0 else 0 for s in range(parts)]
    outs = [shape(2 ** (dims - 1), len(units) * r + m, size) for r, m in zip(rows, more)]

    def kernel(bits_ref, *refs):
        ins, results = refs[: len(arrays)], refs[len(arrays) :]

        def added(terms, at):
            total = ins[numbers[id(terms[0])]][at]
            for term in terms[1:]:
                total = total + ins[numbers[id(term)]][at]
            return total

        def work(number):
            for s, order in enumerate(orders):
                index = [None] * dims
                index[order[0]] = bits_ref[order[0]] ^ flip
                for i, n in enumerate(order[1:]):
                    index[n] = (number >> (dims - 2 - i)) & 1
                for u, unit in enumerate(units):
                    terms, column = unit[s]
                    at = (*index, slice(None), slice(column * size, (column + 1) * size))
                    results[s][number, u * rows[s] : (u + 1) * rows[s]] = added(terms, at)
                if more[s]:
                    results[s][number, len(units) * rows[s] :] = added(extra, tuple(index))

        every(2 ** (dims - 1), work)

    *made, mark = call(kernel, "cut_units", [bits], arrays, outs, after=after)
    return made, mark


def halve(bits, pairs, axes, join, after=(), place=None, blocks=()):
    taken = pairs[0][0].shape[0] // (2 if axes else 1)
    sizes = [a.shape[1] for a, _ in pairs]
    width = pairs[0][0].shape[2]
    flips = (1, 0) if axes else (0,)
    outs = [shape(taken, sum(sizes), width)] if join else [shape(taken, n, width) for n in sizes]
    outs = outs * len(flips)
    arrays = [a for pair in pairs for a in pair]

    def kernel(*refs):
        copies = []
        if blocks:
            place_ref, *refs, sems = refs
            copies = place_rows(place_ref, refs[1 + len(arrays) : 5 + len(arrays)], refs[-1], sems)
        bits_ref, ins, results = refs[0], refs[1 : 1 + len(arrays)], refs[1 + len(arrays) + len(blocks) :]

        def work(number):
            for f, flip in enumerate(flips):
                for s in range(len(pairs)):
                    at = number + ((bits_ref[axes[s]] ^ flip) * taken if axes else 0)
                    total = ins[2 * s][at] + ins[2 * s + 1][at]
                    if join:
                        first = sum(sizes[:s])
                        results[f][number, first : first + sizes[s]] = total
                    else:
                        results[f * len(pairs) + s][number] = total

        every(taken, work)
        for one in copies:
            one.wait()

    far_outs = [shape(4, *blocks[0].shape)] if blocks else []
    *made, mark = call(
        kernel, "halve", [place, bits] if blocks else [bits], arrays + list(blocks), outs,
        far_outs=far_outs, copies=len(blocks), room=6, after=after,
    )
    made, rows = made[: len(outs)], made[len(outs) :]
    half = len(outs) // len(flips)
    return made[:half], made[half:], mark, *rows


class Group:
    def __init__(self, units, extra, bits, names):
        self.units, self.extra, self.bits, self.names = units, extra, bits, names
        size = len(names)
        turn = [0, size - 1, size - 2]
        rest = list(range(size - 3, 0, -1))
        self.orders = [turn[s:] + turn[:s] + rest for s in range(3)]
        self.stage = 0
        self.pairs = None

    def send(self, blocks):
        return [
            swap(block, *self.names[order[self.stage]]) for block, order in zip(blocks, self.orders)
        ]

    def begin(self, after):
        sent, mark = cut_units(self.bits, self.units, self.extra, self.orders, 1, after)
        self.arrived = self.send(sent)
        return mark

    def rest(self, after):
        keep, mark = cut_units(self.bits, self.units, self.extra, self.orders, 0, after)
        self.pairs = list(zip(keep, self.arrived))
        self.stage = 1
        return mark

    def step(self, after, place=None, blocks=()):
        axes = [order[self.stage] for order in self.orders]
        sent, keep, mark, *rows = halve(
            self.bits, self.pairs, axes, self.stage == 3, after, place, blocks
        )
        self.pairs = list(zip(keep, self.send(sent)))
        self.stage += 1
        return (mark, *rows) if rows else mark

    def finish(self, after, place=None, blocks=()):
        (own,), _, mark, *rows = halve(self.bits, self.pairs, None, False, after, place, blocks)
        across = swap(own, "blk", 2)
        return (own, swap(own, "blk", 1), across, swap(across, "blk", 1)), mark, *rows


def chosen(place, b, refs):
    relative = place[1] ^ b
    values = [ref[...] for ref in refs]
    return jnp.where(
        relative < 2,
        jnp.where(relative == 0, values[0], values[1]),
        jnp.where(relative == 2, values[2], values[3]),
    ).astype(f32)


def place_all(place, feed_pieces, own_pieces, rows, shares, blocks, after):
    size = own_pieces[0].shape[2]
    width = 3 * size
    share = width // shares
    extra = own_pieces[0].shape[1] - 3 * rows
    count = 8 + len(blocks)

    def kernel(place_ref, *refs):
        feed_refs, own_refs = refs[:4], refs[4:8]
        down, up, qkv, out, bias_qv, bias_out, gain_one, shift_one, bias_up, bias_down, gain_two, shift_two = (
            refs[count : count + 12]
        )
        copies = place_rows(place_ref, refs[8:12], refs[count + 12], refs[-1]) if blocks else []
        for b in range(4):
            for s in range(3):
                columns = slice(s * size, (s + 1) * size)
                wider = slice(b * width + s * size, b * width + (s + 1) * size)
                at = 2 * s * rows
                value = chosen(place_ref, b, [p.at[0, at : at + rows] for p in feed_refs])
                down[b * rows : (b + 1) * rows, columns] = value
                at = at + rows
                up[:, wider] = chosen(place_ref, b, [p.at[0, at : at + rows] for p in feed_refs])
                at = s * rows + (extra if s else 0)
                value = chosen(place_ref, b, [p.at[0, at : at + rows] for p in own_refs])
                if b == 3:
                    out[:, columns] = value
                else:
                    qkv[:, wider] = value
            value = chosen(place_ref, b, [p.at[0, rows : rows + extra] for p in own_refs])
            targets = (
                ((bias_qv, 0), (bias_qv, 1), (bias_out, 0)),
                ((gain_one, 0), (shift_one, 0), (bias_down, 0)),
                ((gain_two, 0), (shift_two, 0), (bias_up, 0)),
                ((bias_up, 1), (bias_up, 2), (bias_up, 3)),
            )[b]
            for j, (ref, part) in enumerate(targets):
                ref[part * share : (part + 1) * share] = value[j, 0:share]
        for one in copies:
            one.wait()

    vectors = [shape(n * share, dtype=f32) for n in (2, 1, 1, 1, 4, 1, 1, 1)]
    return call(
        kernel, "place_all", [place], [*feed_pieces, *own_pieces, *blocks],
        [
            shape(4 * rows, width, dtype=f32), shape(rows, 4 * width, dtype=f32),
            shape(rows, 3 * width, dtype=f32), shape(rows, width, dtype=f32), *vectors,
        ],
        far_outs=[shape(4, *blocks[0].shape)] if blocks else [], copies=len(blocks), room=16, after=after,
    )[:-1]


def shards(
    tokens, lengths, w_qkv, bias_qv, w_out, bias_out, norm1_gain, norm1_bias, w_up, bias_up,
    w_down, bias_down, norm2_gain, norm2_bias, cotangent,
):
    rows, slots, width = tokens.shape
    shares = lax.axis_size("dp")
    dp_bits = shares.bit_length() - 1
    position = lax.axis_index("blk").astype(jnp.int32)
    group = lax.axis_index("dp").astype(jnp.int32)
    place = jnp.stack([position % 2, position])
    names = [("blk", 2)] + [("dp", 1 << i) for i in reversed(range(dp_bits))]
    bits = jnp.stack([position // 2] + [(group >> i) % 2 for i in reversed(range(dp_bits))])

    def gather_row(array):
        return [pick(array, position)] + [
            swap(pick(array, position ^ i), "blk", i) for i in (2, 3, 1)
        ]

    def in_order(blocks):
        return [blocks[0], blocks[3], blocks[1], blocks[2]]

    def scatter_pairs(blocks):
        own, beside, pair = blocks
        arrived = swap(pair, "blk", 2)
        return [own, swap(beside, "blk", 1), arrived, swap(arrived, "blk", 1)]

    def scatter_row(blocks):
        return [blocks[0]] + [swap(blocks[i], "blk", i) for i in range(1, rows)]

    biases = [
        bias_qv, bias_out, norm1_gain, norm1_bias, bias_down, norm2_gain, norm2_bias, bias_up
    ]
    row = jnp.concatenate([pick(lengths, position), position[None]])
    blocks = in_order(gather_row(tokens))
    qkv_near, out_near, mask, vectors, mark = prepare(
        row, biases, w_qkv, w_out, slots, rows * slots
    )
    cotangent, _ = lax.optimization_barrier((cotangent, blocks[1]))
    cotangents = in_order(gather_row(cotangent))
    normed, inverse, q, k, v, prob, context, row_tokens = attend(
        place, [tokens, *blocks[1:]], vectors, qkv_near, out_near, mask
    )
    keep_active, send_active, slope, lowered, first, o0, o1, o2, o3, vector_two, sum_two = feed(
        place, normed, vectors, cotangents, w_up, w_down, shares
    )
    got_active, got_lowered = swap(send_active, "blk", 1), swap(lowered, "blk", 1)
    keep_up, send_up, grad_bias_up, attended, vector_one, sum_one, mark = grad_up(
        place, lowered, slope, first, w_down, inverse, vectors, w_up, sum_two, normed
    )
    got_up = swap(send_up, "blk", 1)
    down, outputs, mark = grad_down(
        place, keep_active, got_active, lowered, got_lowered, scatter_row([o0, o1, o2, o3]), [mark]
    )

    def chunks(array):
        return array.reshape((2,) * (1 + dp_bits) + (-1, array.shape[-1]))

    down, keep_up, got_up = chunks(down), chunks(keep_up), chunks(got_up)
    feed_group = Group(
        [[([down], s) for s in range(3)], [([keep_up, got_up], s) for s in range(3)]],
        (), bits, names,
    )
    mark = feed_group.begin([mark])
    keeps, sends, small, grads, mark = attend_back(
        place, attended, [vector_one, vector_two, grad_bias_up],
        [row_tokens, context, prob, q, k, v, w_out], shares, [mark],
    )
    gots = [swap(send, "blk", 1) for send in sends]
    small = [chunks(small[0]), chunks(swap(small[1], "blk", 1))] if small else ()
    own_group = Group(
        [[([chunks(keep), chunks(got)], 0) for keep, got in zip(keeps, gots)]], small, bits, names
    )
    share = width // shares
    mark = feed_group.rest([mark])
    mark = feed_group.step([mark])
    mark = own_group.begin([mark])
    tokens_parts, mark = grad_tokens(sum_one, grads, w_qkv, slots, [mark])
    mark = own_group.rest([mark])
    for _ in range(dp_bits - 3):
        mark = feed_group.step([mark])
        mark = own_group.step([mark])
    mark = feed_group.step([mark])
    mark = own_group.step([mark])
    mark = feed_group.step([mark])
    mark = own_group.step([mark])
    mark = own_group.step([mark])
    feed_pieces, mark = feed_group.finish([mark])
    own_pieces, mark = own_group.finish([mark])
    (
        down, up, grad_w_qkv, grad_w_out, sum_qv, sum_out, sum_gain_one, sum_shift_one, sum_up, sum_down,
        sum_gain_two, sum_shift_two, token_grads,
    ) = place_all(place, feed_pieces, own_pieces, share, shares, scatter_pairs(tokens_parts), [mark])
    return (
        outputs,
        token_grads,
        grad_w_qkv,
        sum_qv,
        grad_w_out,
        sum_out,
        sum_gain_one,
        sum_shift_one,
        up,
        sum_up,
        down,
        sum_down,
        sum_gain_two,
        sum_shift_two,
    )


def solution(mesh):
    row_spec = P("dp", "blk", None)
    in_specs = (row_spec, P("dp", None)) + (P(),) * 12 + (row_spec,)
    wide, flat = P("dp", None), P("dp")
    out_specs = (
        row_spec, row_spec, wide, flat, wide, flat, flat, flat, wide, flat, wide, flat, flat, flat,
    )
    return jax.shard_map(shards, mesh=mesh, in_specs=in_specs, out_specs=out_specs, check_vma=False)
```
